32 devices in a mesh: row: 4 (over z), col: 8 (over y, x, core).
Axes of the slice: x: 2, y: 2, z: 4, core: 2. Of those that a mesh axis runs over, the one named last changes fastest.
Arguments:
- queries: bfloat16 [4, 1024, 512], P('row', 'col'), may hold values from -6 to 6
- keys: bfloat16 [8, 512, 512], P('col', 'row'), may hold values from -6 to 6
- values: bfloat16 [8, 512, 512], P('col', 'row'), may hold values from -6 to 6
- outputs: bfloat16 [4, 1024, 512], P('row', 'col'), may hold values from -2 to 2
- grad_out: bfloat16 [4, 1024, 512], P('row', 'col'), may hold values from -48 to 48
- lse: float32 [4, 8, 1024], P('row'), may hold values from 7 to 9.5
- tile_slot: int32 [4, 8, 24], P('row', 'col'), may hold values from 0 to 31, as said below
- tile_live: int32 [4, 8], P('row', 'col'), may hold values from 1 to 24, as said below
- tile_bits: int32 [4, 8, 24, 8, 128], P('row', 'col'), may hold values from 0 to 65535, as said below
Outputs:
- grad_queries: bfloat16 [4, 1024, 512], P('row', 'col')
- grad_keys: bfloat16 [8, 512, 512], P('col', 'row')
- grad_values: bfloat16 [8, 512, 512], P('col', 'row')
The draws below stay inside these ranges and needn't reach their ends.
Inputs may be any that keep to these rules, and one draw needn't show every extreme that they name: `tile_slot`: the 24 entries of one pair of blocks are distinct slots. `tile_live`: some pair of blocks has all 24 entries live. `tile_bits`: each word holds 16 edge bits in its low bits.
All inputs are finite; a program needn't handle non-finite values.
Results may differ from the reference program's by a relative error of at most 0.02.
Values may be sent and summed in bfloat16 or wider, within the bound.
No kernel may reach another device: no remote copies, remote signals or barrier semaphores. Data moves between devices by JAX's collectives and lax.ppermute only.
A program may use at most 64 MiB of HBM per device.

```python
import jax
import jax.numpy as jnp
from jax import lax

HEADS = 8
D = 512
TILE = 128
QROWS = 1024
QBLOCKS = 4
KBLOCKS = 8
KCOLS = 512
CAP = 24


def draw_tile_slot(key, part):
    slot_total = QROWS // TILE * (KCOLS // TILE)
    block_keys = jax.random.split(key, QBLOCKS * KBLOCKS)
    orders = jax.vmap(lambda one_key: jax.random.permutation(one_key, slot_total))(block_keys)
    return orders[:, :CAP].reshape(QBLOCKS, KBLOCKS, CAP).astype(jnp.int32)


def draw_tile_live(key, part):
    key_one, key_two = jax.random.split(key)
    spread = jax.random.randint(key_one, (QBLOCKS, KBLOCKS), 0, CAP, dtype=jnp.int32)
    counts = 1 + spread * spread // CAP
    chosen = jax.random.randint(key_two, (), 0, QBLOCKS * KBLOCKS, dtype=jnp.int32)
    positions = jnp.arange(QBLOCKS * KBLOCKS, dtype=jnp.int32).reshape(QBLOCKS, KBLOCKS)
    return jnp.where(positions == chosen, CAP, counts).astype(jnp.int32)


def draw_tile_bits(key, part):
    words = jax.random.randint(key, (QBLOCKS, KBLOCKS, CAP, TILE // 16, TILE), 0, 65536, dtype=jnp.int32)
    words = words.at[0, 0, 0, 0, 0].set(jnp.int32(65535))
    words = words.at[0, 0, 0, 0, 1].set(jnp.int32(0))
    return words.astype(jnp.int32)


def level_of(own_key, dims, cuts, smallest, largest):
    def one(dim, parts):
        heights = jax.random.uniform(jax.random.fold_in(jax.random.fold_in(own_key, 6), dim), (parts,), jnp.float32, smallest / len(cuts), largest / len(cuts))
        return jnp.repeat(jnp.exp(heights), dims[dim] // parts).reshape((-1,) + (1,) * (len(dims) - dim - 1))

    level = one(*cuts[0])
    for cut in cuts[1:]:
        level = level * one(*cut)
    return level


def bell_draw(key, dims, width, bound, pieces=(), held_as=jnp.bfloat16):
    factor_of = level_of(key, dims, pieces, -0.22, 0.18) if pieces else 1.0
    result = jax.random.normal(key, dims, jnp.float32) * width * factor_of
    return jnp.minimum(jnp.maximum(result, -bound), bound).astype(held_as)


def setup_inputs(seed: int = 0) -> dict:
    splits = jax.random.split(jax.random.key(seed), 10)
    queries = bell_draw(splits[0], (QBLOCKS, QROWS, D), 1.0, 6.0, ((0, 4), (1, 8)))
    keys = bell_draw(splits[1], (KBLOCKS, KCOLS, D), 1.0, 6.0, ((0, 8), (1, 4)))
    values = bell_draw(splits[2], (KBLOCKS, KCOLS, D), 1.0, 6.0, ((0, 8), (1, 4)))
    outputs = bell_draw(splits[3], (QBLOCKS, QROWS, D), 0.3, 2.0, ((0, 4), (1, 8)))
    grad_out = bell_draw(splits[4], (QBLOCKS, QROWS, D), 8.0, 48.0, ((0, 4), (1, 8)))
    lse = jnp.clip(7.0 + 2.5 * jax.random.uniform(splits[5], (QBLOCKS, HEADS, QROWS), jnp.float32) ** level_of(splits[5], (QBLOCKS, HEADS, QROWS), ((0, 4),), -0.2, 0.2), 7.0, 9.5)
    tile_slot = draw_tile_slot(jax.random.fold_in(splits[9], 71), 0)
    tile_live = draw_tile_live(jax.random.fold_in(splits[9], 71), 0)
    tile_bits = draw_tile_bits(jax.random.fold_in(splits[9], 71), 0)
    return {"queries": queries, "keys": keys, "values": values, "outputs": outputs, "grad_out": grad_out, "lse": lse, "tile_slot": tile_slot, "tile_live": tile_live, "tile_bits": tile_bits}


def unpack_bits(packed_rows):
    shifts = jnp.arange(16, dtype=jnp.int32)
    bit_values = jnp.bitwise_and(jnp.right_shift(packed_rows[:, :, None], shifts), 1)
    return jnp.transpose(bit_values, (1, 0, 2)).reshape(packed_rows.shape[1], packed_rows.shape[0] * 16) == 1


def row_delta(grads, outs, head_count):
    leading = grads.shape[:-1]
    model_width = grads.shape[-1]
    product = (grads.astype(jnp.float32) * outs.astype(jnp.float32)).reshape(leading + (head_count, model_width // head_count))
    return jnp.swapaxes(jnp.sum(product, axis=-1), -1, -2).astype(jnp.bfloat16)


def add_rows(total, piece, start):
    current = lax.dynamic_slice_in_dim(total, start, piece.shape[0], 0)
    return lax.dynamic_update_slice_in_dim(total, current + piece, start, 0)


def add_block(total, piece, block_col, start):
    zero_index = jnp.int32(0)
    current = lax.dynamic_slice(total, (block_col, start, zero_index), (1, piece.shape[0], piece.shape[1]))
    return lax.dynamic_update_slice(total, current + piece[None], (block_col, start, zero_index))


def reference(queries, keys, values, outputs, grad_out, lse, tile_slot, tile_live, tile_bits):
    block_rows = queries.shape[0]
    query_count = queries.shape[1]
    model_width = queries.shape[2]
    block_cols = keys.shape[0]
    key_count = keys.shape[1]
    head_count = lse.shape[1]
    head_dim = model_width // head_count
    tile_size = tile_bits.shape[4]
    capacity = tile_slot.shape[2]
    key_tiles = key_count // tile_size
    scaling = float(head_dim) ** -0.5
    highest = lax.Precision.HIGHEST
    delta_all = lax.optimization_barrier(row_delta(grad_out, outputs, head_count)).astype(jnp.float32)

    def per_block(block_row, state):
        grad_q_all, grad_k_all, grad_v_all = state
        block_row = block_row.astype(jnp.int32)
        query_block = lax.dynamic_index_in_dim(queries, block_row, 0, keepdims=False).astype(jnp.float32)
        grad_block = lax.dynamic_index_in_dim(grad_out, block_row, 0, keepdims=False).astype(jnp.float32)
        lse_block = lax.dynamic_index_in_dim(lse, block_row, 0, keepdims=False)
        delta_block = lax.dynamic_index_in_dim(delta_all, block_row, 0, keepdims=False)

        def per_tile(flat_index, running):
            flat_index = flat_index.astype(jnp.int32)
            block_col = flat_index // capacity
            entry_index = flat_index % capacity
            slot_value = tile_slot[block_row, block_col, entry_index]
            live_count = tile_live[block_row, block_col]

            def compute(partial_sums):
                grad_q, grad_k, grad_v = partial_sums
                q_start = (slot_value // key_tiles) * tile_size
                k_start = (slot_value % key_tiles) * tile_size
                zero_index = jnp.int32(0)
                q_tile = lax.dynamic_slice_in_dim(query_block, q_start, tile_size, 0).reshape(tile_size, head_count, head_dim)
                g_tile = lax.dynamic_slice_in_dim(grad_block, q_start, tile_size, 0).reshape(tile_size, head_count, head_dim)
                k_tile = lax.dynamic_slice(keys, (block_col, k_start, zero_index), (1, tile_size, model_width))[0]
                k_tile = k_tile.astype(jnp.float32).reshape(tile_size, head_count, head_dim)
                v_tile = lax.dynamic_slice(values, (block_col, k_start, zero_index), (1, tile_size, model_width))[0]
                v_tile = v_tile.astype(jnp.float32).reshape(tile_size, head_count, head_dim)
                lse_tile = lax.dynamic_slice_in_dim(lse_block, q_start, tile_size, 1)
                delta_tile = lax.dynamic_slice_in_dim(delta_block, q_start, tile_size, 1)
                edge_mask = unpack_bits(tile_bits[block_row, block_col, entry_index])
                scores = jnp.einsum("ihd,jhd->hij", q_tile, k_tile, precision=highest) * scaling
                attn_prob = jnp.where(edge_mask[None], jnp.exp(scores - lse_tile[:, :, None]), 0.0)
                prob_low = lax.optimization_barrier(attn_prob.astype(jnp.bfloat16)).astype(jnp.float32)
                value_tile_grad = jnp.einsum("hij,ihd->jhd", prob_low, g_tile, precision=highest).reshape(tile_size, model_width)
                grad_prob = jnp.einsum("ihd,jhd->hij", g_tile, v_tile, precision=highest)
                score_grad = attn_prob * (grad_prob - delta_tile[:, :, None])
                score_low = lax.optimization_barrier(score_grad.astype(jnp.bfloat16)).astype(jnp.float32)
                query_tile_grad = jnp.einsum("hij,jhd->ihd", score_low, k_tile, precision=highest).reshape(tile_size, model_width) * scaling
                key_tile_grad = jnp.einsum("hij,ihd->jhd", score_low, q_tile, precision=highest).reshape(tile_size, model_width) * scaling
                grad_q = add_rows(grad_q, query_tile_grad, q_start)
                grad_k = add_block(grad_k, key_tile_grad, block_col, k_start)
                grad_v = add_block(grad_v, value_tile_grad, block_col, k_start)
                return (grad_q, grad_k, grad_v)

            return lax.cond(entry_index < live_count, compute, lambda unchanged: unchanged, running)

        start_sums = (jnp.zeros((query_count, model_width), jnp.float32), jnp.zeros(keys.shape, jnp.float32), jnp.zeros(keys.shape, jnp.float32))
        grad_q, grad_k, grad_v = lax.fori_loop(0, block_cols * capacity, per_tile, start_sums)
        grad_q_all = lax.dynamic_update_index_in_dim(grad_q_all, grad_q, block_row, 0)
        grad_k_all = grad_k_all + lax.optimization_barrier(grad_k.astype(jnp.bfloat16)).astype(jnp.float32)
        grad_v_all = grad_v_all + lax.optimization_barrier(grad_v.astype(jnp.bfloat16)).astype(jnp.float32)
        return (grad_q_all, grad_k_all, grad_v_all)

    initial = (jnp.zeros(queries.shape, jnp.float32), jnp.zeros(keys.shape, jnp.float32), jnp.zeros(keys.shape, jnp.float32))
    grad_q_all, grad_k_all, grad_v_all = lax.fori_loop(0, block_rows, per_block, initial)
    return (grad_q_all.astype(jnp.bfloat16), grad_k_all.astype(jnp.bfloat16), grad_v_all.astype(jnp.bfloat16))
```

```python
import functools

import jax
import jax.numpy as jnp
import numpy as np
from jax import lax
from jax.experimental import pallas as pl
from jax.experimental.pallas import tpu as pltpu
from jax.sharding import Mesh
from jax.sharding import PartitionSpec as P

F32 = jnp.float32
BF16 = jnp.bfloat16
LANES = 128
PAD = 16
LOG2E = 1.4426950408889634
NT = (((1,), (1,)), ((), ()))
NN = (((1,), (0,)), ((), ()))
PARAMS = pltpu.CompilerParams(vmem_limit_bytes=40 * 1024 * 1024)
VMEM = pl.BlockSpec(memory_space=pltpu.VMEM)
SMEM = pl.BlockSpec(memory_space=pltpu.SMEM)


def pack_kernel(heads, q_ref, g_ref, o_ref, k_ref, v_ref, qg_ref, kv_ref):
    chips, cores, _, half = qg_ref.shape
    rows = q_ref.shape[1]
    krows = k_ref.shape[1]
    width = q_ref.shape[2]
    head_dim = width // heads
    q, g, k, v = q_ref[0], g_ref[0], k_ref[0], v_ref[0]
    product = g.astype(F32) * o_ref[0].astype(F32)
    feature = lax.broadcasted_iota(jnp.int32, (2 * PAD, width), 1)
    head = lax.broadcasted_iota(jnp.int32, (2 * PAD, width), 0)
    local = heads // cores
    wanted = jnp.where(head % PAD < local, head // PAD * local + head % PAD, -1)
    pick = (feature // head_dim == wanted).astype(F32)
    delta = lax.dot_general(
        pick, product, NT, precision=lax.Precision.HIGHEST, preferred_element_type=F32
    ).astype(BF16)
    for core in range(cores):
        lanes = slice(core * half, (core + 1) * half)
        for chip in range(chips):
            qg_ref[chip, core, :rows] = q[:, lanes]
            qg_ref[chip, core, rows : 2 * rows] = g[:, lanes]
            qg_ref[chip, core, 2 * rows :, :rows] = delta[core * PAD : (core + 1) * PAD]
            qg_ref[chip, core, 2 * rows :, rows:] = jnp.zeros((PAD, half - rows), BF16)
        for row in range(kv_ref.shape[0]):
            kv_ref[row, core, :krows] = k[:, lanes]
            kv_ref[row, core, krows:] = v[:, lanes]


def pair_kernel(
    head_dim, tile, capacity,
    info_ref, qg_ref, kv_ref, own_ref, sib_ref, lse_ref,
    dq_ref, dkv_ref,
    q_scr, g_scr, k2t_scr, lse_scr, delta_scr, dqt_scr, dk_scr, dv_scr,
):
    sources, _, half = qg_ref.shape
    rows = (qg_ref.shape[1] - PAD) // 2
    row_count, cores, krows2, _ = kv_ref.shape
    krows = krows2 // 2
    per = tile // krows
    key_tiles = row_count // per
    pairs = half // LANES
    local = half // head_dim
    scaling = float(head_dim) ** -0.5
    core = info_ref[2 * (capacity + 1)]

    lse_scr[...] = lse_ref[core] * LOG2E
    for source in range(sources):
        span = slice(source * rows, (source + 1) * rows)
        q_scr[span] = qg_ref[source, :rows]
        g_scr[span] = qg_ref[source, rows : 2 * rows]
        delta_scr[:, span] = qg_ref[source, 2 * rows :, :rows].astype(F32)
    low_lane = lax.broadcasted_iota(jnp.int32, (tile, LANES), 1) < head_dim
    low_row = lax.broadcasted_iota(jnp.int32, (LANES, tile), 0) < head_dim
    zero = jnp.zeros((tile, LANES), BF16)
    zero_t = jnp.zeros((LANES, tile), BF16)
    bit = lax.shift_left(
        jnp.int32(1), lax.broadcasted_iota(jnp.int32, (tile // 16, 16, tile), 1)
    ).reshape(tile, tile)

    def key_part(w, block, part):
        piece = kv_ref[pl.ds(w * per, per), block, part * krows : (part + 1) * krows]
        return piece.reshape(tile, half)

    for block in range(cores):
        for w in range(key_tiles):
            flipped = key_part(w, block, 0).T
            for pair in range(pairs):
                part = flipped[pair * LANES : (pair + 1) * LANES]
                k2t_scr[block * key_tiles + w, pair] = jnp.concatenate(
                    [jnp.where(low_row, part, zero_t), jnp.where(low_row, zero_t, part)], axis=1
                )
    dqt_scr[...] = jnp.zeros_like(dqt_scr)
    dk_scr[...] = jnp.zeros_like(dk_scr)
    dv_scr[...] = jnp.zeros_like(dv_scr)

    def twice(piece):
        return jnp.concatenate(
            [jnp.where(low_lane, piece, zero), jnp.where(low_lane, zero, piece)], axis=0
        )

    for which, bits_ref in enumerate((own_ref, sib_ref)):
        base = which * (capacity + 1)
        block = core if which == 0 else 1 - core

        def one_tile(entry, _, base=base, block=block, bits_ref=bits_ref):
            slot = info_ref[base + entry]
            u = slot // key_tiles
            w = slot % key_tiles
            kidx = block * key_tiles + w
            qrow = pl.multiple_of(u * tile, tile)
            words = bits_ref[entry]
            words = jnp.broadcast_to(words[:, None, :], (tile // 16, 16, tile)).reshape(tile, tile)
            edge = (words & bit) != 0
            k_tile = key_part(w, block, 0)
            v_tile = key_part(w, block, 1)
            q_tile = q_scr[pl.ds(qrow, tile)]
            g_tile = g_scr[pl.ds(qrow, tile)]
            lse_tile = lse_scr[:, pl.ds(qrow, tile)]
            delta_tile = delta_scr[:, pl.ds(qrow, tile)]
            for pair in range(pairs):
                lanes = slice(pair * LANES, (pair + 1) * LANES)
                q2 = twice(q_tile[:, lanes])
                g2 = twice(g_tile[:, lanes])
                scores = lax.dot_general(k_tile[:, lanes], q2, NT, preferred_element_type=F32)
                grad_prob = lax.dot_general(v_tile[:, lanes], g2, NT, preferred_element_type=F32)
                probs, grads = [], []
                for side in range(2):
                    h = 2 * pair + side
                    s = scores[:, side * tile : (side + 1) * tile]
                    gp = grad_prob[:, side * tile : (side + 1) * tile]
                    p = jnp.exp2(s * (scaling * LOG2E) - lse_tile[h : h + 1])
                    p = jnp.where(edge, p, 0.0)
                    ds = p * (gp - delta_tile[h : h + 1])
                    probs.append(p.astype(BF16))
                    grads.append(ds.astype(BF16))
                p2 = jnp.concatenate(probs, axis=1)
                ds2 = jnp.concatenate(grads, axis=1)
                dv_scr[kidx, :, lanes] += lax.dot_general(p2, g2, NN, preferred_element_type=F32)
                dk_scr[kidx, :, lanes] += lax.dot_general(ds2, q2, NN, preferred_element_type=F32)
                dqt_scr[u, lanes] += lax.dot_general(
                    k2t_scr[kidx, pair], jnp.concatenate(grads, axis=0), NN,
                    preferred_element_type=F32,
                )
            return 0

        lax.fori_loop(0, info_ref[base + capacity], one_tile, 0)

    flat = []
    for u in range(dqt_scr.shape[0]):
        flat.append((dqt_scr[u] * scaling).T.astype(BF16))
    per_q = tile // rows
    for source in range(sources):
        inner = source % per_q
        dq_ref[source] = flat[source // per_q][inner * rows : (inner + 1) * rows]
    for block in range(cores):
        for w in range(key_tiles):
            dk = (dk_scr[block * key_tiles + w] * scaling).astype(BF16)
            dv = dv_scr[block * key_tiles + w].astype(BF16)
            for inner in range(per):
                span = slice(inner * krows, (inner + 1) * krows)
                dkv_ref[w * per + inner, block, :krows] = dk[span]
                dkv_ref[w * per + inner, block, krows:] = dv[span]


def sum_kernel(dq_ref, dkv_ref, dq_out, dk_out, dv_out):
    chips, cores, _, half = dq_ref.shape
    row_count = dkv_ref.shape[0]
    krows = dkv_ref.shape[2] // 2
    for core in range(cores):
        lanes = slice(core * half, (core + 1) * half)
        total = dq_ref[0, core].astype(F32)
        for chip in range(1, chips):
            total += dq_ref[chip, core].astype(F32)
        dq_out[0, :, lanes] = total.astype(BF16)
        total = dkv_ref[0, core].astype(F32)
        for row in range(1, row_count):
            total += dkv_ref[row, core].astype(F32)
        total = total.astype(BF16)
        dk_out[0, :, lanes] = total[:krows]
        dv_out[0, :, lanes] = total[krows:]


def body(sizes, queries, keys, values, outputs, grad_out, lse, tile_slot, tile_live, tile_bits):
    row_count, chips, cores = sizes
    heads = lse.shape[1]
    width = queries.shape[2]
    half = width // cores
    head_dim = width // heads
    local = heads // cores
    tile = tile_bits.shape[4]
    capacity = tile_slot.shape[2]
    rows = queries.shape[1]
    krows = keys.shape[1]
    sources = chips * cores
    query_count = lse.shape[2]
    key_tiles = row_count * krows // tile
    swap = [(core, cores - 1 - core) for core in range(cores)]

    info = jnp.concatenate([tile_slot[0, 0], tile_live[0]])
    info_sib = lax.ppermute(info, "core", swap)
    bits = tile_bits[0, 0]
    bits_sib = lax.ppermute(bits, "core", swap)
    info = jnp.concatenate([info, info_sib, lax.axis_index("core")[None].astype(jnp.int32)])

    qg, kv = pl.pallas_call(
        functools.partial(pack_kernel, heads),
        out_shape=(
            jax.ShapeDtypeStruct((chips, cores, 2 * rows + PAD, half), BF16),
            jax.ShapeDtypeStruct((row_count, cores, 2 * krows, half), BF16),
        ),
        in_specs=[VMEM] * 5,
        out_specs=(VMEM, VMEM),
        compiler_params=PARAMS,
        name="pack",
    )(queries, grad_out, outputs, keys, values)
    qg = qg.reshape(sources, 2 * rows + PAD, half)
    kv = kv.reshape(row_count * cores, 2 * krows, half)
    kv = lax.all_to_all(kv, ("row", "core"), 0, 0, tiled=True)
    qg = lax.all_to_all(qg, ("chip", "core"), 0, 0, tiled=True)
    kv = kv.reshape(row_count, cores, 2 * krows, half)

    dq, dkv = pl.pallas_call(
        functools.partial(pair_kernel, head_dim, tile, capacity),
        out_shape=(
            jax.ShapeDtypeStruct((sources, rows, half), BF16),
            jax.ShapeDtypeStruct((row_count, cores, 2 * krows, half), BF16),
        ),
        in_specs=[SMEM] + [VMEM] * 5,
        out_specs=(VMEM, VMEM),
        scratch_shapes=[
            pltpu.VMEM((query_count, half), BF16),
            pltpu.VMEM((query_count, half), BF16),
            pltpu.VMEM((cores * key_tiles, half // LANES, LANES, 2 * tile), BF16),
            pltpu.VMEM((local, query_count), F32),
            pltpu.VMEM((PAD, query_count), F32),
            pltpu.VMEM((query_count // tile, half, tile), F32),
            pltpu.VMEM((cores * key_tiles, tile, half), F32),
            pltpu.VMEM((cores * key_tiles, tile, half), F32),
        ],
        compiler_params=PARAMS,
        name="pair",
    )(info, qg, kv, bits, bits_sib, lse.reshape(cores, local, query_count))

    dkv = lax.all_to_all(
        dkv.reshape(row_count * cores, 2 * krows, half), ("row", "core"), 0, 0, tiled=True
    )
    dq = lax.all_to_all(dq, ("chip", "core"), 0, 0, tiled=True)
    return pl.pallas_call(
        sum_kernel,
        out_shape=(
            jax.ShapeDtypeStruct((1, rows, width), BF16),
            jax.ShapeDtypeStruct((1, krows, width), BF16),
            jax.ShapeDtypeStruct((1, krows, width), BF16),
        ),
        in_specs=[VMEM] * 2,
        out_specs=(VMEM, VMEM, VMEM),
        compiler_params=PARAMS,
        name="total",
    )(
        dq.reshape(chips, cores, rows, half),
        dkv.reshape(row_count, cores, 2 * krows, half),
    )


def solution(mesh):
    row_count, columns = mesh.devices.shape
    cores = 2
    chips = columns // cores
    fine = Mesh(mesh.devices.reshape(row_count, chips, cores), ("row", "chip", "core"))
    col = ("chip", "core")
    in_specs = (
        P("row", col, None),
        P(col, "row", None),
        P(col, "row", None),
        P("row", col, None),
        P("row", col, None),
        P("row", None, None),
        P("row", col, None),
        P("row", col),
        P("row", col, None, None, None),
    )
    out_specs = (P("row", col, None), P(col, "row", None), P(col, "row", None))
    return jax.shard_map(
        functools.partial(body, (row_count, chips, cores)),
        mesh=fine, in_specs=in_specs, out_specs=out_specs, check_vma=False,
    )
```

```python
import functools

import jax
import jax.numpy as jnp
from jax import lax
from jax.experimental import pallas as pl
from jax.experimental.pallas import tpu as pltpu
from jax.sharding import Mesh
from jax.sharding import PartitionSpec as P

F32 = jnp.float32
BF16 = jnp.bfloat16
LANES = 128
PAD = 16
LOG2E = 1.4426950408889634
NT = (((1,), (1,)), ((), ()))
NN = (((1,), (0,)), ((), ()))
LARGE = pltpu.CompilerParams(vmem_limit_bytes=58 * 1024 * 1024)
MEDIUM = pltpu.CompilerParams(vmem_limit_bytes=28 * 1024 * 1024)
SMALL = pltpu.CompilerParams(vmem_limit_bytes=12 * 1024 * 1024)
VMEM = pl.BlockSpec(memory_space=pltpu.VMEM)
SMEM = pl.BlockSpec(memory_space=pltpu.SMEM)
HBM = pl.BlockSpec(memory_space=pl.ANY)


def pack_kernel(
    heads, place_ref, q_hbm, g_hbm, o_hbm, k_hbm, v_hbm,
    qg_own, qg_oth, kv_own, kv_oth, q_ref, g_ref, o_ref, k_ref, v_ref, sems,
):
    pairs = ((k_hbm, k_ref), (v_hbm, v_ref), (q_hbm, q_ref), (g_hbm, g_ref), (o_hbm, o_ref))
    copies = [pltpu.make_async_copy(a, b, sems.at[i]) for i, (a, b) in enumerate(pairs)]
    for copy in copies:
        copy.start()
    half = qg_own.shape[1]
    rows, width = q_ref.shape[1:]
    krows = k_ref.shape[1]
    head_dim = width // heads
    local = heads // 2
    swapped = place_ref[2] == 1
    for copy in copies:
        copy.wait()

    def halves(piece):
        low, high = piece[:, :half], piece[:, half:]
        return jnp.where(swapped, high, low), jnp.where(swapped, low, high)

    kv_own[:krows], kv_oth[:krows] = halves(k_ref[0])
    kv_own[krows:], kv_oth[krows:] = halves(v_ref[0])
    qg_own[:rows], qg_oth[:rows] = halves(q_ref[0])
    qg_own[rows : 2 * rows], qg_oth[rows : 2 * rows] = halves(g_ref[0])
    product = g_ref[0].astype(F32) * o_ref[0].astype(F32)
    feature = lax.broadcasted_iota(jnp.int32, (2 * PAD, width), 1)
    head = lax.broadcasted_iota(jnp.int32, (2 * PAD, width), 0)
    wanted = jnp.where(head % PAD < local, head // PAD * local + head % PAD, -1)
    pick = (feature // head_dim == wanted).astype(F32)
    delta = lax.dot_general(
        pick, product, NT, precision=lax.Precision.HIGHEST, preferred_element_type=F32
    ).astype(BF16)
    for ref, swap in ((qg_own, swapped), (qg_oth, jnp.logical_not(swapped))):
        ref[2 * rows :, :rows] = jnp.where(swap, delta[PAD:], delta[:PAD])
        ref[2 * rows :, rows:] = jnp.zeros((PAD, half - rows), BF16)


def pair_kernel(head_dim, tile, capacity, sources, key_sources, place_ref, info_ref, *refs):
    qg_refs, refs = refs[:sources], refs[sources:]
    kv_refs, refs = refs[:key_sources], refs[key_sources:]
    own_ref, sib_ref, lse_ref = refs[:3]
    refs = refs[3:]
    dq_refs, refs = refs[:sources], refs[sources:]
    dkv_refs, refs = refs[:key_sources], refs[key_sources:]
    q_scr, g_scr, k_scr, v_scr, k2t_scr, lse_scr, delta_scr, dqt_scr, dk_scr, dv_scr = refs
    half = q_scr.shape[1]
    rows = dq_refs[0].shape[0]
    krows = dkv_refs[0].shape[0] // 2
    key_count = k_scr.shape[1]
    key_tiles = key_count // tile
    pairs = half // LANES
    scaling = float(head_dim) ** -0.5
    row, chip, core = place_ref[0], place_ref[1], place_ref[2]
    column = chip * 2 + core
    line = row * 2 + core

    lse_scr[...] = lse_ref[core] * LOG2E
    for step in range(sources):
        source = column ^ step
        start = pl.multiple_of(source * rows, rows)
        q_scr[pl.ds(start, rows)] = qg_refs[step][:rows]
        g_scr[pl.ds(start, rows)] = qg_refs[step][rows : 2 * rows]
        delta = qg_refs[step][2 * rows :, :rows].astype(F32)
        tiles_of = source * rows // tile
        if rows == tile:
            delta_scr[tiles_of] = delta
        else:
            for inner in range(tile // rows):
                @pl.when(source % (tile // rows) == inner)
                def _(inner=inner, delta=delta, tiles_of=tiles_of):
                    delta_scr[tiles_of, :, inner * rows : (inner + 1) * rows] = delta
    for step in range(key_sources):
        source = line ^ step
        start = pl.multiple_of(source // 2 * krows, krows)
        k_scr[source % 2, pl.ds(start, krows)] = kv_refs[step][:krows]
        v_scr[source % 2, pl.ds(start, krows)] = kv_refs[step][krows:]
    low_lane = lax.broadcasted_iota(jnp.int32, (tile, LANES), 1) < head_dim
    low_row = lax.broadcasted_iota(jnp.int32, (LANES, tile), 0) < head_dim
    zero = jnp.zeros((tile, LANES), BF16)
    zero_t = jnp.zeros((LANES, tile), BF16)
    bit = lax.shift_left(
        jnp.int32(1), lax.broadcasted_iota(jnp.int32, (tile // 16, 16, tile), 1)
    ).reshape(tile, tile)

    for block in range(2):
        for w in range(key_tiles):
            flipped = k_scr[block, w * tile : (w + 1) * tile].T
            for pair in range(pairs):
                part = flipped[pair * LANES : (pair + 1) * LANES]
                k2t_scr[block * key_tiles + w, pair] = jnp.concatenate(
                    [jnp.where(low_row, part, zero_t), jnp.where(low_row, zero_t, part)], axis=1
                )
    dqt_scr[...] = jnp.zeros_like(dqt_scr)
    dk_scr[...] = jnp.zeros_like(dk_scr)
    dv_scr[...] = jnp.zeros_like(dv_scr)

    def twice(piece):
        return jnp.concatenate(
            [jnp.where(low_lane, piece, zero), jnp.where(low_lane, zero, piece)], axis=0
        )

    for which, bits_ref in enumerate((own_ref, sib_ref)):
        base = which * (capacity + 1)
        block = core if which == 0 else 1 - core

        def one_tile(entry, _, base=base, block=block, bits_ref=bits_ref):
            slot = info_ref[base + entry]
            u = slot // key_tiles
            w = slot % key_tiles
            kidx = block * key_tiles + w
            qrow = pl.multiple_of(u * tile, tile)
            krow = pl.multiple_of(w * tile, tile)
            words = bits_ref[entry]
            words = jnp.broadcast_to(words[:, None, :], (tile // 16, 16, tile)).reshape(tile, tile)
            edge = (words & bit) != 0
            k_tile = k_scr[block, pl.ds(krow, tile)]
            v_tile = v_scr[block, pl.ds(krow, tile)]
            q_tile = q_scr[pl.ds(qrow, tile)]
            g_tile = g_scr[pl.ds(qrow, tile)]
            lse_tile = lse_scr[:, pl.ds(qrow, tile)]
            delta_tile = delta_scr[u]
            for pair in range(pairs):
                lanes = slice(pair * LANES, (pair + 1) * LANES)
                q2 = twice(q_tile[:, lanes])
                g2 = twice(g_tile[:, lanes])
                scores = lax.dot_general(k_tile[:, lanes], q2, NT, preferred_element_type=F32)
                grad_prob = lax.dot_general(v_tile[:, lanes], g2, NT, preferred_element_type=F32)
                probs, grads = [], []
                for side in range(2):
                    h = 2 * pair + side
                    s = scores[:, side * tile : (side + 1) * tile]
                    gp = grad_prob[:, side * tile : (side + 1) * tile]
                    p = jnp.exp2(s * (scaling * LOG2E) - lse_tile[h : h + 1])
                    p = jnp.where(edge, p, 0.0)
                    ds = p * (gp - delta_tile[h : h + 1])
                    probs.append(p.astype(BF16))
                    grads.append(ds.astype(BF16))
                p2 = jnp.concatenate(probs, axis=1)
                ds2 = jnp.concatenate(grads, axis=1)
                dv_scr[kidx, :, lanes] += lax.dot_general(p2, g2, NN, preferred_element_type=F32)
                dk_scr[kidx, :, lanes] += lax.dot_general(ds2, q2, NN, preferred_element_type=F32)
                dqt_scr[u, lanes] += lax.dot_general(
                    k2t_scr[kidx, pair], jnp.concatenate(grads, axis=0), NN,
                    preferred_element_type=F32,
                )
            return 0

        lax.fori_loop(0, info_ref[base + capacity], one_tile, 0)

    for step in range(key_sources):
        target = line ^ step
        start = target // 2 * krows
        kidx = target % 2 * key_tiles + start // tile
        inner = pl.multiple_of(start % tile, krows)
        dk = dk_scr[kidx, pl.ds(inner, krows)] * scaling
        dkv_refs[step][:krows] = dk.astype(BF16)
        dkv_refs[step][krows:] = dv_scr[kidx, pl.ds(inner, krows)].astype(BF16)
    for u in range(dqt_scr.shape[0]):
        q_scr[u * tile : (u + 1) * tile] = (dqt_scr[u] * scaling).T.astype(BF16)
    for step in range(sources):
        start = pl.multiple_of((column ^ step) * rows, rows)
        dq_refs[step][...] = q_scr[pl.ds(start, rows)]


def sum_kernel(sources, key_sources, place_ref, *refs):
    dq_refs, refs = refs[:sources], refs[sources:]
    dkv_refs, refs = refs[:key_sources], refs[key_sources:]
    dq_out, dk_out, dv_out = refs
    krows = dkv_refs[0].shape[0] // 2
    half = dq_refs[0].shape[1]
    swapped = place_ref[2] == 1

    def total(parts):
        own = parts[0][...].astype(F32)
        other = parts[1][...].astype(F32)
        for step in range(2, len(parts), 2):
            own += parts[step][...].astype(F32)
            other += parts[step + 1][...].astype(F32)
        own, other = own.astype(BF16), other.astype(BF16)
        return jnp.where(swapped, other, own), jnp.where(swapped, own, other)

    low, high = total(dkv_refs)
    dk_out[0, :, :half], dk_out[0, :, half:] = low[:krows], high[:krows]
    dv_out[0, :, :half], dv_out[0, :, half:] = low[krows:], high[krows:]
    low, high = total(dq_refs)
    dq_out[0, :, :half], dq_out[0, :, half:] = low, high


def exchange(own_of, axes, count):
    out = [own_of(0)]
    for step in range(1, count):
        pairs = [(place, place ^ step) for place in range(count)]
        out.append(lax.ppermute(own_of(step), axes, pairs))
    return out


def body(sizes, queries, keys, values, outputs, grad_out, lse, tile_slot, tile_live, tile_bits):
    row_count, chips, cores = sizes
    heads = lse.shape[1]
    width = queries.shape[2]
    half = width // cores
    head_dim = width // heads
    local = heads // cores
    tile = tile_bits.shape[4]
    capacity = tile_slot.shape[2]
    rows = queries.shape[1]
    krows = keys.shape[1]
    sources = chips * cores
    key_sources = row_count * cores
    query_count = lse.shape[2]
    key_count = row_count * krows
    key_tiles = key_count // tile
    swap = [(core, cores - 1 - core) for core in range(cores)]
    place = jnp.stack([lax.axis_index(name) for name in ("row", "chip", "core")]).astype(jnp.int32)

    qg_shape = jax.ShapeDtypeStruct((2 * rows + PAD, half), BF16)
    kv_shape = jax.ShapeDtypeStruct((2 * krows, half), BF16)
    dq_shape = jax.ShapeDtypeStruct((rows, half), BF16)
    qg_own, qg_oth, kv_own, kv_oth = pl.pallas_call(
        functools.partial(pack_kernel, heads),
        out_shape=(qg_shape, qg_shape, kv_shape, kv_shape),
        in_specs=[SMEM] + [HBM] * 5,
        out_specs=(VMEM,) * 4,
        scratch_shapes=[
            pltpu.VMEM(queries.shape, BF16),
            pltpu.VMEM(queries.shape, BF16),
            pltpu.VMEM(queries.shape, BF16),
            pltpu.VMEM(keys.shape, BF16),
            pltpu.VMEM(keys.shape, BF16),
            pltpu.SemaphoreType.DMA((5,)),
        ],
        compiler_params=LARGE,
        name="pack",
    )(place, queries, grad_out, outputs, keys, values)
    kv = exchange(lambda step: (kv_own, kv_oth)[step % 2], ("row", "core"), key_sources)
    qg = exchange(lambda step: (qg_own, qg_oth)[step % 2], ("chip", "core"), sources)
    info = jnp.concatenate([tile_slot[0, 0], tile_live[0]])
    info = jnp.concatenate([info, lax.ppermute(info, "core", swap)])
    bits = tile_bits[0, 0]
    bits_sib = lax.ppermute(bits, "core", swap)

    parts = pl.pallas_call(
        functools.partial(pair_kernel, head_dim, tile, capacity, sources, key_sources),
        out_shape=(dq_shape,) * sources + (kv_shape,) * key_sources,
        in_specs=[SMEM] * 2 + [VMEM] * (sources + key_sources + 3),
        out_specs=(VMEM,) * (sources + key_sources),
        scratch_shapes=[
            pltpu.VMEM((query_count, half), BF16),
            pltpu.VMEM((query_count, half), BF16),
            pltpu.VMEM((cores, key_count, half), BF16),
            pltpu.VMEM((cores, key_count, half), BF16),
            pltpu.VMEM((cores * key_tiles, half // LANES, LANES, 2 * tile), BF16),
            pltpu.VMEM((local, query_count), F32),
            pltpu.VMEM((query_count // tile, PAD, tile), F32),
            pltpu.VMEM((query_count // tile, half, tile), F32),
            pltpu.VMEM((cores * key_tiles, tile, half), F32),
            pltpu.VMEM((cores * key_tiles, tile, half), F32),
        ],
        compiler_params=MEDIUM,
        name="pair",
    )(place, info, *qg, *kv, bits, bits_sib, lse.reshape(cores, local, query_count))

    dq_parts, dkv_parts = parts[:sources], parts[sources:]
    dkv = exchange(lambda step: dkv_parts[step], ("row", "core"), key_sources)
    dq = exchange(lambda step: dq_parts[step], ("chip", "core"), sources)
    return pl.pallas_call(
        functools.partial(sum_kernel, sources, key_sources),
        out_shape=(
            jax.ShapeDtypeStruct((1, rows, width), BF16),
            jax.ShapeDtypeStruct((1, krows, width), BF16),
            jax.ShapeDtypeStruct((1, krows, width), BF16),
        ),
        in_specs=[SMEM] + [VMEM] * (sources + key_sources),
        out_specs=(VMEM, VMEM, VMEM),
        compiler_params=SMALL,
        name="total",
    )(place, *dq, *dkv)


def solution(mesh):
    row_count, columns = mesh.devices.shape
    cores = 2
    chips = columns // cores
    fine = Mesh(mesh.devices.reshape(row_count, chips, cores), ("row", "chip", "core"))
    col = ("chip", "core")
    in_specs = (
        P("row", col, None),
        P(col, "row", None),
        P(col, "row", None),
        P("row", col, None),
        P("row", col, None),
        P("row", None, None),
        P("row", col, None),
        P("row", col),
        P("row", col, None, None, None),
    )
    out_specs = (P("row", col, None), P(col, "row", None), P(col, "row", None))
    return jax.shard_map(
        functools.partial(body, (row_count, chips, cores)),
        mesh=fine, in_specs=in_specs, out_specs=out_specs, check_vma=False,
    )
```

```python
import functools

import jax
import jax.numpy as jnp
from jax import lax
from jax.experimental import pallas as pl
from jax.experimental.pallas import tpu as pltpu
from jax.sharding import Mesh
from jax.sharding import PartitionSpec as P


F32 = jnp.float32
BF16 = jnp.bfloat16
I32 = jnp.int32
LANES = 128
PAD = 16
QUARTERS = 4
LOG2E = 1.4426950408889634
NT = (((1,), (1,)), ((), ()))
NN = (((1,), (0,)), ((), ()))
LARGE = pltpu.CompilerParams(vmem_limit_bytes=58 * 1024 * 1024)
MEDIUM = pltpu.CompilerParams(vmem_limit_bytes=28 * 1024 * 1024)
SMALL = pltpu.CompilerParams(vmem_limit_bytes=12 * 1024 * 1024)
VMEM = pl.BlockSpec(memory_space=pltpu.VMEM)
SMEM = pl.BlockSpec(memory_space=pltpu.SMEM)
HBM = pl.BlockSpec(memory_space=pl.ANY)


def lanes_of(quarter):
    return pl.ds(pl.multiple_of(quarter * LANES, LANES), LANES)


def pack_kernel(
    heads, place_ref, q_hbm, g_hbm, o_hbm, k_hbm, v_hbm, bits_hbm, slot_ref, live_ref, *refs
):
    qg_refs, refs = refs[:QUARTERS], refs[QUARTERS:]
    kv_refs, refs = refs[:QUARTERS], refs[QUARTERS:]
    packed_ref, q_ref, g_ref, o_ref, k_ref, v_ref, bits_ref, delta_ref, sems = refs
    arrays = (
        (q_hbm, q_ref), (g_hbm, g_ref), (o_hbm, o_ref),
        (k_hbm, k_ref), (v_hbm, v_ref), (bits_hbm, bits_ref),
    )
    copies = [pltpu.make_async_copy(a, b, sems.at[i]) for i, (a, b) in enumerate(arrays)]
    for copy in copies:
        copy.start()
    rows, width = q_ref.shape[1:]
    krows = k_ref.shape[1]
    head_dim = width // heads
    local = heads // QUARTERS
    capacity = bits_ref.shape[2]
    quarter = place_ref[0] % 2 * 2 + place_ref[2]
    feature = lax.broadcasted_iota(I32, (QUARTERS * PAD, width), 1)
    line = lax.broadcasted_iota(I32, (QUARTERS * PAD, width), 0)
    wanted = jnp.where(line % PAD < local, line // PAD * local + line % PAD, -1)
    pick = (feature // head_dim == wanted).astype(F32)
    for copy in copies:
        copy.wait()
    product = g_ref[0].astype(F32) * o_ref[0].astype(F32)
    delta = lax.dot_general(
        pick, product, NT, precision=lax.Precision.HIGHEST, preferred_element_type=F32
    ).astype(BF16)
    for index in range(QUARTERS):
        delta_ref[index] = delta[index * PAD : (index + 1) * PAD]
    for step in range(QUARTERS):
        target = quarter ^ step
        lanes = lanes_of(target)
        qg_refs[step][:rows] = q_ref[0, :, lanes]
        qg_refs[step][rows : 2 * rows] = g_ref[0, :, lanes]
        if rows < LANES:
            qg_refs[step][2 * rows :] = jnp.zeros((PAD, LANES), BF16)
        qg_refs[step][2 * rows :, :rows] = delta_ref[target]
        kv_refs[step][:krows] = k_ref[0, :, lanes]
        kv_refs[step][krows:] = v_ref[0, :, lanes]
    for entry in range(capacity):
        words = bits_ref[0, 0, entry]
        span = slice(entry % 2 * 4, entry % 2 * 4 + 4)
        packed_ref[entry // 2, span] = words[:4] | lax.shift_left(words[4:], I32(16))
    packed_ref[capacity // 2] = jnp.zeros((8, LANES), I32)
    packed_ref[capacity // 2, 0:1, 0:capacity] = slot_ref[0]
    packed_ref[capacity // 2, 1:2, 0:1] = live_ref[...]


def join_kernel(place_ref, *refs):
    out = refs[-1]
    quarter = place_ref[0] % 2 * 2 + place_ref[2]
    for step in range(QUARTERS):
        out[quarter ^ step] = refs[step][...]


def pair_kernel(sizes, place_ref, *refs):
    head_dim, tile, capacity, chips, key_sources = sizes
    qg_refs, refs = refs[:chips], refs[chips:]
    kv_refs, refs = refs[:key_sources], refs[key_sources:]
    bits_refs, refs = refs[:QUARTERS], refs[QUARTERS:]
    lse_refs, refs = refs[:2], refs[2:]
    dq_refs, refs = refs[:chips], refs[chips:]
    dkv_refs, refs = refs[:key_sources], refs[key_sources:]
    (q2_scr, g2_scr, k_scr, v_scr, k2t_scr, lse_scr, delta_scr, dqt_scr, dk_scr, dv_scr, dq_scr,
     info, sems) = refs
    rows = (qg_refs[0].shape[1] - PAD) // 2
    krows = kv_refs[0].shape[0] // 2
    query_tiles = q2_scr.shape[1]
    key_tiles = k_scr.shape[1]
    scaling = float(head_dim) ** -0.5
    row, chip, core = place_ref[0], place_ref[1], place_ref[2]
    side = row % 2
    quarter = side * 2 + core
    line = row * 2 + core

    copies = [
        pltpu.make_async_copy(ref.at[capacity // 2], info.at[i], sems.at[i])
        for i, ref in enumerate(bits_refs)
    ]
    for copy in copies:
        copy.start()

    for step, ref in enumerate(lse_refs):
        every = ref[0] * LOG2E
        own = every[:2]
        for index in range(1, QUARTERS):
            own = jnp.where(quarter == index, every[2 * index : 2 * index + 2], own)
        for u in range(query_tiles):
            lse_scr[side ^ step, u] = own[:, u * tile : (u + 1) * tile]
    low = lax.broadcasted_iota(I32, (rows, LANES), 1) < head_dim
    none = jnp.zeros((rows, LANES), BF16)
    for step in range(chips):
        for index in range(QUARTERS):
            source = (chip ^ step) * 2 + index % 2
            start = source * rows
            u = start // tile
            inner = pl.multiple_of(start % tile, rows)
            block = index // 2
            for scr, part in ((q2_scr, 0), (g2_scr, 1)):
                piece = qg_refs[step][index, part * rows : (part + 1) * rows]
                scr[block, u, 0, pl.ds(inner, rows)] = jnp.where(low, piece, none)
                scr[block, u, 1, pl.ds(inner, rows)] = jnp.where(low, none, piece)
            delta = qg_refs[step][index, 2 * rows :, :rows].astype(F32)
            if rows == tile:
                delta_scr[block, u] = delta
            else:
                for part in range(tile // rows):
                    @pl.when(source % (tile // rows) == part)
                    def _(part=part, delta=delta, u=u, block=block):
                        delta_scr[block, u, :, part * rows : (part + 1) * rows] = delta
    for step in range(key_sources):
        source = line ^ step
        start = source // 2 * krows
        inner = pl.multiple_of(start % tile, krows)
        k_scr[source % 2, start // tile, pl.ds(inner, krows)] = kv_refs[step][:krows]
        v_scr[source % 2, start // tile, pl.ds(inner, krows)] = kv_refs[step][krows:]
    low_row = lax.broadcasted_iota(I32, (LANES, tile), 0) < head_dim
    none_t = jnp.zeros((LANES, tile), BF16)
    for block in range(2):
        for w in range(key_tiles):
            flipped = k_scr[block, w].T
            k2t_scr[block, w] = jnp.concatenate(
                [jnp.where(low_row, flipped, none_t), jnp.where(low_row, none_t, flipped)], axis=1
            )
    dqt_scr[...] = jnp.zeros_like(dqt_scr)
    dk_scr[...] = jnp.zeros_like(dk_scr)
    dv_scr[...] = jnp.zeros_like(dv_scr)
    place_in = lax.broadcasted_iota(I32, (2, 4, 16, tile), 2)
    upper = lax.broadcasted_iota(I32, (2, 4, 16, tile), 0)
    bit = lax.shift_left(I32(1), place_in + 16 * upper).reshape(tile, tile)
    for copy in copies:
        copy.wait()

    for step in range(QUARTERS):
        qb = side ^ (step // 2)
        kb = core ^ (step % 2)
        live = info[step, 1, 0]
        bits_ref = bits_refs[step]

        def two_tiles(index, _, step=step, qb=qb, kb=kb, live=live, bits_ref=bits_ref):
            both = bits_ref[index]
            second = jnp.where(index * 2 + 1 < live, I32(-1), I32(0))
            work = []
            for part in range(2):
                slot = info[step, 0, index * 2 + part]
                u = slot // key_tiles
                w = slot % key_tiles
                words = both[part * 4 : part * 4 + 4]
                if part:
                    words = words & second
                words = jnp.broadcast_to(words[:, None, :], (4, 16, tile)).reshape(64, tile)
                edge = (jnp.concatenate([words, words], axis=0) & bit) != 0
                q2 = q2_scr[qb, u].reshape(2 * tile, LANES)
                g2 = g2_scr[qb, u].reshape(2 * tile, LANES)
                scores = lax.dot_general(k_scr[kb, w], q2, NT, preferred_element_type=F32)
                grad_prob = lax.dot_general(v_scr[kb, w], g2, NT, preferred_element_type=F32)
                work.append((u, w, edge, q2, g2, scores, grad_prob))
            done = []
            for u, w, edge, q2, g2, scores, grad_prob in work:
                lse_tile = lse_scr[qb, u]
                delta_tile = delta_scr[qb, u]
                probs, grads = [], []
                for h in range(2):
                    s = scores[:, h * tile : (h + 1) * tile]
                    gp = grad_prob[:, h * tile : (h + 1) * tile]
                    p = jnp.exp2(s * (scaling * LOG2E) - lse_tile[h : h + 1])
                    p = jnp.where(edge, p, 0.0)
                    ds = p * (gp - delta_tile[h : h + 1])
                    probs.append(p.astype(BF16))
                    grads.append(ds.astype(BF16))
                done.append((
                    lax.dot_general(
                        jnp.concatenate(probs, axis=1), g2, NN, preferred_element_type=F32
                    ),
                    lax.dot_general(
                        jnp.concatenate(grads, axis=1), q2, NN, preferred_element_type=F32
                    ),
                    lax.dot_general(
                        k2t_scr[kb, w], jnp.concatenate(grads, axis=0), NN,
                        preferred_element_type=F32,
                    ),
                ))
            for (u, w, *_), (dv, dk, dqt) in zip(work, done):
                dv_scr[kb, w] += dv
                dk_scr[kb, w] += dk
                dqt_scr[qb, u] += dqt
            return 0

        lax.fori_loop(0, (live + 1) // 2, two_tiles, 0)

    for step in range(key_sources):
        target = line ^ step
        start = target // 2 * krows
        inner = pl.multiple_of(start % tile, krows)
        dk = dk_scr[target % 2, start // tile, pl.ds(inner, krows)] * scaling
        dv = dv_scr[target % 2, start // tile, pl.ds(inner, krows)]
        dkv_refs[step][:krows] = dk.astype(BF16)
        dkv_refs[step][krows:] = dv.astype(BF16)
    for block in range(2):
        for u in range(query_tiles):
            dq_scr[block, u * tile : (u + 1) * tile] = (dqt_scr[block, u] * scaling).astype(BF16).T
    for step in range(chips):
        for index in range(QUARTERS):
            start = pl.multiple_of(((chip ^ step) * 2 + index % 2) * rows, rows)
            dq_refs[step][index] = dq_scr[index // 2, pl.ds(start, rows)]


def query_sum_kernel(chips, place_ref, *refs):
    parts, outs = refs[:chips], refs[chips:]
    quarter = place_ref[0] % 2 * 2 + place_ref[2]
    for step in range(QUARTERS):
        target = quarter ^ step
        total = parts[0][target].astype(F32)
        for part in parts[1:]:
            total += part[target].astype(F32)
        outs[step][...] = total.astype(BF16)


def finish_kernel(key_sources, place_ref, *refs):
    dq_refs, refs = refs[:QUARTERS], refs[QUARTERS:]
    dkv_refs, refs = refs[:key_sources], refs[key_sources:]
    dq_out, dk_out, dv_out = refs
    krows = dkv_refs[0].shape[0] // 2
    quarter = place_ref[0] % 2 * 2 + place_ref[2]
    for step in range(QUARTERS):
        lanes = lanes_of(quarter ^ step)
        dq_out[0, :, lanes] = dq_refs[step][...]
        total = dkv_refs[step][...].astype(F32)
        for other in range(step + QUARTERS, key_sources, QUARTERS):
            total += dkv_refs[other][...].astype(F32)
        total = total.astype(BF16)
        dk_out[0, :, lanes] = total[:krows]
        dv_out[0, :, lanes] = total[krows:]


def send(block, axes, count, step):
    return lax.ppermute(block, axes, [(place, place ^ step) for place in range(count)])


def body(sizes, queries, keys, values, outputs, grad_out, lse, tile_slot, tile_live, tile_bits):
    row_count, chips, cores = sizes
    heads = lse.shape[1]
    width = queries.shape[2]
    head_dim = width // heads
    tile = tile_bits.shape[4]
    capacity = tile_slot.shape[2]
    rows = queries.shape[1]
    krows = keys.shape[1]
    key_sources = row_count * cores
    query_tiles = lse.shape[2] // tile
    key_tiles = row_count * krows // tile
    line = ("row", "core")
    place = jnp.stack([lax.axis_index(name) for name in ("row", "chip", "core")]).astype(I32)

    qg_shape = jax.ShapeDtypeStruct((2 * rows + PAD, LANES), BF16)
    kv_shape = jax.ShapeDtypeStruct((2 * krows, LANES), BF16)
    packed_shape = jax.ShapeDtypeStruct((capacity // 2 + 1, 8, LANES), I32)
    packed = pl.pallas_call(
        functools.partial(pack_kernel, heads),
        out_shape=(qg_shape,) * QUARTERS + (kv_shape,) * QUARTERS + (packed_shape,),
        in_specs=[SMEM] + [HBM] * 6 + [VMEM] * 2,
        out_specs=(VMEM,) * (2 * QUARTERS + 1),
        scratch_shapes=[
            pltpu.VMEM(queries.shape, BF16),
            pltpu.VMEM(queries.shape, BF16),
            pltpu.VMEM(queries.shape, BF16),
            pltpu.VMEM(keys.shape, BF16),
            pltpu.VMEM(keys.shape, BF16),
            pltpu.VMEM(tile_bits.shape, I32),
            pltpu.VMEM((QUARTERS, PAD, rows), BF16),
            pltpu.SemaphoreType.DMA((6,)),
        ],
        compiler_params=LARGE,
        name="pack",
    )(place, queries, grad_out, outputs, keys, values, tile_bits, tile_slot, tile_live)
    qg_own, kv_own, bits_own = packed[:QUARTERS], packed[QUARTERS : 2 * QUARTERS], packed[-1]

    qg_group = [qg_own[0]] + [
        send(qg_own[step], line, key_sources, step) for step in range(1, QUARTERS)
    ]
    bits = [bits_own] + [send(bits_own, line, key_sources, step) for step in range(1, QUARTERS)]
    lse_other = send(lse, "row", row_count, 1)
    joined = pl.pallas_call(
        join_kernel,
        out_shape=jax.ShapeDtypeStruct((QUARTERS,) + qg_shape.shape, BF16),
        in_specs=[SMEM] + [VMEM] * QUARTERS,
        out_specs=VMEM,
        compiler_params=SMALL,
        name="join",
    )(place, *qg_group)
    qg = [joined] + [send(joined, "chip", chips, step) for step in range(1, chips)]
    kv = [kv_own[0]] + [
        send(kv_own[step % QUARTERS], line, key_sources, step) for step in range(1, key_sources)
    ]

    dq_shape = jax.ShapeDtypeStruct((QUARTERS, rows, LANES), BF16)
    parts = pl.pallas_call(
        functools.partial(pair_kernel, (head_dim, tile, capacity, chips, key_sources)),
        out_shape=(dq_shape,) * chips + (kv_shape,) * key_sources,
        in_specs=[SMEM] + [VMEM] * (chips + key_sources + QUARTERS + 2),
        out_specs=(VMEM,) * (chips + key_sources),
        scratch_shapes=[
            pltpu.VMEM((2, query_tiles, 2, tile, LANES), BF16),
            pltpu.VMEM((2, query_tiles, 2, tile, LANES), BF16),
            pltpu.VMEM((2, key_tiles, tile, LANES), BF16),
            pltpu.VMEM((2, key_tiles, tile, LANES), BF16),
            pltpu.VMEM((2, key_tiles, LANES, 2 * tile), BF16),
            pltpu.VMEM((2, query_tiles, 2, tile), F32),
            pltpu.VMEM((2, query_tiles, PAD, tile), F32),
            pltpu.VMEM((2, query_tiles, LANES, tile), F32),
            pltpu.VMEM((2, key_tiles, tile, LANES), F32),
            pltpu.VMEM((2, key_tiles, tile, LANES), F32),
            pltpu.VMEM((2, query_tiles * tile, LANES), BF16),
            pltpu.SMEM((QUARTERS, 8, LANES), I32),
            pltpu.SemaphoreType.DMA((QUARTERS,)),
        ],
        compiler_params=MEDIUM,
        name="pair",
    )(place, *qg, *kv, *bits, lse, lse_other)

    dq_parts, dkv_parts = parts[:chips], parts[chips:]
    dq_parts = [dq_parts[0]] + [
        send(dq_parts[step], "chip", chips, step) for step in range(1, chips)
    ]
    dkv = [dkv_parts[0]] + [
        send(dkv_parts[step], line, key_sources, step) for step in range(1, key_sources)
    ]
    dq = pl.pallas_call(
        functools.partial(query_sum_kernel, chips),
        out_shape=(jax.ShapeDtypeStruct((rows, LANES), BF16),) * QUARTERS,
        in_specs=[SMEM] + [VMEM] * chips,
        out_specs=(VMEM,) * QUARTERS,
        compiler_params=SMALL,
        name="query_sum",
    )(place, *dq_parts)
    dq = [dq[0]] + [send(dq[step], line, key_sources, step) for step in range(1, QUARTERS)]
    return pl.pallas_call(
        functools.partial(finish_kernel, key_sources),
        out_shape=(
            jax.ShapeDtypeStruct((1, rows, width), BF16),
            jax.ShapeDtypeStruct((1, krows, width), BF16),
            jax.ShapeDtypeStruct((1, krows, width), BF16),
        ),
        in_specs=[SMEM] + [VMEM] * (QUARTERS + key_sources),
        out_specs=(VMEM, VMEM, VMEM),
        compiler_params=SMALL,
        name="finish",
    )(place, *dq, *dkv)


def solution(mesh):
    row_count, columns = mesh.devices.shape
    cores = 2
    chips = columns // cores
    fine = Mesh(mesh.devices.reshape(row_count, chips, cores), ("row", "chip", "core"))
    col = ("chip", "core")
    in_specs = (
        P("row", col, None),
        P(col, "row", None),
        P(col, "row", None),
        P("row", col, None),
        P("row", col, None),
        P("row", None, None),
        P("row", col, None),
        P("row", col),
        P("row", col, None, None, None),
    )
    out_specs = (P("row", col, None), P(col, "row", None), P(col, "row", None))
    return jax.shard_map(
        functools.partial(body, (row_count, chips, cores)),
        mesh=fine, in_specs=in_specs, out_specs=out_specs, check_vma=False,
    )
```

```python
import functools

import jax
import jax.numpy as jnp
from jax import lax
from jax.experimental import pallas as pl
from jax.experimental.pallas import tpu as pltpu
from jax.sharding import Mesh
from jax.sharding import PartitionSpec as P


F32 = jnp.float32
BF16 = jnp.bfloat16
I32 = jnp.int32
LANES = 128
PAD = 16
QUARTERS = 4
LOG2E = 1.4426950408889634
NT = (((1,), (1,)), ((), ()))
NN = (((1,), (0,)), ((), ()))
MEDIUM = pltpu.CompilerParams(vmem_limit_bytes=28 * 1024 * 1024)
SMALL = pltpu.CompilerParams(vmem_limit_bytes=12 * 1024 * 1024)
VMEM = pl.BlockSpec(memory_space=pltpu.VMEM)
HBM = pl.BlockSpec(memory_space=pltpu.HBM)


def lanes_of(quarter):
    return pl.ds(pl.multiple_of(quarter * LANES, LANES), LANES)


def my_place():
    row, chip, core = (lax.axis_index(name) for name in ("row", "chip", "core"))
    return row, chip, core, row % 2 * 2 + core


def pack_kernel(
    heads, q_hbm, g_hbm, o_hbm, k_hbm, v_hbm, bits_hbm, slot_ref, live_ref,
    qg_own, qg_pair0, qg_pair1, kv_own, sib_ref, packed_ref,
    q_ref, g_ref, o_ref, k_ref, v_ref, bits_ref, delta_ref, sems,
):
    arrays = (
        (q_hbm, q_ref), (g_hbm, g_ref), (o_hbm, o_ref),
        (k_hbm, k_ref), (v_hbm, v_ref), (bits_hbm, bits_ref),
    )
    copies = [pltpu.make_async_copy(a, b, sems.at[i]) for i, (a, b) in enumerate(arrays)]
    for copy in copies:
        copy.start()
    rows, width = q_ref.shape[1:]
    krows = k_ref.shape[1]
    head_dim = width // heads
    local = heads // QUARTERS
    capacity = bits_ref.shape[2]
    quarter = my_place()[3]
    feature = lax.broadcasted_iota(I32, (QUARTERS * PAD, width), 1)
    line = lax.broadcasted_iota(I32, (QUARTERS * PAD, width), 0)
    wanted = jnp.where(line % PAD < local, line // PAD * local + line % PAD, -1)
    pick = (feature // head_dim == wanted).astype(F32)
    packed_ref[capacity // 2] = jnp.zeros((8, LANES), I32)
    packed_ref[capacity // 2, 0:1, 0:capacity] = slot_ref[0]
    packed_ref[capacity // 2, 1:2, 0:1] = live_ref[...]
    for copy in copies:
        copy.wait()
    product = g_ref[0].astype(F32) * o_ref[0].astype(F32)
    delta = lax.dot_general(
        pick, product, NT, precision=lax.Precision.HIGHEST, preferred_element_type=F32
    ).astype(BF16)
    for index in range(QUARTERS):
        delta_ref[index] = delta[index * PAD : (index + 1) * PAD]
    base = 4 * krows
    for step, (ref, start) in enumerate(
        ((qg_own, 0), (sib_ref, base), (qg_pair0, 0), (qg_pair1, 0))
    ):
        lanes = lanes_of(quarter ^ step)
        ref[start : start + rows] = q_ref[0, :, lanes]
        ref[start + rows : start + 2 * rows] = g_ref[0, :, lanes]
        if rows < LANES:
            ref[start + 2 * rows : start + 2 * rows + PAD] = jnp.zeros((PAD, LANES), BF16)
        ref[start + 2 * rows : start + 2 * rows + PAD, :rows] = delta_ref[quarter ^ step]
    for side in range(2):
        for ref, step in ((kv_own, 2 * side), (sib_ref, 2 * side + 1)):
            lanes = lanes_of(quarter ^ step)
            start = side * 2 * krows
            ref[start : start + krows] = k_ref[0, :, lanes]
            ref[start + krows : start + 2 * krows] = v_ref[0, :, lanes]
    for entry in range(capacity):
        words = bits_ref[0, 0, entry]
        span = slice(entry % 2 * 4, entry % 2 * 4 + 4)
        packed_ref[entry // 2, span] = words[:4] | lax.shift_left(words[4:], I32(16))


def join_kernel(
    krows, qg_own, qg_pair0, qg_pair1, kv_own, sib_ref, bits_own, bits_sib,
    qg_out, kv_same, kv_pair, bits_out,
):
    row, chip, core, quarter = my_place()
    qg_out[quarter] = qg_own[...]
    qg_out[quarter ^ 1] = sib_ref[4 * krows :]
    qg_out[quarter ^ 2] = qg_pair0[...]
    qg_out[quarter ^ 3] = qg_pair1[...]
    for side, ref in enumerate((kv_same, kv_pair)):
        span = slice(side * 2 * krows, (side + 1) * 2 * krows)
        ref[core] = kv_own[span]
        ref[1 - core] = sib_ref[span]
    bits_out[core] = bits_own[...]
    bits_out[1 - core] = bits_sib[...]


def pair_kernel(sizes, *refs):
    head_dim, tile, capacity, chips, row_count = sizes
    qg_refs, refs = refs[:chips], refs[chips:]
    kv_refs, refs = refs[:row_count], refs[row_count:]
    bits_refs, refs = refs[:2], refs[2:]
    lse_refs, refs = refs[:2], refs[2:]
    dq_refs, refs = refs[:chips], refs[chips:]
    dkv_refs, refs = refs[:row_count], refs[row_count:]
    (q2_scr, g2_scr, q2t_scr, g2t_scr, k_scr, v_scr, k2t_scr, lse_scr, delta_scr,
     dqt_scr, dk_scr, dv_scr, dq_scr, info, sems) = refs
    rows = (qg_refs[0].shape[1] - PAD) // 2
    krows = kv_refs[0].shape[1] // 2
    query_tiles = q2_scr.shape[1]
    key_tiles = k_scr.shape[1]
    scaling = float(head_dim) ** -0.5
    row, chip, core, quarter = my_place()
    side = row % 2

    copies = [
        pltpu.make_async_copy(
            bits_refs[i // 2].at[i % 2, capacity // 2], info.at[i], sems.at[i]
        )
        for i in range(QUARTERS)
    ]
    for copy in copies:
        copy.start()

    for step, ref in enumerate(lse_refs):
        every = ref[0] * LOG2E
        own = every[:2]
        for index in range(1, QUARTERS):
            own = jnp.where(quarter == index, every[2 * index : 2 * index + 2], own)
        for u in range(query_tiles):
            lse_scr[side ^ step, u] = own[:, u * tile : (u + 1) * tile]
    low = lax.broadcasted_iota(I32, (rows, LANES), 1) < head_dim
    none = jnp.zeros((rows, LANES), BF16)
    for step in range(chips):
        for index in range(QUARTERS):
            source = (chip ^ step) * 2 + index % 2
            start = source * rows
            u = start // tile
            inner = pl.multiple_of(start % tile, rows)
            block = index // 2
            for scr, part in ((q2_scr, 0), (g2_scr, 1)):
                piece = qg_refs[step][index, part * rows : (part + 1) * rows]
                scr[block, u, 0, pl.ds(inner, rows)] = jnp.where(low, piece, none)
                scr[block, u, 1, pl.ds(inner, rows)] = jnp.where(low, none, piece)
            delta = qg_refs[step][index, 2 * rows :, :rows].astype(F32)
            if rows == tile:
                delta_scr[block, u] = delta
            else:
                for part in range(tile // rows):
                    @pl.when(source % (tile // rows) == part)
                    def _(part=part, delta=delta, u=u, block=block):
                        delta_scr[block, u, :, part * rows : (part + 1) * rows] = delta
    for step in range(row_count):
        start = (row ^ step) * krows
        inner = pl.multiple_of(start % tile, krows)
        for block in range(2):
            k_scr[block, start // tile, pl.ds(inner, krows)] = kv_refs[step][block, :krows]
            v_scr[block, start // tile, pl.ds(inner, krows)] = kv_refs[step][block, krows:]
    low_row = lax.broadcasted_iota(I32, (LANES, tile), 0) < head_dim
    none_t = jnp.zeros((LANES, tile), BF16)
    for block in range(2):
        for w in range(key_tiles):
            flipped = k_scr[block, w].T
            k2t_scr[block, w] = jnp.concatenate(
                [jnp.where(low_row, flipped, none_t), jnp.where(low_row, none_t, flipped)], axis=1
            )
    for block in range(2):
        for u in range(query_tiles):
            for part in range(2):
                lanes = slice(part * tile, (part + 1) * tile)
                q2t_scr[block, u, :, lanes] = q2_scr[block, u, part].T
                g2t_scr[block, u, :, lanes] = g2_scr[block, u, part].T
    dqt_scr[...] = jnp.zeros_like(dqt_scr)
    dk_scr[...] = jnp.zeros_like(dk_scr)
    dv_scr[...] = jnp.zeros_like(dv_scr)
    place_in = lax.broadcasted_iota(I32, (2, 4, 16, tile), 2)
    upper = lax.broadcasted_iota(I32, (2, 4, 16, tile), 0)
    bit = lax.shift_left(I32(1), place_in + 16 * upper).reshape(tile, tile)
    for copy in copies:
        copy.wait()

    for step in range(QUARTERS):
        qb = side ^ (step // 2)
        kb = step % 2
        live = info[step, 1, 0]

        def two_tiles(index, _, step=step, qb=qb, kb=kb, live=live):
            both = bits_refs[step // 2][kb, index]
            second = jnp.where(index * 2 + 1 < live, I32(-1), I32(0))
            work = []
            for part in range(2):
                slot = info[step, 0, index * 2 + part]
                u = slot // key_tiles
                w = slot % key_tiles
                words = both[part * 4 : part * 4 + 4]
                if part:
                    words = words & second
                words = jnp.broadcast_to(words[:, None, :], (4, 16, tile)).reshape(64, tile)
                edge = (jnp.concatenate([words, words], axis=0) & bit) != 0
                q2 = q2_scr[qb, u].reshape(2 * tile, LANES)
                g2 = g2_scr[qb, u].reshape(2 * tile, LANES)
                scores = lax.dot_general(
                    k_scr[kb, w], q2t_scr[qb, u], NN, preferred_element_type=F32
                )
                grad_prob = lax.dot_general(
                    v_scr[kb, w], g2t_scr[qb, u], NN, preferred_element_type=F32
                )
                work.append((u, w, edge, q2, g2, scores, grad_prob))
            done = []
            for u, w, edge, q2, g2, scores, grad_prob in work:
                lse_tile = lse_scr[qb, u]
                delta_tile = delta_scr[qb, u]
                probs, grads = [], []
                for h in range(2):
                    s = scores[:, h * tile : (h + 1) * tile]
                    gp = grad_prob[:, h * tile : (h + 1) * tile]
                    p = jnp.exp2(s * (scaling * LOG2E) - lse_tile[h : h + 1])
                    p = jnp.where(edge, p, 0.0)
                    ds = p * (gp - delta_tile[h : h + 1])
                    probs.append(p.astype(BF16))
                    grads.append(ds.astype(BF16))
                done.append((
                    lax.dot_general(
                        jnp.concatenate(probs, axis=1), g2, NN, preferred_element_type=F32
                    ),
                    lax.dot_general(
                        jnp.concatenate(grads, axis=1), q2, NN, preferred_element_type=F32
                    ),
                    lax.dot_general(
                        k2t_scr[kb, w], jnp.concatenate(grads, axis=0), NN,
                        preferred_element_type=F32,
                    ),
                ))
            for (u, w, *_), (dv, dk, dqt) in zip(work, done):
                dv_scr[kb, w] += dv
                dk_scr[kb, w] += dk
                dqt_scr[qb, u] += dqt
            return 0

        lax.fori_loop(0, (live + 1) // 2, two_tiles, 0)

    for step in range(row_count):
        start = (row ^ step) * krows
        inner = pl.multiple_of(start % tile, krows)
        for block in range(2):
            dk = dk_scr[block, start // tile, pl.ds(inner, krows)] * scaling
            dv = dv_scr[block, start // tile, pl.ds(inner, krows)]
            dkv_refs[step][block, :krows] = dk.astype(BF16)
            dkv_refs[step][block, krows:] = dv.astype(BF16)
    for block in range(2):
        for u in range(query_tiles):
            dq_scr[block, u * tile : (u + 1) * tile] = (dqt_scr[block, u] * scaling).astype(BF16).T
    for step in range(chips):
        for index in range(QUARTERS):
            start = pl.multiple_of(((chip ^ step) * 2 + index % 2) * rows, rows)
            dq_refs[step][index] = dq_scr[index // 2, pl.ds(start, rows)]


def query_sum_kernel(chips, *refs):
    parts, (same_ref, pair_ref) = refs[:chips], refs[chips:]
    side = my_place()[0] % 2
    for step, ref in enumerate((same_ref, pair_ref)):
        for core in range(2):
            index = (side ^ step) * 2 + core
            total = parts[0][index].astype(F32)
            for part in parts[1:]:
                total += part[index].astype(F32)
            ref[core] = total.astype(BF16)


def key_sum_kernel(row_count, *refs):
    (dq_same, dq_pair), dkv_refs, (own_ref, sib_ref) = refs[:2], refs[2:-2], refs[-2:]
    krows2 = dkv_refs[0].shape[1]
    core = my_place()[2]
    for ref, block in ((own_ref, core), (sib_ref, 1 - core)):
        for side, dq in enumerate((dq_same, dq_pair)):
            total = dkv_refs[side][block].astype(F32)
            for other in range(side + 2, row_count, 2):
                total += dkv_refs[other][block].astype(F32)
            ref[side, :krows2] = total.astype(BF16)
            ref[side, krows2:] = dq[block]


def finish_kernel(krows, own_ref, sib_ref, dq_out, dk_out, dv_out):
    quarter = my_place()[3]
    for core, ref in enumerate((own_ref, sib_ref)):
        for side in range(2):
            lanes = lanes_of(quarter ^ (2 * side + core))
            dk_out[0, :, lanes] = ref[side, :krows]
            dv_out[0, :, lanes] = ref[side, krows : 2 * krows]
            dq_out[0, :, lanes] = ref[side, 2 * krows :]


def send(block, axes, count, step):
    return lax.ppermute(block, axes, [(place, place ^ step) for place in range(count)])


def body(sizes, queries, keys, values, outputs, grad_out, lse, tile_slot, tile_live, tile_bits):
    row_count, chips, cores = sizes
    heads = lse.shape[1]
    width = queries.shape[2]
    head_dim = width // heads
    tile = tile_bits.shape[4]
    capacity = tile_slot.shape[2]
    rows = queries.shape[1]
    krows = keys.shape[1]
    query_tiles = lse.shape[2] // tile
    key_tiles = row_count * krows // tile
    line = ("row", "core")
    places = row_count * cores

    def shape(*dims, dtype=BF16):
        return jax.ShapeDtypeStruct(dims, dtype)

    qg_shape = shape(2 * rows + PAD, LANES)
    kv_shape = shape(2, 2 * krows, LANES)
    qg_own, qg_pair0, qg_pair1, kv_own, to_sibling, bits_own = pl.pallas_call(
        functools.partial(pack_kernel, heads),
        out_shape=(
            qg_shape, qg_shape, qg_shape, shape(4 * krows, LANES),
            shape(4 * krows + 2 * rows + PAD, LANES),
            shape(capacity // 2 + 1, 8, LANES, dtype=I32),
        ),
        in_specs=[HBM] * 6 + [VMEM] * 2,
        out_specs=(VMEM,) * 6,
        scratch_shapes=[
            pltpu.VMEM(queries.shape, BF16),
            pltpu.VMEM(queries.shape, BF16),
            pltpu.VMEM(queries.shape, BF16),
            pltpu.VMEM(keys.shape, BF16),
            pltpu.VMEM(keys.shape, BF16),
            pltpu.VMEM(tile_bits.shape, I32),
            pltpu.VMEM((QUARTERS, PAD, rows), BF16),
            pltpu.SemaphoreType.DMA((6,)),
        ],
        compiler_params=SMALL,
        name="pack",
    )(queries, grad_out, outputs, keys, values, tile_bits, tile_slot, tile_live)

    qg_pair0 = send(qg_pair0, line, places, 2)
    qg_pair1 = send(qg_pair1, line, places, 3)
    from_sibling = send(to_sibling, "core", cores, 1)
    bits_sibling = send(bits_own, "core", cores, 1)
    lse_other = send(lse, "row", row_count, 1)
    qg, kv_same, kv_pair, bits = pl.pallas_call(
        functools.partial(join_kernel, krows),
        out_shape=(
            shape(QUARTERS, 2 * rows + PAD, LANES), kv_shape, kv_shape,
            shape(2, capacity // 2 + 1, 8, LANES, dtype=I32),
        ),
        in_specs=[VMEM] * 7,
        out_specs=(VMEM,) * 4,
        compiler_params=SMALL,
        name="join",
    )(qg_own, qg_pair0, qg_pair1, kv_own, from_sibling, bits_own, bits_sibling)
    kv_out = (kv_same, kv_pair)
    kv = [kv_same] + [
        send(kv_out[step % 2], "row", row_count, step) for step in range(1, row_count)
    ]
    bits_other = send(bits, "row", row_count, 1)
    qg = [qg] + [send(qg, "chip", chips, step) for step in range(1, chips)]

    parts = pl.pallas_call(
        functools.partial(pair_kernel, (head_dim, tile, capacity, chips, row_count)),
        out_shape=(shape(QUARTERS, rows, LANES),) * chips + (kv_shape,) * row_count,
        in_specs=[VMEM] * (chips + row_count + 4),
        out_specs=(VMEM,) * (chips + row_count),
        scratch_shapes=[
            pltpu.VMEM((2, query_tiles, 2, tile, LANES), BF16),
            pltpu.VMEM((2, query_tiles, 2, tile, LANES), BF16),
            pltpu.VMEM((2, query_tiles, LANES, 2 * tile), BF16),
            pltpu.VMEM((2, query_tiles, LANES, 2 * tile), BF16),
            pltpu.VMEM((2, key_tiles, tile, LANES), BF16),
            pltpu.VMEM((2, key_tiles, tile, LANES), BF16),
            pltpu.VMEM((2, key_tiles, LANES, 2 * tile), BF16),
            pltpu.VMEM((2, query_tiles, 2, tile), F32),
            pltpu.VMEM((2, query_tiles, PAD, tile), F32),
            pltpu.VMEM((2, query_tiles, LANES, tile), F32),
            pltpu.VMEM((2, key_tiles, tile, LANES), F32),
            pltpu.VMEM((2, key_tiles, tile, LANES), F32),
            pltpu.VMEM((2, query_tiles * tile, LANES), BF16),
            pltpu.SMEM((QUARTERS, 8, LANES), I32),
            pltpu.SemaphoreType.DMA((QUARTERS,)),
        ],
        compiler_params=MEDIUM,
        name="pair",
    )(*qg, *kv, bits, bits_other, lse, lse_other)

    dq, dkv = parts[:chips], parts[chips:]
    dq = [dq[0]] + [send(dq[step], "chip", chips, step) for step in range(1, chips)]
    dkv = [dkv[0]] + [send(dkv[step], "row", row_count, step) for step in range(1, row_count)]
    dq_same, dq_pair = pl.pallas_call(
        functools.partial(query_sum_kernel, chips),
        out_shape=(shape(2, rows, LANES),) * 2,
        in_specs=[VMEM] * chips,
        out_specs=(VMEM,) * 2,
        compiler_params=SMALL,
        name="query_sum",
    )(*dq)
    dq_pair = send(dq_pair, "row", row_count, 1)
    own, to_sibling = pl.pallas_call(
        functools.partial(key_sum_kernel, row_count),
        out_shape=(shape(2, 2 * krows + rows, LANES),) * 2,
        in_specs=[VMEM] * (2 + row_count),
        out_specs=(VMEM,) * 2,
        compiler_params=SMALL,
        name="key_sum",
    )(dq_same, dq_pair, *dkv)
    from_sibling = send(to_sibling, "core", cores, 1)
    return pl.pallas_call(
        functools.partial(finish_kernel, krows),
        out_shape=(shape(1, rows, width), shape(1, krows, width), shape(1, krows, width)),
        in_specs=[VMEM] * 2,
        out_specs=(VMEM,) * 3,
        compiler_params=SMALL,
        name="finish",
    )(own, from_sibling)


def solution(mesh):
    row_count, columns = mesh.devices.shape
    cores = 2
    chips = columns // cores
    fine = Mesh(mesh.devices.reshape(row_count, chips, cores), ("row", "chip", "core"))
    col = ("chip", "core")
    in_specs = (
        P("row", col, None),
        P(col, "row", None),
        P(col, "row", None),
        P("row", col, None),
        P("row", col, None),
        P("row", None, None),
        P("row", col, None),
        P("row", col),
        P("row", col, None, None, None),
    )
    out_specs = (P("row", col, None), P(col, "row", None), P(col, "row", None))
    return jax.shard_map(
        functools.partial(body, (row_count, chips, cores)),
        mesh=fine, in_specs=in_specs, out_specs=out_specs, check_vma=False,
    )
```

```python
import functools

import jax
import jax.numpy as jnp
from jax import lax
from jax.experimental import pallas as pl
from jax.experimental.pallas import tpu as pltpu
from jax.sharding import Mesh
from jax.sharding import PartitionSpec as P


F32 = jnp.float32
BF16 = jnp.bfloat16
I32 = jnp.int32
LANES = 128
PAD = 16
QUARTERS = 4
LOG2E = 1.4426950408889634
NT = (((1,), (1,)), ((), ()))
NN = (((1,), (0,)), ((), ()))
MEDIUM = pltpu.CompilerParams(vmem_limit_bytes=28 * 1024 * 1024)
PACK = pltpu.CompilerParams(vmem_limit_bytes=int(53.4 * 1024 * 1024))
SMALL = pltpu.CompilerParams(vmem_limit_bytes=12 * 1024 * 1024)
def early(gigaflops):
    return pl.CostEstimate(flops=gigaflops * 10**9, bytes_accessed=0, transcendentals=0)


VMEM = pl.BlockSpec(memory_space=pltpu.VMEM)
HBM = pl.BlockSpec(memory_space=pltpu.HBM)


def lanes_of(quarter):
    return pl.ds(pl.multiple_of(quarter * LANES, LANES), LANES)


def my_place():
    row, chip, core = (lax.axis_index(name) for name in ("row", "chip", "core"))
    return row, chip, core, row % 2 * 2 + core


def pack_kernel(
    heads, q_hbm, g_hbm, o_hbm, k_hbm, v_hbm, bits_hbm, slot_ref, live_ref,
    qg_own, qg_pair0, qg_pair1, kv_own, sib_ref, packed_ref,
    q_ref, g_ref, o_ref, k_ref, v_ref, bits_ref, delta_ref, sems,
):
    arrays = (
        (q_hbm, q_ref), (g_hbm, g_ref), (o_hbm, o_ref),
        (k_hbm, k_ref), (v_hbm, v_ref), (bits_hbm, bits_ref),
    )
    copies = [pltpu.make_async_copy(a, b, sems.at[i]) for i, (a, b) in enumerate(arrays)]
    for copy in copies:
        copy.start()
    rows, width = q_ref.shape[1:]
    krows = k_ref.shape[1]
    head_dim = width // heads
    local = heads // QUARTERS
    capacity = bits_ref.shape[2]
    quarter = my_place()[3]
    feature = lax.broadcasted_iota(I32, (QUARTERS * PAD, width), 1)
    line = lax.broadcasted_iota(I32, (QUARTERS * PAD, width), 0)
    wanted = jnp.where(line % PAD < local, line // PAD * local + line % PAD, -1)
    pick = (feature // head_dim == wanted).astype(F32)
    packed_ref[capacity // 2] = jnp.zeros((8, LANES), I32)
    packed_ref[capacity // 2, 0:1, 0:capacity] = slot_ref[0]
    packed_ref[capacity // 2, 1:2, 0:1] = live_ref[...]
    for copy in copies:
        copy.wait()
    product = g_ref[0].astype(F32) * o_ref[0].astype(F32)
    delta = lax.dot_general(
        pick, product, NT, precision=lax.Precision.HIGHEST, preferred_element_type=F32
    ).astype(BF16)
    for index in range(QUARTERS):
        delta_ref[index] = delta[index * PAD : (index + 1) * PAD]
    base = 4 * krows
    for step, (ref, start) in enumerate(
        ((qg_own, 0), (sib_ref, base), (qg_pair0, 0), (qg_pair1, 0))
    ):
        lanes = lanes_of(quarter ^ step)
        ref[start : start + rows] = q_ref[0, :, lanes]
        ref[start + rows : start + 2 * rows] = g_ref[0, :, lanes]
        if rows < LANES:
            ref[start + 2 * rows : start + 2 * rows + PAD] = jnp.zeros((PAD, LANES), BF16)
        ref[start + 2 * rows : start + 2 * rows + PAD, :rows] = delta_ref[quarter ^ step]
    for side in range(2):
        for ref, step in ((kv_own, 2 * side), (sib_ref, 2 * side + 1)):
            lanes = lanes_of(quarter ^ step)
            start = side * 2 * krows
            ref[start : start + krows] = k_ref[0, :, lanes]
            ref[start + krows : start + 2 * krows] = v_ref[0, :, lanes]
    for entry in range(capacity):
        words = bits_ref[0, 0, entry]
        span = slice(entry % 2 * 4, entry % 2 * 4 + 4)
        packed_ref[entry // 2, span] = words[:4] | lax.shift_left(words[4:], I32(16))


def key_join_kernel(krows, kv_own, sib_ref, kv_same, kv_pair):
    core = my_place()[2]
    for side, ref in enumerate((kv_same, kv_pair)):
        span = slice(side * 2 * krows, (side + 1) * 2 * krows)
        ref[core] = kv_own[span]
        ref[1 - core] = sib_ref[span]


def query_join_kernel(
    krows, tile, qg_own, sib_ref, qg_pair0, qg_pair1, bits_own, bits_pair, lse_own, lse_pair,
    qg_out, bits_out, lse_out,
):
    row, chip, core, quarter = my_place()
    side = row % 2
    qg_out[quarter] = qg_own[...]
    qg_out[quarter ^ 1] = sib_ref[4 * krows :]
    qg_out[quarter ^ 2] = qg_pair0[...]
    qg_out[quarter ^ 3] = qg_pair1[...]
    bits_out[side] = bits_own[...]
    bits_out[1 - side] = bits_pair[...]
    for step, ref in enumerate((lse_own, lse_pair)):
        every = ref[0] * LOG2E
        own = every[:2]
        for index in range(1, QUARTERS):
            own = jnp.where(quarter == index, every[2 * index : 2 * index + 2], own)
        for u in range(lse_out.shape[1]):
            lse_out[side ^ step, u] = own[:, u * tile : (u + 1) * tile]


def key_place_kernel(head_dim, tile, *refs):
    kv_refs, (k_out, v_out, k2t_out) = refs[:-3], refs[-3:]
    krows = kv_refs[0].shape[1] // 2
    row = my_place()[0]
    for step, ref in enumerate(kv_refs):
        start = (row ^ step) * krows
        inner = pl.multiple_of(start % tile, krows)
        for block in range(2):
            k_out[block, start // tile, pl.ds(inner, krows)] = ref[block, :krows]
            v_out[block, start // tile, pl.ds(inner, krows)] = ref[block, krows:]
    low_row = lax.broadcasted_iota(I32, (LANES, tile), 0) < head_dim
    none_t = jnp.zeros((LANES, tile), BF16)
    for block in range(2):
        for w in range(k_out.shape[1]):
            flipped = k_out[block, w].T
            k2t_out[block, w] = jnp.concatenate(
                [jnp.where(low_row, flipped, none_t), jnp.where(low_row, none_t, flipped)], axis=1
            )


def pair_kernel(sizes, *refs):
    head_dim, tile, capacity, chips, row_count = sizes
    qg_refs, refs = refs[:chips], refs[chips:]
    (k_scr, v_scr, k2t_scr), refs = refs[:3], refs[3:]
    bits_refs, lse_ref, refs = refs[:2], refs[2], refs[3:]
    dqt_ref, dkv_refs, refs = refs[0], refs[1 : 1 + row_count], refs[1 + row_count :]
    q2_scr, g2_scr, delta_scr, dqt_scr, dk_scr, dv_scr, info, sems = refs
    rows = (qg_refs[0].shape[1] - PAD) // 2
    krows = dkv_refs[0].shape[1] // 2
    query_tiles = q2_scr.shape[1]
    key_tiles = k_scr.shape[1]
    scaling = float(head_dim) ** -0.5
    row, chip, core, quarter = my_place()
    side = row % 2

    copies = [
        pltpu.make_async_copy(
            bits_refs[i % 2].at[i // 2, capacity // 2], info.at[i], sems.at[i]
        )
        for i in range(QUARTERS)
    ]
    for copy in copies:
        copy.start()

    low = lax.broadcasted_iota(I32, (rows, LANES), 1) < head_dim
    none = jnp.zeros((rows, LANES), BF16)
    for step in range(chips):
        for index in range(QUARTERS):
            source = (chip ^ step) * 2 + index % 2
            start = source * rows
            u = start // tile
            inner = pl.multiple_of(start % tile, rows)
            block = index // 2
            for scr, part in ((q2_scr, 0), (g2_scr, 1)):
                piece = qg_refs[step][index, part * rows : (part + 1) * rows]
                scr[block, u, 0, pl.ds(inner, rows)] = jnp.where(low, piece, none)
                scr[block, u, 1, pl.ds(inner, rows)] = jnp.where(low, none, piece)
            delta = qg_refs[step][index, 2 * rows :, :rows].astype(F32)
            if rows == tile:
                delta_scr[block, u] = delta
            else:
                for part in range(tile // rows):
                    @pl.when(source % (tile // rows) == part)
                    def _(part=part, delta=delta, u=u, block=block):
                        delta_scr[block, u, :, part * rows : (part + 1) * rows] = delta
    dqt_scr[...] = jnp.zeros_like(dqt_scr)
    dk_scr[...] = jnp.zeros_like(dk_scr)
    dv_scr[...] = jnp.zeros_like(dv_scr)
    place_in = lax.broadcasted_iota(I32, (2, 4, 16, tile), 2)
    upper = lax.broadcasted_iota(I32, (2, 4, 16, tile), 0)
    bit = lax.shift_left(I32(1), place_in + 16 * upper).reshape(tile, tile)
    for copy in copies:
        copy.wait()

    for step in range(QUARTERS):
        qb = step // 2
        kb = core ^ (step % 2)
        live = info[step, 1, 0]

        def two_tiles(index, _, step=step, qb=qb, kb=kb, live=live):
            both = bits_refs[step % 2][qb, index]
            second = jnp.where(index * 2 + 1 < live, I32(-1), I32(0))
            work = []
            for part in range(2):
                slot = info[step, 0, index * 2 + part]
                u = slot // key_tiles
                w = slot % key_tiles
                words = both[part * 4 : part * 4 + 4]
                if part:
                    words = words & second
                words = jnp.broadcast_to(words[:, None, :], (4, 16, tile)).reshape(64, tile)
                edge = (jnp.concatenate([words, words], axis=0) & bit) != 0
                q2 = q2_scr[qb, u].reshape(2 * tile, LANES)
                g2 = g2_scr[qb, u].reshape(2 * tile, LANES)
                scores = lax.dot_general(k_scr[kb, w], q2, NT, preferred_element_type=F32)
                grad_prob = lax.dot_general(v_scr[kb, w], g2, NT, preferred_element_type=F32)
                work.append((u, w, edge, q2, g2, scores, grad_prob))
            done = []
            for u, w, edge, q2, g2, scores, grad_prob in work:
                lse_tile = lse_ref[qb, u]
                delta_tile = delta_scr[qb, u]
                probs, grads = [], []
                for h in range(2):
                    s = scores[:, h * tile : (h + 1) * tile]
                    gp = grad_prob[:, h * tile : (h + 1) * tile]
                    p = jnp.exp2(s * (scaling * LOG2E) - lse_tile[h : h + 1])
                    p = jnp.where(edge, p, 0.0)
                    ds = p * (gp - delta_tile[h : h + 1])
                    probs.append(p.astype(BF16))
                    grads.append(ds.astype(BF16))
                done.append((
                    lax.dot_general(
                        jnp.concatenate(probs, axis=1), g2, NN, preferred_element_type=F32
                    ),
                    lax.dot_general(
                        jnp.concatenate(grads, axis=1), q2, NN, preferred_element_type=F32
                    ),
                    lax.dot_general(
                        k2t_scr[kb, w], jnp.concatenate(grads, axis=0), NN,
                        preferred_element_type=F32,
                    ),
                ))
            for (u, w, *_), (dv, dk, dqt) in zip(work, done):
                dv_scr[kb, w] += dv
                dk_scr[kb, w] += dk
                dqt_scr[qb, u] += dqt
            return 0

        lax.fori_loop(0, (live + 1) // 2, two_tiles, 0)

    for step in range(row_count):
        start = (row ^ step) * krows
        inner = pl.multiple_of(start % tile, krows)
        for block in range(2):
            dk = dk_scr[block, start // tile, pl.ds(inner, krows)] * scaling
            dv = dv_scr[block, start // tile, pl.ds(inner, krows)]
            dkv_refs[step][block, :krows] = dk.astype(BF16)
            dkv_refs[step][block, krows:] = dv.astype(BF16)
    dqt_ref[...] = (dqt_scr[...] * scaling).astype(BF16)


def turn_kernel(rows, dqt_ref, *refs):
    dq_refs, dq_scr = refs[:-1], refs[-1]
    tile = dqt_ref.shape[3]
    chip = my_place()[1]
    for block in range(2):
        for u in range(dqt_ref.shape[1]):
            dq_scr[block, u * tile : (u + 1) * tile] = dqt_ref[block, u].T
    for step, ref in enumerate(dq_refs):
        for index in range(QUARTERS):
            start = pl.multiple_of(((chip ^ step) * 2 + index % 2) * rows, rows)
            ref[index] = dq_scr[index // 2, pl.ds(start, rows)]


def query_sum_kernel(chips, *refs):
    parts, (same_ref, pair_ref) = refs[:chips], refs[chips:]
    side = my_place()[0] % 2
    for step, ref in enumerate((same_ref, pair_ref)):
        for core in range(2):
            index = (side ^ step) * 2 + core
            total = parts[0][index].astype(F32)
            for part in parts[1:]:
                total += part[index].astype(F32)
            ref[core] = total.astype(BF16)


def key_sum_kernel(row_count, *refs):
    dkv_refs, (own_ref, sib_ref) = refs[:-2], refs[-2:]
    core = my_place()[2]
    for ref, block in ((own_ref, core), (sib_ref, 1 - core)):
        for side in range(2):
            total = dkv_refs[side][block].astype(F32)
            for other in range(side + 2, row_count, 2):
                total += dkv_refs[other][block].astype(F32)
            ref[side] = total.astype(BF16)


def bundle_kernel(dkv_ref, dq_same, dq_pair, out):
    krows2 = dkv_ref.shape[1]
    sibling = 1 - my_place()[2]
    out[:, :krows2] = dkv_ref[...]
    for side, dq in enumerate((dq_same, dq_pair)):
        out[side, krows2:] = dq[sibling]


def finish_kernel(krows, dkv_own, dq_same, dq_pair, sib_ref, dq_out, dk_out, dv_out):
    row, chip, core, quarter = my_place()
    for side, dq in enumerate((dq_same, dq_pair)):
        for step, ref in enumerate((dkv_own, sib_ref)):
            lanes = lanes_of(quarter ^ (2 * side + step))
            dk_out[0, :, lanes] = ref[side, :krows]
            dv_out[0, :, lanes] = ref[side, krows : 2 * krows]
            dq_out[0, :, lanes] = ref[side, 2 * krows :] if step else dq[core]


def send(block, axes, count, step):
    return lax.ppermute(block, axes, [(place, place ^ step) for place in range(count)])


def body(sizes, queries, keys, values, outputs, grad_out, lse, tile_slot, tile_live, tile_bits):
    row_count, chips, cores = sizes
    heads = lse.shape[1]
    width = queries.shape[2]
    head_dim = width // heads
    tile = tile_bits.shape[4]
    capacity = tile_slot.shape[2]
    rows = queries.shape[1]
    krows = keys.shape[1]
    query_tiles = lse.shape[2] // tile
    key_tiles = row_count * krows // tile
    line = ("row", "core")
    places = row_count * cores

    def shape(*dims, dtype=BF16):
        return jax.ShapeDtypeStruct(dims, dtype)

    qg_shape = shape(2 * rows + PAD, LANES)
    kv_shape = shape(2, 2 * krows, LANES)
    qg_own, qg_pair0, qg_pair1, kv_own, to_sibling, bits_own = pl.pallas_call(
        functools.partial(pack_kernel, heads),
        out_shape=(
            qg_shape, qg_shape, qg_shape, shape(4 * krows, LANES),
            shape(4 * krows + 2 * rows + PAD, LANES),
            shape(capacity // 2 + 1, 8, LANES, dtype=I32),
        ),
        in_specs=[HBM] * 6 + [VMEM] * 2,
        out_specs=(VMEM,) * 6,
        scratch_shapes=[
            pltpu.VMEM(queries.shape, BF16),
            pltpu.VMEM(queries.shape, BF16),
            pltpu.VMEM(queries.shape, BF16),
            pltpu.VMEM(keys.shape, BF16),
            pltpu.VMEM(keys.shape, BF16),
            pltpu.VMEM(tile_bits.shape, I32),
            pltpu.VMEM((QUARTERS, PAD, rows), BF16),
            pltpu.SemaphoreType.DMA((6,)),
        ],
        compiler_params=PACK,
        name="pack",
    )(queries, grad_out, outputs, keys, values, tile_bits, tile_slot, tile_live)

    qg_pair0 = send(qg_pair0, line, places, 2)
    qg_pair1 = send(qg_pair1, line, places, 3)
    from_sibling = send(to_sibling, "core", cores, 1)
    bits_pair = send(bits_own, "row", row_count, 1)
    lse_pair = send(lse, "row", row_count, 1)
    kv_same, kv_pair = pl.pallas_call(
        functools.partial(key_join_kernel, krows),
        out_shape=(kv_shape, kv_shape),
        in_specs=[VMEM] * 2,
        out_specs=(VMEM,) * 2,
        compiler_params=SMALL,
        name="key_join",
    )(kv_own, from_sibling)
    kv_out = (kv_same, kv_pair)
    kv = [kv_same] + [
        send(kv_out[step % 2], "row", row_count, step) for step in range(1, row_count)
    ]
    qg, bits, lse2 = pl.pallas_call(
        functools.partial(query_join_kernel, krows, tile),
        out_shape=(
            shape(QUARTERS, 2 * rows + PAD, LANES),
            shape(2, capacity // 2 + 1, 8, LANES, dtype=I32),
            shape(2, query_tiles, 2, tile, dtype=F32),
        ),
        in_specs=[VMEM] * 8,
        out_specs=(VMEM,) * 3,
        compiler_params=SMALL,
        cost_estimate=early(20),
        name="query_join",
    )(qg_own, from_sibling, qg_pair0, qg_pair1, bits_own, bits_pair, lse, lse_pair)
    qg = [qg] + [send(qg, "chip", chips, step) for step in range(1, chips)]
    bits_sibling = send(bits, "core", cores, 1)

    placed = pl.pallas_call(
        functools.partial(key_place_kernel, head_dim, tile),
        out_shape=(
            shape(2, key_tiles, tile, LANES), shape(2, key_tiles, tile, LANES),
            shape(2, key_tiles, LANES, 2 * tile),
        ),
        in_specs=[VMEM] * row_count,
        out_specs=(VMEM,) * 3,
        compiler_params=SMALL,
        cost_estimate=early(20),
        name="key_place",
    )(*kv)
    parts = pl.pallas_call(
        functools.partial(pair_kernel, (head_dim, tile, capacity, chips, row_count)),
        out_shape=(shape(2, query_tiles, LANES, tile),) + (kv_shape,) * row_count,
        in_specs=[VMEM] * (chips + 6),
        out_specs=(VMEM,) * (1 + row_count),
        scratch_shapes=[
            pltpu.VMEM((2, query_tiles, 2, tile, LANES), BF16),
            pltpu.VMEM((2, query_tiles, 2, tile, LANES), BF16),
            pltpu.VMEM((2, query_tiles, PAD, tile), F32),
            pltpu.VMEM((2, query_tiles, LANES, tile), F32),
            pltpu.VMEM((2, key_tiles, tile, LANES), F32),
            pltpu.VMEM((2, key_tiles, tile, LANES), F32),
            pltpu.SMEM((QUARTERS, 8, LANES), I32),
            pltpu.SemaphoreType.DMA((QUARTERS,)),
        ],
        compiler_params=MEDIUM,
        name="pair",
    )(*qg, *placed, bits, bits_sibling, lse2)

    dkv = parts[1:]
    dq = pl.pallas_call(
        functools.partial(turn_kernel, rows),
        out_shape=(shape(QUARTERS, rows, LANES),) * chips,
        in_specs=[VMEM],
        out_specs=(VMEM,) * chips,
        scratch_shapes=[pltpu.VMEM((2, query_tiles * tile, LANES), BF16)],
        compiler_params=SMALL,
        name="turn",
    )(parts[0])
    dq = [dq[0]] + [send(dq[step], "chip", chips, step) for step in range(1, chips)]
    dkv = [dkv[0]] + [send(dkv[step], "row", row_count, step) for step in range(1, row_count)]
    dq_same, dq_pair = pl.pallas_call(
        functools.partial(query_sum_kernel, chips),
        out_shape=(shape(2, rows, LANES),) * 2,
        in_specs=[VMEM] * chips,
        out_specs=(VMEM,) * 2,
        compiler_params=SMALL,
        name="query_sum",
    )(*dq)
    dq_pair = send(dq_pair, "row", row_count, 1)
    dkv_own, dkv_sibling = pl.pallas_call(
        functools.partial(key_sum_kernel, row_count),
        out_shape=(kv_shape,) * 2,
        in_specs=[VMEM] * row_count,
        out_specs=(VMEM,) * 2,
        compiler_params=SMALL,
        cost_estimate=early(20),
        name="key_sum",
    )(*dkv)
    to_sibling = pl.pallas_call(
        bundle_kernel,
        out_shape=shape(2, 2 * krows + rows, LANES),
        in_specs=[VMEM] * 3,
        out_specs=VMEM,
        compiler_params=SMALL,
        name="bundle",
    )(dkv_sibling, dq_same, dq_pair)
    from_sibling = send(to_sibling, "core", cores, 1)
    return pl.pallas_call(
        functools.partial(finish_kernel, krows),
        out_shape=(shape(1, rows, width), shape(1, krows, width), shape(1, krows, width)),
        in_specs=[VMEM] * 4,
        out_specs=(VMEM,) * 3,
        compiler_params=SMALL,
        name="finish",
    )(dkv_own, dq_same, dq_pair, from_sibling)


def solution(mesh):
    row_count, columns = mesh.devices.shape
    cores = 2
    chips = columns // cores
    fine = Mesh(mesh.devices.reshape(row_count, chips, cores), ("row", "chip", "core"))
    col = ("chip", "core")
    in_specs = (
        P("row", col, None),
        P(col, "row", None),
        P(col, "row", None),
        P("row", col, None),
        P("row", col, None),
        P("row", None, None),
        P("row", col, None),
        P("row", col),
        P("row", col, None, None, None),
    )
    out_specs = (P("row", col, None), P(col, "row", None), P(col, "row", None))
    return jax.shard_map(
        functools.partial(body, (row_count, chips, cores)),
        mesh=fine, in_specs=in_specs, out_specs=out_specs, check_vma=False,
    )
```

```python
import functools

import jax
import jax.numpy as jnp
from jax import lax
from jax.experimental import pallas as pl
from jax.experimental.pallas import tpu as pltpu
from jax.sharding import Mesh
from jax.sharding import PartitionSpec as P


F32 = jnp.float32
BF16 = jnp.bfloat16
I32 = jnp.int32
LANES = 128
PAD = 16
QUARTERS = 4
LOG2E = 1.4426950408889634
LSE_UNIT = 2.0**21
NT = (((1,), (1,)), ((), ()))
NN = (((1,), (0,)), ((), ()))
MEDIUM = pltpu.CompilerParams(vmem_limit_bytes=28 * 1024 * 1024)
PACK = pltpu.CompilerParams(vmem_limit_bytes=int(53.5 * 1024 * 1024))
SMALL = pltpu.CompilerParams(vmem_limit_bytes=12 * 1024 * 1024)
def early(gigaflops):
    return pl.CostEstimate(flops=gigaflops * 10**9, bytes_accessed=0, transcendentals=0)


VMEM = pl.BlockSpec(memory_space=pltpu.VMEM)
HBM = pl.BlockSpec(memory_space=pltpu.HBM)


def lanes_of(quarter):
    return pl.ds(pl.multiple_of(quarter * LANES, LANES), LANES)


def my_place():
    row, chip, core = (lax.axis_index(name) for name in ("row", "chip", "core"))
    return row, chip, core, row % 2 * 2 + core


def pack_kernel(
    heads, q_hbm, g_hbm, o_hbm, k_hbm, v_hbm, bits_hbm, lse_hbm, slot_ref, live_ref,
    qg_own, pair0_ref, pair1_ref, kv_own, sib_ref, packed_ref, lse_own,
    q_ref, g_ref, o_ref, k_ref, v_ref, bits_ref, lse_ref, delta_ref, sems,
):
    arrays = (
        (q_hbm, q_ref), (g_hbm, g_ref), (o_hbm, o_ref), (k_hbm, k_ref),
        (v_hbm, v_ref), (bits_hbm, bits_ref), (lse_hbm, lse_ref),
    )
    copies = [pltpu.make_async_copy(a, b, sems.at[i]) for i, (a, b) in enumerate(arrays)]
    for copy in copies:
        copy.start()
    rows, width = q_ref.shape[1:]
    krows = k_ref.shape[1]
    head_dim = width // heads
    local = heads // QUARTERS
    capacity = bits_ref.shape[2]
    quarter = my_place()[3]
    feature = lax.broadcasted_iota(I32, (QUARTERS * PAD, width), 1)
    line = lax.broadcasted_iota(I32, (QUARTERS * PAD, width), 0)
    wanted = jnp.where(line % PAD < local, line // PAD * local + line % PAD, -1)
    pick = (feature // head_dim == wanted).astype(F32)
    packed_ref[capacity // 2] = jnp.zeros((8, LANES), I32)
    packed_ref[capacity // 2, 0:1, 0:capacity] = slot_ref[0]
    packed_ref[capacity // 2, 1:2, 0:1] = live_ref[...]
    for copy in copies:
        copy.wait()
    product = g_ref[0].astype(F32) * o_ref[0].astype(F32)
    delta = lax.dot_general(
        pick, product, NT, precision=lax.Precision.HIGHEST, preferred_element_type=F32
    ).astype(BF16)
    for index in range(QUARTERS):
        delta_ref[index] = delta[index * PAD : (index + 1) * PAD]
    for step, (ref, start) in enumerate(
        ((qg_own, 0), (sib_ref, 4 * krows), (pair0_ref, 2 * krows), (pair1_ref, 2 * krows))
    ):
        lanes = lanes_of(quarter ^ step)
        ref[start : start + rows] = q_ref[0, :, lanes]
        ref[start + rows : start + 2 * rows] = g_ref[0, :, lanes]
        if rows < LANES:
            ref[start + 2 * rows : start + 2 * rows + PAD] = jnp.zeros((PAD, LANES), BF16)
        ref[start + 2 * rows : start + 2 * rows + PAD, :rows] = delta_ref[quarter ^ step]
    for step, targets in enumerate((
        ((kv_own, 0),), ((sib_ref, 0),),
        ((kv_own, 2 * krows), (pair0_ref, 0)), ((sib_ref, 2 * krows), (pair1_ref, 0)),
    )):
        lanes = lanes_of(quarter ^ step)
        for ref, start in targets:
            ref[start : start + krows] = k_ref[0, :, lanes]
            ref[start + krows : start + 2 * krows] = v_ref[0, :, lanes]
    every = lse_ref[0]

    def lse_of(wanted_quarter):
        own = every[:local]
        for index in range(1, QUARTERS):
            own = jnp.where(
                wanted_quarter == index, every[local * index : local * (index + 1)], own
            )
        return own

    mine = lse_of(quarter) * LOG2E
    other = (lse_of(quarter ^ 2) * LSE_UNIT).astype(I32)
    for u in range(lse_own.shape[0]):
        lanes = slice(u * LANES, (u + 1) * LANES)
        lse_own[u] = mine[:, lanes]
        packed_ref[capacity // 2 + 1 + u // 4, u % 4 * 2 : u % 4 * 2 + 2] = other[:, lanes]
    for entry in range(capacity):
        words = bits_ref[0, 0, entry]
        span = slice(entry % 2 * 4, entry % 2 * 4 + 4)
        packed_ref[entry // 2, span] = words[:4] | lax.shift_left(words[4:], I32(16))


def key_join_kernel(krows, kv_own, sib_ref, kv_same, kv_pair):
    core = my_place()[2]
    for side, ref in enumerate((kv_same, kv_pair)):
        span = slice(side * 2 * krows, (side + 1) * 2 * krows)
        ref[core] = kv_own[span]
        ref[1 - core] = sib_ref[span]


def query_join_kernel(
    krows, slabs, qg_own, sib_ref, pair0_ref, pair1_ref, bits_own, bits_pair, lse_own,
    qg_out, bits_out, lse_out,
):
    row, chip, core, quarter = my_place()
    side = row % 2
    qg_out[quarter] = qg_own[...]
    qg_out[quarter ^ 1] = sib_ref[4 * krows :]
    qg_out[quarter ^ 2] = pair0_ref[2 * krows :]
    qg_out[quarter ^ 3] = pair1_ref[2 * krows :]
    bits_out[side] = bits_own[:slabs]
    bits_out[1 - side] = bits_pair[:slabs]
    lse_out[side] = lse_own[...]
    for u in range(lse_out.shape[1]):
        fixed = bits_pair[slabs + u // 4, u % 4 * 2 : u % 4 * 2 + 2]
        lse_out[1 - side, u] = fixed.astype(F32) * (LOG2E / LSE_UNIT)


def key_place_kernel(head_dim, tile, pair0_ref, pair1_ref, *refs):
    kv_refs, (k_out, v_out, k2t_out) = refs[:-3], refs[-3:]
    krows = kv_refs[0].shape[1] // 2
    row, chip, core, quarter = my_place()
    blocks = [(0, 0, kv_refs[0].at[0]), (0, 1, kv_refs[0].at[1])]
    blocks += [(1, core, pair0_ref), (1, 1 - core, pair1_ref)]
    for index, ref in enumerate(kv_refs[1:]):
        blocks += [(index + 2, 0, ref.at[0]), (index + 2, 1, ref.at[1])]
    for step, block, ref in blocks:
        start = (row ^ step) * krows
        inner = pl.multiple_of(start % tile, krows)
        k_out[block, start // tile, pl.ds(inner, krows)] = ref[:krows]
        v_out[block, start // tile, pl.ds(inner, krows)] = ref[krows : 2 * krows]
    low_row = lax.broadcasted_iota(I32, (LANES, tile), 0) < head_dim
    none_t = jnp.zeros((LANES, tile), BF16)
    for block in range(2):
        for w in range(k_out.shape[1]):
            flipped = k_out[block, w].T
            k2t_out[block, w] = jnp.concatenate(
                [jnp.where(low_row, flipped, none_t), jnp.where(low_row, none_t, flipped)], axis=1
            )


def pair_kernel(sizes, *refs):
    head_dim, tile, capacity, chips, row_count = sizes
    qg_refs, refs = refs[:chips], refs[chips:]
    (k_scr, v_scr, k2t_scr), refs = refs[:3], refs[3:]
    bits_refs, lse_ref, refs = refs[:2], refs[2], refs[3:]
    dqt_ref, dkv_refs, refs = refs[0], refs[1 : 1 + row_count], refs[1 + row_count :]
    q2_scr, g2_scr, delta_scr, dqt_scr, dk_scr, dv_scr, info, sems = refs
    rows = (qg_refs[0].shape[1] - PAD) // 2
    krows = dkv_refs[0].shape[1] // 2
    query_tiles = q2_scr.shape[1]
    key_tiles = k_scr.shape[1]
    scaling = float(head_dim) ** -0.5
    row, chip, core, quarter = my_place()
    side = row % 2

    copies = [
        pltpu.make_async_copy(
            bits_refs[i % 2].at[i // 2, capacity // 2], info.at[i], sems.at[i]
        )
        for i in range(QUARTERS)
    ]
    for copy in copies:
        copy.start()

    low = lax.broadcasted_iota(I32, (rows, LANES), 1) < head_dim
    none = jnp.zeros((rows, LANES), BF16)
    for step in range(chips):
        for index in range(QUARTERS):
            source = (chip ^ step) * 2 + index % 2
            start = source * rows
            u = start // tile
            inner = pl.multiple_of(start % tile, rows)
            block = index // 2
            for scr, part in ((q2_scr, 0), (g2_scr, 1)):
                piece = qg_refs[step][index, part * rows : (part + 1) * rows]
                scr[block, u, 0, pl.ds(inner, rows)] = jnp.where(low, piece, none)
                scr[block, u, 1, pl.ds(inner, rows)] = jnp.where(low, none, piece)
            delta = qg_refs[step][index, 2 * rows :, :rows].astype(F32)
            if rows == tile:
                delta_scr[block, u] = delta
            else:
                for part in range(tile // rows):
                    @pl.when(source % (tile // rows) == part)
                    def _(part=part, delta=delta, u=u, block=block):
                        delta_scr[block, u, :, part * rows : (part + 1) * rows] = delta
    dqt_scr[...] = jnp.zeros_like(dqt_scr)
    dk_scr[...] = jnp.zeros_like(dk_scr)
    dv_scr[...] = jnp.zeros_like(dv_scr)
    place_in = lax.broadcasted_iota(I32, (2, 4, 16, tile), 2)
    upper = lax.broadcasted_iota(I32, (2, 4, 16, tile), 0)
    bit = lax.shift_left(I32(1), place_in + 16 * upper).reshape(tile, tile)
    for copy in copies:
        copy.wait()

    for step in range(QUARTERS):
        qb = step // 2
        kb = core ^ (step % 2)
        live = info[step, 1, 0]

        def two_tiles(index, _, step=step, qb=qb, kb=kb, live=live):
            both = bits_refs[step % 2][qb, index]
            second = jnp.where(index * 2 + 1 < live, I32(-1), I32(0))
            work = []
            for part in range(2):
                slot = info[step, 0, index * 2 + part]
                u = slot // key_tiles
                w = slot % key_tiles
                words = both[part * 4 : part * 4 + 4]
                if part:
                    words = words & second
                words = jnp.broadcast_to(words[:, None, :], (4, 16, tile)).reshape(64, tile)
                edge = (jnp.concatenate([words, words], axis=0) & bit) != 0
                q2 = q2_scr[qb, u].reshape(2 * tile, LANES)
                g2 = g2_scr[qb, u].reshape(2 * tile, LANES)
                scores = lax.dot_general(k_scr[kb, w], q2, NT, preferred_element_type=F32)
                grad_prob = lax.dot_general(v_scr[kb, w], g2, NT, preferred_element_type=F32)
                work.append((u, w, edge, q2, g2, scores, grad_prob))
            done = []
            for u, w, edge, q2, g2, scores, grad_prob in work:
                lse_tile = lse_ref[qb, u]
                delta_tile = delta_scr[qb, u]
                probs, grads = [], []
                for h in range(2):
                    s = scores[:, h * tile : (h + 1) * tile]
                    gp = grad_prob[:, h * tile : (h + 1) * tile]
                    p = jnp.exp2(s * (scaling * LOG2E) - lse_tile[h : h + 1])
                    p = jnp.where(edge, p, 0.0)
                    ds = p * (gp - delta_tile[h : h + 1])
                    probs.append(p.astype(BF16))
                    grads.append(ds.astype(BF16))
                done.append((
                    lax.dot_general(
                        jnp.concatenate(probs, axis=1), g2, NN, preferred_element_type=F32
                    ),
                    lax.dot_general(
                        jnp.concatenate(grads, axis=1), q2, NN, preferred_element_type=F32
                    ),
                    lax.dot_general(
                        k2t_scr[kb, w], jnp.concatenate(grads, axis=0), NN,
                        preferred_element_type=F32,
                    ),
                ))
            for (u, w, *_), (dv, dk, dqt) in zip(work, done):
                dv_scr[kb, w] += dv
                dk_scr[kb, w] += dk
                dqt_scr[qb, u] += dqt
            return 0

        lax.fori_loop(0, (live + 1) // 2, two_tiles, 0)

    for step in range(row_count):
        start = (row ^ step) * krows
        inner = pl.multiple_of(start % tile, krows)
        for block in range(2):
            dk = dk_scr[block, start // tile, pl.ds(inner, krows)] * scaling
            dv = dv_scr[block, start // tile, pl.ds(inner, krows)]
            dkv_refs[step][block, :krows] = dk.astype(BF16)
            dkv_refs[step][block, krows:] = dv.astype(BF16)
    dqt_ref[...] = (dqt_scr[...] * scaling).astype(BF16)


def turn_kernel(rows, dqt_ref, *refs):
    dq_refs, dq_scr = refs[:-1], refs[-1]
    tile = dqt_ref.shape[3]
    chip = my_place()[1]
    for block in range(2):
        for u in range(dqt_ref.shape[1]):
            dq_scr[block, u * tile : (u + 1) * tile] = dqt_ref[block, u].T
    for step, ref in enumerate(dq_refs):
        for index in range(QUARTERS):
            start = pl.multiple_of(((chip ^ step) * 2 + index % 2) * rows, rows)
            ref[index] = dq_scr[index // 2, pl.ds(start, rows)]


def query_sum_kernel(chips, *refs):
    parts, outs = refs[:chips], refs[chips:]
    quarter = my_place()[3]
    for step, out in enumerate(outs):
        total = parts[0][quarter ^ step].astype(F32)
        for part in parts[1:]:
            total += part[quarter ^ step].astype(F32)
        out[...] = total.astype(BF16)


def key_sum_kernel(row_count, *refs):
    dkv_refs, (own_ref, sib_ref) = refs[:-2], refs[-2:]
    core = my_place()[2]
    for ref, block in ((own_ref, core), (sib_ref, 1 - core)):
        for side in range(2):
            total = dkv_refs[side][block].astype(F32)
            for other in range(side + 2, row_count, 2):
                total += dkv_refs[other][block].astype(F32)
            ref[side] = total.astype(BF16)


def finish_kernel(own_ref, sib_ref, *refs):
    dq_refs, (dq_out, dk_out, dv_out) = refs[:QUARTERS], refs[QUARTERS:]
    krows = dk_out.shape[1]
    quarter = my_place()[3]
    for step, dq in enumerate(dq_refs):
        lanes = lanes_of(quarter ^ step)
        dkv = (own_ref, sib_ref)[step % 2]
        dk_out[0, :, lanes] = dkv[step // 2, :krows]
        dv_out[0, :, lanes] = dkv[step // 2, krows:]
        dq_out[0, :, lanes] = dq[...]


def send(block, axes, count, step):
    return lax.ppermute(block, axes, [(place, place ^ step) for place in range(count)])


def body(sizes, queries, keys, values, outputs, grad_out, lse, tile_slot, tile_live, tile_bits):
    row_count, chips, cores = sizes
    heads = lse.shape[1]
    width = queries.shape[2]
    head_dim = width // heads
    tile = tile_bits.shape[4]
    capacity = tile_slot.shape[2]
    rows = queries.shape[1]
    krows = keys.shape[1]
    query_tiles = lse.shape[2] // tile
    key_tiles = row_count * krows // tile
    line = ("row", "core")
    places = row_count * cores

    def shape(*dims, dtype=BF16):
        return jax.ShapeDtypeStruct(dims, dtype)

    qg_shape = shape(2 * rows + PAD, LANES)
    kv_shape = shape(2, 2 * krows, LANES)
    slabs = capacity // 2 + 1
    pair_shape = shape(2 * krows + 2 * rows + PAD, LANES)
    qg_own, pair0, pair1, kv_own, to_sibling, bits_own, lse_own = pl.pallas_call(
        functools.partial(pack_kernel, heads),
        out_shape=(
            qg_shape, pair_shape, pair_shape, shape(4 * krows, LANES),
            shape(4 * krows + 2 * rows + PAD, LANES),
            shape(slabs + query_tiles // 4, 8, LANES, dtype=I32),
            shape(query_tiles, 2, tile, dtype=F32),
        ),
        in_specs=[HBM] * 7 + [VMEM] * 2,
        out_specs=(VMEM,) * 7,
        scratch_shapes=[
            pltpu.VMEM(queries.shape, BF16),
            pltpu.VMEM(queries.shape, BF16),
            pltpu.VMEM(queries.shape, BF16),
            pltpu.VMEM(keys.shape, BF16),
            pltpu.VMEM(keys.shape, BF16),
            pltpu.VMEM(tile_bits.shape, I32),
            pltpu.VMEM(lse.shape, F32),
            pltpu.VMEM((QUARTERS, PAD, rows), BF16),
            pltpu.SemaphoreType.DMA((7,)),
        ],
        compiler_params=PACK,
        name="pack",
    )(queries, grad_out, outputs, keys, values, tile_bits, lse, tile_slot, tile_live)

    pair0 = send(pair0, line, places, 2)
    pair1 = send(pair1, line, places, 3)
    from_sibling = send(to_sibling, "core", cores, 1)
    bits_pair = send(bits_own, "row", row_count, 1)
    kv_same, kv_pair = pl.pallas_call(
        functools.partial(key_join_kernel, krows),
        out_shape=(kv_shape, kv_shape),
        in_specs=[VMEM] * 2,
        out_specs=(VMEM,) * 2,
        compiler_params=SMALL,
        name="key_join",
    )(kv_own, from_sibling)
    kv_out = (kv_same, kv_pair)
    kv = [kv_same] + [
        send(kv_out[step % 2], "row", row_count, step) for step in range(2, row_count)
    ]
    qg, bits, lse2 = pl.pallas_call(
        functools.partial(query_join_kernel, krows, slabs),
        out_shape=(
            shape(QUARTERS, 2 * rows + PAD, LANES),
            shape(2, slabs, 8, LANES, dtype=I32),
            shape(2, query_tiles, 2, tile, dtype=F32),
        ),
        in_specs=[VMEM] * 7,
        out_specs=(VMEM,) * 3,
        compiler_params=SMALL,
        cost_estimate=early(20),
        name="query_join",
    )(qg_own, from_sibling, pair0, pair1, bits_own, bits_pair, lse_own)
    qg = [qg] + [send(qg, "chip", chips, step) for step in range(1, chips)]
    bits_sibling = send(bits, "core", cores, 1)

    placed = pl.pallas_call(
        functools.partial(key_place_kernel, head_dim, tile),
        out_shape=(
            shape(2, key_tiles, tile, LANES), shape(2, key_tiles, tile, LANES),
            shape(2, key_tiles, LANES, 2 * tile),
        ),
        in_specs=[VMEM] * (row_count + 1),
        out_specs=(VMEM,) * 3,
        compiler_params=SMALL,
        cost_estimate=early(20),
        name="key_place",
    )(pair0, pair1, *kv)
    parts = pl.pallas_call(
        functools.partial(pair_kernel, (head_dim, tile, capacity, chips, row_count)),
        out_shape=(shape(2, query_tiles, LANES, tile),) + (kv_shape,) * row_count,
        in_specs=[VMEM] * (chips + 6),
        out_specs=(VMEM,) * (1 + row_count),
        scratch_shapes=[
            pltpu.VMEM((2, query_tiles, 2, tile, LANES), BF16),
            pltpu.VMEM((2, query_tiles, 2, tile, LANES), BF16),
            pltpu.VMEM((2, query_tiles, PAD, tile), F32),
            pltpu.VMEM((2, query_tiles, LANES, tile), F32),
            pltpu.VMEM((2, key_tiles, tile, LANES), F32),
            pltpu.VMEM((2, key_tiles, tile, LANES), F32),
            pltpu.SMEM((QUARTERS, 8, LANES), I32),
            pltpu.SemaphoreType.DMA((QUARTERS,)),
        ],
        compiler_params=MEDIUM,
        name="pair",
    )(*qg, *placed, bits, bits_sibling, lse2)

    dkv = parts[1:]
    dq = pl.pallas_call(
        functools.partial(turn_kernel, rows),
        out_shape=(shape(QUARTERS, rows, LANES),) * chips,
        in_specs=[VMEM],
        out_specs=(VMEM,) * chips,
        scratch_shapes=[pltpu.VMEM((2, query_tiles * tile, LANES), BF16)],
        compiler_params=SMALL,
        name="turn",
    )(parts[0])
    dq = [dq[0]] + [send(dq[step], "chip", chips, step) for step in range(1, chips)]
    dkv = [dkv[0]] + [send(dkv[step], "row", row_count, step) for step in range(1, row_count)]
    dq = pl.pallas_call(
        functools.partial(query_sum_kernel, chips),
        out_shape=(shape(rows, LANES),) * QUARTERS,
        in_specs=[VMEM] * chips,
        out_specs=(VMEM,) * QUARTERS,
        compiler_params=SMALL,
        name="query_sum",
    )(*dq)
    dq = [dq[0]] + [send(dq[step], line, places, step) for step in range(1, QUARTERS)]
    dkv_own, dkv_sibling = pl.pallas_call(
        functools.partial(key_sum_kernel, row_count),
        out_shape=(kv_shape,) * 2,
        in_specs=[VMEM] * row_count,
        out_specs=(VMEM,) * 2,
        compiler_params=SMALL,
        name="key_sum",
    )(*dkv)
    dkv_sibling = send(dkv_sibling, "core", cores, 1)
    return pl.pallas_call(
        finish_kernel,
        out_shape=(shape(1, rows, width), shape(1, krows, width), shape(1, krows, width)),
        in_specs=[VMEM] * (2 + QUARTERS),
        out_specs=(VMEM,) * 3,
        compiler_params=SMALL,
        name="finish",
    )(dkv_own, dkv_sibling, *dq)


def solution(mesh):
    row_count, columns = mesh.devices.shape
    cores = 2
    chips = columns // cores
    fine = Mesh(mesh.devices.reshape(row_count, chips, cores), ("row", "chip", "core"))
    col = ("chip", "core")
    in_specs = (
        P("row", col, None),
        P(col, "row", None),
        P(col, "row", None),
        P("row", col, None),
        P("row", col, None),
        P("row", None, None),
        P("row", col, None),
        P("row", col),
        P("row", col, None, None, None),
    )
    out_specs = (P("row", col, None), P(col, "row", None), P(col, "row", None))
    return jax.shard_map(
        functools.partial(body, (row_count, chips, cores)),
        mesh=fine, in_specs=in_specs, out_specs=out_specs, check_vma=False,
    )
```

```python
import functools

import jax
import jax.numpy as jnp
from jax import lax
from jax.experimental import pallas as pl
from jax.experimental.pallas import tpu as pltpu
from jax.sharding import Mesh
from jax.sharding import PartitionSpec as P


F32 = jnp.float32
BF16 = jnp.bfloat16
I32 = jnp.int32
LANES = 128
PAD = 16
QUARTERS = 4
LOG2E = 1.4426950408889634
LSE_UNIT = 2.0**21
NT = (((1,), (1,)), ((), ()))
NN = (((1,), (0,)), ((), ()))
MEDIUM = pltpu.CompilerParams(vmem_limit_bytes=28 * 1024 * 1024)
PACK = pltpu.CompilerParams(vmem_limit_bytes=int(53.6 * 1024 * 1024))
SMALL = pltpu.CompilerParams(vmem_limit_bytes=12 * 1024 * 1024)
def early(gigaflops):
    return pl.CostEstimate(flops=gigaflops * 10**9, bytes_accessed=0, transcendentals=0)


VMEM = pl.BlockSpec(memory_space=pltpu.VMEM)
HBM = pl.BlockSpec(memory_space=pltpu.HBM)


def lanes_of(quarter):
    return pl.ds(pl.multiple_of(quarter * LANES, LANES), LANES)


def my_place():
    row, chip, core = (lax.axis_index(name) for name in ("row", "chip", "core"))
    return row, chip, core, row % 2 * 2 + core


def pack_kernel(
    heads, q_hbm, g_hbm, o_hbm, k_hbm, v_hbm, bits_hbm, lse_hbm, slot_ref, live_ref,
    qg_own, pair0_ref, pair1_ref, kv_own, sib_ref, packed_ref, lse_own,
    q_ref, g_ref, o_ref, k_ref, v_ref, bits_ref, lse_ref, delta_ref, sems,
):
    arrays = (
        (q_hbm, q_ref), (g_hbm, g_ref), (o_hbm, o_ref), (k_hbm, k_ref),
        (v_hbm, v_ref), (bits_hbm, bits_ref), (lse_hbm, lse_ref),
    )
    copies = [pltpu.make_async_copy(a, b, sems.at[i]) for i, (a, b) in enumerate(arrays)]
    for copy in copies:
        copy.start()
    rows, width = q_ref.shape[1:]
    krows = k_ref.shape[1]
    head_dim = width // heads
    local = heads // QUARTERS
    capacity = bits_ref.shape[2]
    quarter = my_place()[3]
    feature = lax.broadcasted_iota(I32, (QUARTERS * PAD, width), 1)
    line = lax.broadcasted_iota(I32, (QUARTERS * PAD, width), 0)
    wanted = jnp.where(line % PAD < local, line // PAD * local + line % PAD, -1)
    pick = (feature // head_dim == wanted).astype(F32)
    packed_ref[capacity // 2] = jnp.zeros((8, LANES), I32)
    packed_ref[capacity // 2, 0:1, 0:capacity] = slot_ref[0]
    packed_ref[capacity // 2, 1:2, 0:1] = live_ref[...]
    for copy in copies:
        copy.wait()
    product = g_ref[0].astype(F32) * o_ref[0].astype(F32)
    delta = lax.dot_general(
        pick, product, NT, precision=lax.Precision.HIGHEST, preferred_element_type=F32
    ).astype(BF16)
    for index in range(QUARTERS):
        delta_ref[index] = delta[index * PAD : (index + 1) * PAD]
    for step, (ref, start) in enumerate(
        ((qg_own, 0), (sib_ref, 4 * krows), (pair0_ref, 0), (pair1_ref, 0))
    ):
        lanes = lanes_of(quarter ^ step)
        ref[start : start + rows] = q_ref[0, :, lanes]
        ref[start + rows : start + 2 * rows] = g_ref[0, :, lanes]
        if rows < LANES:
            ref[start + 2 * rows : start + 2 * rows + PAD] = jnp.zeros((PAD, LANES), BF16)
        ref[start + 2 * rows : start + 2 * rows + PAD, :rows] = delta_ref[quarter ^ step]
    for step in range(QUARTERS):
        ref = (kv_own, sib_ref)[step % 2]
        lanes = lanes_of(quarter ^ step)
        start = step // 2 * 2 * krows
        ref[start : start + krows] = k_ref[0, :, lanes]
        ref[start + krows : start + 2 * krows] = v_ref[0, :, lanes]
    every = lse_ref[0]

    def lse_of(wanted_quarter):
        own = every[:local]
        for index in range(1, QUARTERS):
            own = jnp.where(
                wanted_quarter == index, every[local * index : local * (index + 1)], own
            )
        return own

    mine = lse_of(quarter) * LOG2E
    other = (lse_of(quarter ^ 2) * LSE_UNIT).astype(I32)
    for u in range(lse_own.shape[0]):
        lanes = slice(u * LANES, (u + 1) * LANES)
        lse_own[u] = mine[:, lanes]
        packed_ref[capacity // 2 + 1 + u // 4, u % 4 * 2 : u % 4 * 2 + 2] = other[:, lanes]
    for entry in range(capacity):
        words = bits_ref[0, 0, entry]
        span = slice(entry % 2 * 4, entry % 2 * 4 + 4)
        packed_ref[entry // 2, span] = words[:4] | lax.shift_left(words[4:], I32(16))


def key_join_kernel(krows, kv_own, sib_ref, kv_same, kv_pair):
    core = my_place()[2]
    for side, ref in enumerate((kv_same, kv_pair)):
        span = slice(side * 2 * krows, (side + 1) * 2 * krows)
        ref[core] = kv_own[span]
        ref[1 - core] = sib_ref[span]


def query_join_kernel(
    krows, slabs, qg_own, sib_ref, pair0_ref, pair1_ref, bits_own, bits_pair, lse_own,
    qg_out, bits_out, lse_out,
):
    row, chip, core, quarter = my_place()
    side = row % 2
    qg_out[quarter] = qg_own[...]
    qg_out[quarter ^ 1] = sib_ref[4 * krows :]
    qg_out[quarter ^ 2] = pair0_ref[...]
    qg_out[quarter ^ 3] = pair1_ref[...]
    bits_out[side] = bits_own[:slabs]
    bits_out[1 - side] = bits_pair[:slabs]
    lse_out[side] = lse_own[...]
    for u in range(lse_out.shape[1]):
        fixed = bits_pair[slabs + u // 4, u % 4 * 2 : u % 4 * 2 + 2]
        lse_out[1 - side, u] = fixed.astype(F32) * (LOG2E / LSE_UNIT)


def key_place_kernel(head_dim, tile, bits_own, bits_sib, *refs):
    kv_refs, (k_out, v_out, k2t_out, bits_out, info_out) = refs[:-5], refs[-5:]
    krows = kv_refs[0].shape[1] // 2
    row, chip, core, quarter = my_place()
    for step, ref in enumerate(kv_refs):
        start = (row ^ step) * krows
        inner = pl.multiple_of(start % tile, krows)
        for block in range(2):
            k_out[block, start // tile, pl.ds(inner, krows)] = ref[block, :krows]
            v_out[block, start // tile, pl.ds(inner, krows)] = ref[block, krows:]
    low_row = lax.broadcasted_iota(I32, (LANES, tile), 0) < head_dim
    none_t = jnp.zeros((LANES, tile), BF16)
    for block in range(2):
        for w in range(k_out.shape[1]):
            flipped = k_out[block, w].T
            k2t_out[block, w] = jnp.concatenate(
                [jnp.where(low_row, flipped, none_t), jnp.where(low_row, none_t, flipped)], axis=1
            )
    capacity = bits_out.shape[1]
    for block in range(2):
        for ref, column in ((bits_own, core), (bits_sib, 1 - core)):
            which = block * 2 + column
            for entry in range(capacity):
                span = slice(entry % 2 * 4, entry % 2 * 4 + 4)
                bits_out[which, entry] = ref[block, entry // 2, span]
            info_out[which] = ref[block, capacity // 2]


def query_place_kernel(head_dim, tile, *refs):
    qg_refs, (q2_out, g2_out, delta_out) = refs[:-3], refs[-3:]
    rows = (qg_refs[0].shape[1] - PAD) // 2
    chip = my_place()[1]
    low = lax.broadcasted_iota(I32, (rows, LANES), 1) < head_dim
    none = jnp.zeros((rows, LANES), BF16)
    for step, ref in enumerate(qg_refs):
        for index in range(QUARTERS):
            source = (chip ^ step) * 2 + index % 2
            start = source * rows
            u = start // tile
            inner = pl.multiple_of(start % tile, rows)
            block = index // 2
            for out, part in ((q2_out, 0), (g2_out, 1)):
                piece = ref[index, part * rows : (part + 1) * rows]
                out[block, u, 0, pl.ds(inner, rows)] = jnp.where(low, piece, none)
                out[block, u, 1, pl.ds(inner, rows)] = jnp.where(low, none, piece)
            delta = ref[index, 2 * rows :, :rows].astype(F32)
            if rows == tile:
                delta_out[block, u] = delta
            else:
                for part in range(tile // rows):
                    @pl.when(source % (tile // rows) == part)
                    def _(part=part, delta=delta, u=u, block=block):
                        delta_out[block, u, :, part * rows : (part + 1) * rows] = delta


def pair_kernel(head_dim, krows, steps, far, *refs):
    (q2_ref, g2_ref, delta_ref, k_ref, v_ref, k2t_ref, bits_ref, info_hbm, lse_ref), refs = (
        refs[:9], refs[9:]
    )
    if not far:
        dqt_far, refs = refs[0], refs[1:]
    dqt_ref, dkv_refs, refs = refs[0], refs[1 : 1 + len(steps)], refs[1 + len(steps) :]
    dqt_scr, dk_scr, dv_scr, info, todo, sem = refs
    key_tiles, tile = k_ref.shape[1:3]
    scaling = float(head_dim) ** -0.5
    row = my_place()[0]
    copy = pltpu.make_async_copy(info_hbm, info, sem)
    copy.start()
    dqt_scr[...] = jnp.zeros_like(dqt_scr) if far else dqt_far[...]
    dk_scr[...] = jnp.zeros_like(dk_scr)
    dv_scr[...] = jnp.zeros_like(dv_scr)
    place_in = lax.broadcasted_iota(I32, (2, 4, 16, tile), 2)
    upper = lax.broadcasted_iota(I32, (2, 4, 16, tile), 0)
    bit = lax.shift_left(I32(1), place_in + 16 * upper).reshape(tile, tile)
    copy.wait()

    count = I32(0)
    near0, near1 = row * krows // tile, (row ^ 1) * krows // tile
    for which in range(QUARTERS):

        def listed(entry, count, which=which):
            slot = info[which, 0, entry]
            w = slot % key_tiles
            near = jnp.logical_or(w == near0, w == near1)
            todo[count] = slot + 32 * entry + 1024 * which
            return count + jnp.where(near, I32(1 - far), I32(far))

        count = lax.fori_loop(0, info[which, 1, 0], listed, count)

    def two_tiles(index, _):
        work = []
        for part in range(2):
            item = todo[jnp.minimum(index * 2 + part, count - 1)]
            slot = item % 32
            which = item // 1024
            qb, kb = which // 2, which % 2
            u = slot // key_tiles
            w = slot % key_tiles
            words = bits_ref[which, item // 32 % 32]
            if part:
                words = words & jnp.where(index * 2 + 1 < count, I32(-1), I32(0))
            words = jnp.broadcast_to(words[:, None, :], (4, 16, tile)).reshape(64, tile)
            edge = (jnp.concatenate([words, words], axis=0) & bit) != 0
            q2 = q2_ref[qb, u].reshape(2 * tile, LANES)
            g2 = g2_ref[qb, u].reshape(2 * tile, LANES)
            scores = lax.dot_general(k_ref[kb, w], q2, NT, preferred_element_type=F32)
            grad_prob = lax.dot_general(v_ref[kb, w], g2, NT, preferred_element_type=F32)
            work.append((qb, kb, u, w, edge, q2, g2, scores, grad_prob))
        done = []
        for qb, kb, u, w, edge, q2, g2, scores, grad_prob in work:
            lse_tile = lse_ref[qb, u]
            delta_tile = delta_ref[qb, u]
            probs, grads = [], []
            for h in range(2):
                s = scores[:, h * tile : (h + 1) * tile]
                gp = grad_prob[:, h * tile : (h + 1) * tile]
                p = jnp.exp2(s * (scaling * LOG2E) - lse_tile[h : h + 1])
                p = jnp.where(edge, p, 0.0)
                ds = p * (gp - delta_tile[h : h + 1])
                probs.append(p.astype(BF16))
                grads.append(ds.astype(BF16))
            done.append((
                lax.dot_general(
                    jnp.concatenate(probs, axis=1), g2, NN, preferred_element_type=F32
                ),
                lax.dot_general(
                    jnp.concatenate(grads, axis=1), q2, NN, preferred_element_type=F32
                ),
                lax.dot_general(
                    k2t_ref[kb, w], jnp.concatenate(grads, axis=0), NN,
                    preferred_element_type=F32,
                ),
            ))
        for (qb, kb, u, w, *_), (dv, dk, dqt) in zip(work, done):
            dv_scr[kb, w] += dv
            dk_scr[kb, w] += dk
            dqt_scr[qb, u] += dqt
        return 0

    lax.fori_loop(0, (count + 1) // 2, two_tiles, 0)

    for step, ref in zip(steps, dkv_refs):
        start = (row ^ step) * krows
        inner = pl.multiple_of(start % tile, krows)
        for block in range(2):
            dk = dk_scr[block, start // tile, pl.ds(inner, krows)] * scaling
            dv = dv_scr[block, start // tile, pl.ds(inner, krows)]
            ref[block, :krows] = dk.astype(BF16)
            ref[block, krows:] = dv.astype(BF16)
    dqt_ref[...] = dqt_scr[...] if far else (dqt_scr[...] * scaling).astype(BF16)


def turn_kernel(rows, dqt_ref, *refs):
    dq_refs, dq_scr = refs[:-1], refs[-1]
    tile = dqt_ref.shape[3]
    chip = my_place()[1]
    for block in range(2):
        for u in range(dqt_ref.shape[1]):
            dq_scr[block, u * tile : (u + 1) * tile] = dqt_ref[block, u].T
    for step, ref in enumerate(dq_refs):
        for index in range(QUARTERS):
            start = pl.multiple_of(((chip ^ step) * 2 + index % 2) * rows, rows)
            ref[index] = dq_scr[index // 2, pl.ds(start, rows)]


def query_sum_kernel(chips, *refs):
    parts, outs = refs[:chips], refs[chips:]
    quarter = my_place()[3]
    for step, out in enumerate(outs):
        total = parts[0][quarter ^ step].astype(F32)
        for part in parts[1:]:
            total += part[quarter ^ step].astype(F32)
        out[...] = total.astype(BF16)


def far_sum_kernel(*refs):
    parts, out = refs[:-1], refs[-1]
    for side in range(2):
        total = parts[side][...].astype(F32)
        for other in range(side + 2, len(parts), 2):
            total += parts[other][...].astype(F32)
        out[side] = total


def key_sum_kernel(far_ref, *refs):
    parts, (own_ref, sib_ref) = refs[:-2], refs[-2:]
    core = my_place()[2]
    for ref, block in ((own_ref, core), (sib_ref, 1 - core)):
        for side in range(2):
            total = far_ref[side, block]
            for other in range(side, len(parts), 2):
                total += parts[other][block].astype(F32)
            ref[side] = total.astype(BF16)


def finish_kernel(own_ref, sib_ref, *refs):
    dq_refs, (dq_out, dk_out, dv_out) = refs[:QUARTERS], refs[QUARTERS:]
    krows = dk_out.shape[1]
    quarter = my_place()[3]
    for step, dq in enumerate(dq_refs):
        lanes = lanes_of(quarter ^ step)
        dkv = (own_ref, sib_ref)[step % 2]
        dk_out[0, :, lanes] = dkv[step // 2, :krows]
        dv_out[0, :, lanes] = dkv[step // 2, krows:]
        dq_out[0, :, lanes] = dq[...]


def send(block, axes, count, step):
    return lax.ppermute(block, axes, [(place, place ^ step) for place in range(count)])


def body(sizes, queries, keys, values, outputs, grad_out, lse, tile_slot, tile_live, tile_bits):
    row_count, chips, cores = sizes
    heads = lse.shape[1]
    width = queries.shape[2]
    head_dim = width // heads
    tile = tile_bits.shape[4]
    capacity = tile_slot.shape[2]
    rows = queries.shape[1]
    krows = keys.shape[1]
    query_tiles = lse.shape[2] // tile
    key_tiles = row_count * krows // tile
    line = ("row", "core")
    places = row_count * cores

    def shape(*dims, dtype=BF16):
        return jax.ShapeDtypeStruct(dims, dtype)

    qg_shape = shape(2 * rows + PAD, LANES)
    kv_shape = shape(2, 2 * krows, LANES)
    slabs = capacity // 2 + 1
    qg_own, pair0, pair1, kv_own, to_sibling, bits_own, lse_own = pl.pallas_call(
        functools.partial(pack_kernel, heads),
        out_shape=(
            qg_shape, qg_shape, qg_shape, shape(4 * krows, LANES),
            shape(4 * krows + 2 * rows + PAD, LANES),
            shape(slabs + query_tiles // 4, 8, LANES, dtype=I32),
            shape(query_tiles, 2, tile, dtype=F32),
        ),
        in_specs=[HBM] * 7 + [VMEM] * 2,
        out_specs=(VMEM,) * 7,
        scratch_shapes=[
            pltpu.VMEM(queries.shape, BF16),
            pltpu.VMEM(queries.shape, BF16),
            pltpu.VMEM(queries.shape, BF16),
            pltpu.VMEM(keys.shape, BF16),
            pltpu.VMEM(keys.shape, BF16),
            pltpu.VMEM(tile_bits.shape, I32),
            pltpu.VMEM(lse.shape, F32),
            pltpu.VMEM((QUARTERS, PAD, rows), BF16),
            pltpu.SemaphoreType.DMA((7,)),
        ],
        compiler_params=PACK,
        name="pack",
    )(queries, grad_out, outputs, keys, values, tile_bits, lse, tile_slot, tile_live)

    pair0 = send(pair0, line, places, 2)
    pair1 = send(pair1, line, places, 3)
    from_sibling = send(to_sibling, "core", cores, 1)
    bits_pair = send(bits_own, "row", row_count, 1)
    kv_same, kv_pair = pl.pallas_call(
        functools.partial(key_join_kernel, krows),
        out_shape=(kv_shape, kv_shape),
        in_specs=[VMEM] * 2,
        out_specs=(VMEM,) * 2,
        compiler_params=SMALL,
        name="key_join",
    )(kv_own, from_sibling)
    kv_out = (kv_same, kv_pair)
    kv = [kv_same] + [
        send(kv_out[step % 2], "row", row_count, step) for step in range(1, row_count)
    ]
    qg, bits, lse2 = pl.pallas_call(
        functools.partial(query_join_kernel, krows, slabs),
        out_shape=(
            shape(QUARTERS, 2 * rows + PAD, LANES),
            shape(2, slabs, 8, LANES, dtype=I32),
            shape(2, query_tiles, 2, tile, dtype=F32),
        ),
        in_specs=[VMEM] * 7,
        out_specs=(VMEM,) * 3,
        compiler_params=SMALL,
        name="query_join",
    )(qg_own, from_sibling, pair0, pair1, bits_own, bits_pair, lse_own)
    qg = [qg] + [send(qg, "chip", chips, step) for step in range(1, chips)]
    bits_sibling = send(bits, "core", cores, 1)

    placed_keys = pl.pallas_call(
        functools.partial(key_place_kernel, head_dim, tile),
        out_shape=(
            shape(2, key_tiles, tile, LANES), shape(2, key_tiles, tile, LANES),
            shape(2, key_tiles, LANES, 2 * tile),
            shape(QUARTERS, capacity, 4, LANES, dtype=I32), shape(QUARTERS, 8, LANES, dtype=I32),
        ),
        in_specs=[VMEM] * (row_count + 2),
        out_specs=(VMEM,) * 5,
        compiler_params=SMALL,
        name="key_place",
    )(bits, bits_sibling, *kv)
    placed_queries = pl.pallas_call(
        functools.partial(query_place_kernel, head_dim, tile),
        out_shape=(
            shape(2, query_tiles, 2, tile, LANES), shape(2, query_tiles, 2, tile, LANES),
            shape(2, query_tiles, PAD, tile, dtype=F32),
        ),
        in_specs=[VMEM] * chips,
        out_specs=(VMEM,) * 3,
        compiler_params=SMALL,
        name="query_place",
    )(*qg)
    near = max(2, tile // krows)
    dkv = [None] * row_count
    dqt = ()
    for far, steps in ((1, range(near, row_count)), (0, range(near))):
        dqt, *parts = pl.pallas_call(
            functools.partial(pair_kernel, head_dim, krows, tuple(steps), far),
            out_shape=(shape(2, query_tiles, LANES, tile, dtype=F32 if far else BF16),)
            + (kv_shape,) * len(steps),
            in_specs=[VMEM] * (9 + len(dqt)),
            out_specs=(VMEM,) * (1 + len(steps)),
            scratch_shapes=[
                pltpu.VMEM((2, query_tiles, LANES, tile), F32),
                pltpu.VMEM((2, key_tiles, tile, LANES), F32),
                pltpu.VMEM((2, key_tiles, tile, LANES), F32),
                pltpu.SMEM((QUARTERS, 8, LANES), I32),
                pltpu.SMEM((QUARTERS * capacity + 1,), I32),
                pltpu.SemaphoreType.DMA,
            ],
            compiler_params=MEDIUM,
            cost_estimate=early(10),
            name="far" if far else "near",
        )(*placed_queries, *placed_keys, lse2, *dqt)
        dqt = (dqt,)
        for step, part in zip(steps, parts):
            dkv[step] = part

    dq = pl.pallas_call(
        functools.partial(turn_kernel, rows),
        out_shape=(shape(QUARTERS, rows, LANES),) * chips,
        in_specs=[VMEM],
        out_specs=(VMEM,) * chips,
        scratch_shapes=[pltpu.VMEM((2, query_tiles * tile, LANES), BF16)],
        compiler_params=SMALL,
        name="turn",
    )(*dqt)
    dq = [dq[0]] + [send(dq[step], "chip", chips, step) for step in range(1, chips)]
    dkv = [dkv[0]] + [send(dkv[step], "row", row_count, step) for step in range(1, row_count)]
    dq = pl.pallas_call(
        functools.partial(query_sum_kernel, chips),
        out_shape=(shape(rows, LANES),) * QUARTERS,
        in_specs=[VMEM] * chips,
        out_specs=(VMEM,) * QUARTERS,
        compiler_params=SMALL,
        name="query_sum",
    )(*dq)
    dq = [dq[0]] + [send(dq[step], line, places, step) for step in range(1, QUARTERS)]
    far_sum = pl.pallas_call(
        far_sum_kernel,
        out_shape=shape(2, 2, 2 * krows, LANES, dtype=F32),
        in_specs=[VMEM] * (row_count - near),
        out_specs=VMEM,
        compiler_params=SMALL,
        cost_estimate=early(20),
        name="far_sum",
    )(*dkv[near:])
    dkv_own, dkv_sibling = pl.pallas_call(
        key_sum_kernel,
        out_shape=(kv_shape,) * 2,
        in_specs=[VMEM] * (1 + near),
        out_specs=(VMEM,) * 2,
        compiler_params=SMALL,
        name="key_sum",
    )(far_sum, *dkv[:near])
    dkv_sibling = send(dkv_sibling, "core", cores, 1)
    return pl.pallas_call(
        finish_kernel,
        out_shape=(shape(1, rows, width), shape(1, krows, width), shape(1, krows, width)),
        in_specs=[VMEM] * (2 + QUARTERS),
        out_specs=(VMEM,) * 3,
        compiler_params=SMALL,
        name="finish",
    )(dkv_own, dkv_sibling, *dq)


def solution(mesh):
    row_count, columns = mesh.devices.shape
    cores = 2
    chips = columns // cores
    fine = Mesh(mesh.devices.reshape(row_count, chips, cores), ("row", "chip", "core"))
    col = ("chip", "core")
    in_specs = (
        P("row", col, None),
        P(col, "row", None),
        P(col, "row", None),
        P("row", col, None),
        P("row", col, None),
        P("row", None, None),
        P("row", col, None),
        P("row", col),
        P("row", col, None, None, None),
    )
    out_specs = (P("row", col, None), P(col, "row", None), P(col, "row", None))
    return jax.shard_map(
        functools.partial(body, (row_count, chips, cores)),
        mesh=fine, in_specs=in_specs, out_specs=out_specs, check_vma=False,
    )
```

```python
import functools

import jax
import jax.numpy as jnp
from jax import lax
from jax.experimental import pallas as pl
from jax.experimental.pallas import tpu as pltpu
from jax.sharding import Mesh
from jax.sharding import PartitionSpec as P


F32 = jnp.float32
BF16 = jnp.bfloat16
I32 = jnp.int32
LANES = 128
PAD = 16
QUARTERS = 4
LOG2E = 1.4426950408889634
LSE_UNIT = 2.0**21
NT = (((1,), (1,)), ((), ()))
NN = (((1,), (0,)), ((), ()))
MEDIUM = pltpu.CompilerParams(vmem_limit_bytes=28 * 1024 * 1024)
PACK = pltpu.CompilerParams(vmem_limit_bytes=int(53.6 * 1024 * 1024))
SMALL = pltpu.CompilerParams(vmem_limit_bytes=12 * 1024 * 1024)
def early(gigaflops):
    return pl.CostEstimate(flops=gigaflops * 10**9, bytes_accessed=0, transcendentals=0)


VMEM = pl.BlockSpec(memory_space=pltpu.VMEM)
HBM = pl.BlockSpec(memory_space=pltpu.HBM)


def lanes_of(quarter):
    return pl.ds(pl.multiple_of(quarter * LANES, LANES), LANES)


def my_place():
    row, chip, core = (lax.axis_index(name) for name in ("row", "chip", "core"))
    return row, chip, core, row % 2 * 2 + core


def pack_query_kernel(
    heads, q_hbm, g_hbm, o_hbm, own_ref, sib_ref, pair0_ref, pair1_ref,
    q_ref, g_ref, o_ref, delta_ref, sems,
):
    arrays = ((q_hbm, q_ref), (g_hbm, g_ref), (o_hbm, o_ref))
    copies = [pltpu.make_async_copy(a, b, sems.at[i]) for i, (a, b) in enumerate(arrays)]
    for copy in copies:
        copy.start()
    rows, width = q_ref.shape[1:]
    head_dim = width // heads
    local = heads // QUARTERS
    quarter = my_place()[3]
    feature = lax.broadcasted_iota(I32, (QUARTERS * PAD, width), 1)
    line = lax.broadcasted_iota(I32, (QUARTERS * PAD, width), 0)
    wanted = jnp.where(line % PAD < local, line // PAD * local + line % PAD, -1)
    pick = (feature // head_dim == wanted).astype(F32)
    for copy in copies:
        copy.wait()
    product = g_ref[0].astype(F32) * o_ref[0].astype(F32)
    delta = lax.dot_general(
        pick, product, NT, precision=lax.Precision.HIGHEST, preferred_element_type=F32
    ).astype(BF16)
    for index in range(QUARTERS):
        delta_ref[index] = delta[index * PAD : (index + 1) * PAD]
    for step, ref in enumerate((own_ref, sib_ref, pair0_ref, pair1_ref)):
        lanes = lanes_of(quarter ^ step)
        ref[:rows] = q_ref[0, :, lanes]
        ref[rows : 2 * rows] = g_ref[0, :, lanes]
        if rows < LANES:
            ref[2 * rows :] = jnp.zeros((PAD, LANES), BF16)
        ref[2 * rows :, :rows] = delta_ref[quarter ^ step]


def pack_key_kernel(
    local, k_hbm, v_hbm, bits_hbm, lse_hbm, slot_ref, live_ref, _after0, _after1, _after2,
    own_ref, sib_ref, packed_ref, lse_own, k_ref, v_ref, bits_ref, lse_ref, sems,
):
    arrays = ((k_hbm, k_ref), (v_hbm, v_ref), (bits_hbm, bits_ref), (lse_hbm, lse_ref))
    copies = [pltpu.make_async_copy(a, b, sems.at[i]) for i, (a, b) in enumerate(arrays)]
    for copy in copies:
        copy.start()
    krows = k_ref.shape[1]
    capacity = bits_ref.shape[2]
    quarter = my_place()[3]
    packed_ref[capacity // 2] = jnp.zeros((8, LANES), I32)
    packed_ref[capacity // 2, 0:1, 0:capacity] = slot_ref[0]
    packed_ref[capacity // 2, 1:2, 0:1] = live_ref[...]
    for copy in copies:
        copy.wait()
    for step in range(QUARTERS):
        ref = (own_ref, sib_ref)[step % 2]
        lanes = lanes_of(quarter ^ step)
        start = step // 2 * 2 * krows
        ref[start : start + krows] = k_ref[0, :, lanes]
        ref[start + krows : start + 2 * krows] = v_ref[0, :, lanes]
    every = lse_ref[0]

    def lse_of(wanted_quarter):
        own = every[:local]
        for index in range(1, QUARTERS):
            own = jnp.where(
                wanted_quarter == index, every[local * index : local * (index + 1)], own
            )
        return own

    mine = lse_of(quarter) * LOG2E
    other = (lse_of(quarter ^ 2) * LSE_UNIT).astype(I32)
    for u in range(lse_own.shape[0]):
        lanes = slice(u * LANES, (u + 1) * LANES)
        lse_own[u] = mine[:, lanes]
        packed_ref[capacity // 2 + 1 + u // 4, u % 4 * 2 : u % 4 * 2 + 2] = other[:, lanes]
    for entry in range(capacity):
        words = bits_ref[0, 0, entry]
        span = slice(entry % 2 * 4, entry % 2 * 4 + 4)
        packed_ref[entry // 2, span] = words[:4] | lax.shift_left(words[4:], I32(16))


def key_join_kernel(krows, kv_own, sib_ref, kv_same, kv_pair):
    core = my_place()[2]
    for side, ref in enumerate((kv_same, kv_pair)):
        span = slice(side * 2 * krows, (side + 1) * 2 * krows)
        ref[core] = kv_own[span]
        ref[1 - core] = sib_ref[span]


def query_join_kernel(own_ref, sib_ref, pair0_ref, pair1_ref, out):
    quarter = my_place()[3]
    for step, ref in enumerate((own_ref, sib_ref, pair0_ref, pair1_ref)):
        out[quarter ^ step] = ref[...]


def far_join_kernel(*refs):
    for index, ref in enumerate(refs[:-1]):
        refs[-1][index] = ref[...]


def pair_kernel(sizes, *refs):
    head_dim, tile, capacity, chips, row_count = sizes
    qg_refs, refs = refs[:chips], refs[chips:]
    (same_ref, pair_ref, far_ref), refs = refs[:3], refs[3:]
    bits_refs, lse_own, refs = refs[:QUARTERS], refs[QUARTERS], refs[QUARTERS + 1 :]
    dqt_ref, dkv_refs, refs = refs[0], refs[1 : 1 + row_count], refs[1 + row_count :]
    (q2_scr, g2_scr, k_scr, v_scr, k2t_scr, lse_scr, delta_scr, dqt_scr, dk_scr, dv_scr,
     info, sems) = refs
    rows = (qg_refs[0].shape[1] - PAD) // 2
    krows = dkv_refs[0].shape[1] // 2
    query_tiles = q2_scr.shape[1]
    key_tiles = k_scr.shape[1]
    scaling = float(head_dim) ** -0.5
    row, chip, core, quarter = my_place()
    side = row % 2
    slabs = capacity // 2 + 1

    copies = [
        pltpu.make_async_copy(ref.at[slabs - 1], info.at[i], sems.at[i])
        for i, ref in enumerate(bits_refs)
    ]
    for copy in copies:
        copy.start()
    lse_scr[side] = lse_own[...]
    for u in range(query_tiles):
        fixed = bits_refs[2][slabs + u // 4, u % 4 * 2 : u % 4 * 2 + 2]
        lse_scr[1 - side, u] = fixed.astype(F32) * (LOG2E / LSE_UNIT)
    low = lax.broadcasted_iota(I32, (rows, LANES), 1) < head_dim
    none = jnp.zeros((rows, LANES), BF16)
    for step in range(chips):
        for index in range(QUARTERS):
            source = (chip ^ step) * 2 + index % 2
            start = source * rows
            u = start // tile
            inner = pl.multiple_of(start % tile, rows)
            block = index // 2
            for scr, part in ((q2_scr, 0), (g2_scr, 1)):
                piece = qg_refs[step][index, part * rows : (part + 1) * rows]
                scr[block, u, 0, pl.ds(inner, rows)] = jnp.where(low, piece, none)
                scr[block, u, 1, pl.ds(inner, rows)] = jnp.where(low, none, piece)
            delta = qg_refs[step][index, 2 * rows :, :rows].astype(F32)
            if rows == tile:
                delta_scr[block, u] = delta
            else:
                for part in range(tile // rows):
                    @pl.when(source % (tile // rows) == part)
                    def _(part=part, delta=delta, u=u, block=block):
                        delta_scr[block, u, :, part * rows : (part + 1) * rows] = delta
    sources = [same_ref, pair_ref] + [far_ref.at[index] for index in range(row_count - 2)]
    for step, ref in enumerate(sources):
        start = (row ^ step) * krows
        inner = pl.multiple_of(start % tile, krows)
        for block in range(2):
            k_scr[block, start // tile, pl.ds(inner, krows)] = ref[block, :krows]
            v_scr[block, start // tile, pl.ds(inner, krows)] = ref[block, krows:]
    low_row = lax.broadcasted_iota(I32, (LANES, tile), 0) < head_dim
    none_t = jnp.zeros((LANES, tile), BF16)
    for block in range(2):
        for w in range(key_tiles):
            flipped = k_scr[block, w].T
            k2t_scr[block, w] = jnp.concatenate(
                [jnp.where(low_row, flipped, none_t), jnp.where(low_row, none_t, flipped)], axis=1
            )
    dqt_scr[...] = jnp.zeros_like(dqt_scr)
    dk_scr[...] = jnp.zeros_like(dk_scr)
    dv_scr[...] = jnp.zeros_like(dv_scr)
    place_in = lax.broadcasted_iota(I32, (2, 4, 16, tile), 2)
    upper = lax.broadcasted_iota(I32, (2, 4, 16, tile), 0)
    bit = lax.shift_left(I32(1), place_in + 16 * upper).reshape(tile, tile)
    for copy in copies:
        copy.wait()

    for step in range(QUARTERS):
        qb = side ^ (step // 2)
        kb = core ^ (step % 2)
        live = info[step, 1, 0]

        def two_tiles(index, _, step=step, qb=qb, kb=kb, live=live):
            both = bits_refs[step][index]
            second = jnp.where(index * 2 + 1 < live, I32(-1), I32(0))
            work = []
            for part in range(2):
                slot = info[step, 0, index * 2 + part]
                u = slot // key_tiles
                w = slot % key_tiles
                words = both[part * 4 : part * 4 + 4]
                if part:
                    words = words & second
                words = jnp.broadcast_to(words[:, None, :], (4, 16, tile)).reshape(64, tile)
                edge = (jnp.concatenate([words, words], axis=0) & bit) != 0
                q2 = q2_scr[qb, u].reshape(2 * tile, LANES)
                g2 = g2_scr[qb, u].reshape(2 * tile, LANES)
                scores = lax.dot_general(k_scr[kb, w], q2, NT, preferred_element_type=F32)
                grad_prob = lax.dot_general(v_scr[kb, w], g2, NT, preferred_element_type=F32)
                work.append((u, w, edge, q2, g2, scores, grad_prob))
            done = []
            for u, w, edge, q2, g2, scores, grad_prob in work:
                lse_tile = lse_scr[qb, u]
                delta_tile = delta_scr[qb, u]
                probs, grads = [], []
                for h in range(2):
                    s = scores[:, h * tile : (h + 1) * tile]
                    gp = grad_prob[:, h * tile : (h + 1) * tile]
                    p = jnp.exp2(s * (scaling * LOG2E) - lse_tile[h : h + 1])
                    p = jnp.where(edge, p, 0.0)
                    ds = p * (gp - delta_tile[h : h + 1])
                    probs.append(p.astype(BF16))
                    grads.append(ds.astype(BF16))
                done.append((
                    lax.dot_general(
                        jnp.concatenate(probs, axis=1), g2, NN, preferred_element_type=F32
                    ),
                    lax.dot_general(
                        jnp.concatenate(grads, axis=1), q2, NN, preferred_element_type=F32
                    ),
                    lax.dot_general(
                        k2t_scr[kb, w], jnp.concatenate(grads, axis=0), NN,
                        preferred_element_type=F32,
                    ),
                ))
            for (u, w, *_), (dv, dk, dqt) in zip(work, done):
                dv_scr[kb, w] += dv
                dk_scr[kb, w] += dk
                dqt_scr[qb, u] += dqt
            return 0

        lax.fori_loop(0, (live + 1) // 2, two_tiles, 0)

    for step in range(row_count):
        start = (row ^ step) * krows
        inner = pl.multiple_of(start % tile, krows)
        for block in range(2):
            dk = dk_scr[block, start // tile, pl.ds(inner, krows)] * scaling
            dv = dv_scr[block, start // tile, pl.ds(inner, krows)]
            dkv_refs[step][block, :krows] = dk.astype(BF16)
            dkv_refs[step][block, krows:] = dv.astype(BF16)
    dqt_ref[...] = (dqt_scr[...] * scaling).astype(BF16)


def turn_kernel(rows, dqt_ref, *refs):
    dq_refs, dq_scr = refs[:-1], refs[-1]
    tile = dqt_ref.shape[3]
    chip = my_place()[1]
    for block in range(2):
        for u in range(dqt_ref.shape[1]):
            dq_scr[block, u * tile : (u + 1) * tile] = dqt_ref[block, u].T
    for step, ref in enumerate(dq_refs):
        for index in range(QUARTERS):
            start = pl.multiple_of(((chip ^ step) * 2 + index % 2) * rows, rows)
            ref[index] = dq_scr[index // 2, pl.ds(start, rows)]


def query_sum_kernel(chips, *refs):
    parts, (same_ref, pair_ref) = refs[:chips], refs[chips:]
    side = my_place()[0] % 2
    for step, ref in enumerate((same_ref, pair_ref)):
        for core in range(2):
            index = (side ^ step) * 2 + core
            total = parts[0][index].astype(F32)
            for part in parts[1:]:
                total += part[index].astype(F32)
            ref[core] = total.astype(BF16)


def key_sum_kernel(row_count, *refs):
    dkv_refs, (own_ref, sib_ref) = refs[:-2], refs[-2:]
    core = my_place()[2]
    for ref, block in ((own_ref, core), (sib_ref, 1 - core)):
        for side in range(2):
            total = dkv_refs[side][block].astype(F32)
            for other in range(side + 2, row_count, 2):
                total += dkv_refs[other][block].astype(F32)
            ref[side] = total.astype(BF16)


def bundle_kernel(dkv_ref, dq_same, dq_pair, out):
    krows2 = dkv_ref.shape[1]
    sibling = 1 - my_place()[2]
    out[:, :krows2] = dkv_ref[...]
    for side, dq in enumerate((dq_same, dq_pair)):
        out[side, krows2:] = dq[sibling]


def finish_kernel(krows, dkv_own, dq_same, dq_pair, sib_ref, dq_out, dk_out, dv_out):
    row, chip, core, quarter = my_place()
    for side, dq in enumerate((dq_same, dq_pair)):
        for step, ref in enumerate((dkv_own, sib_ref)):
            lanes = lanes_of(quarter ^ (2 * side + step))
            dk_out[0, :, lanes] = ref[side, :krows]
            dv_out[0, :, lanes] = ref[side, krows : 2 * krows]
            dq_out[0, :, lanes] = ref[side, 2 * krows :] if step else dq[core]


def send(block, axes, count, step):
    return lax.ppermute(block, axes, [(place, place ^ step) for place in range(count)])


def body(sizes, queries, keys, values, outputs, grad_out, lse, tile_slot, tile_live, tile_bits):
    row_count, chips, cores = sizes
    heads = lse.shape[1]
    width = queries.shape[2]
    head_dim = width // heads
    tile = tile_bits.shape[4]
    capacity = tile_slot.shape[2]
    rows = queries.shape[1]
    krows = keys.shape[1]
    query_tiles = lse.shape[2] // tile
    key_tiles = row_count * krows // tile
    line = ("row", "core")
    places = row_count * cores

    def shape(*dims, dtype=BF16):
        return jax.ShapeDtypeStruct(dims, dtype)

    qg_shape = shape(2 * rows + PAD, LANES)
    kv_shape = shape(2, 2 * krows, LANES)
    slabs = capacity // 2 + 1
    qg_own, qg_sibling, pair0, pair1 = pl.pallas_call(
        functools.partial(pack_query_kernel, heads),
        out_shape=(qg_shape,) * QUARTERS,
        in_specs=[HBM] * 3,
        out_specs=(VMEM,) * QUARTERS,
        scratch_shapes=[
            pltpu.VMEM(queries.shape, BF16),
            pltpu.VMEM(queries.shape, BF16),
            pltpu.VMEM(queries.shape, BF16),
            pltpu.VMEM((QUARTERS, PAD, rows), BF16),
            pltpu.SemaphoreType.DMA((3,)),
        ],
        compiler_params=PACK,
        name="pack_query",
    )(queries, grad_out, outputs)
    pair0 = send(pair0, line, places, 2)
    pair1 = send(pair1, line, places, 3)
    qg_sibling = send(qg_sibling, "core", cores, 1)
    kv_own, kv_sibling, bits_own, lse_own = pl.pallas_call(
        functools.partial(pack_key_kernel, heads // QUARTERS),
        out_shape=(
            shape(4 * krows, LANES), shape(4 * krows, LANES),
            shape(slabs + query_tiles // 4, 8, LANES, dtype=I32),
            shape(query_tiles, 2, tile, dtype=F32),
        ),
        in_specs=[HBM] * 4 + [VMEM] * 2 + [HBM] * 3,
        out_specs=(VMEM,) * 4,
        scratch_shapes=[
            pltpu.VMEM(keys.shape, BF16),
            pltpu.VMEM(keys.shape, BF16),
            pltpu.VMEM(tile_bits.shape, I32),
            pltpu.VMEM(lse.shape, F32),
            pltpu.SemaphoreType.DMA((4,)),
        ],
        compiler_params=PACK,
        name="pack_key",
    )(keys, values, tile_bits, lse, tile_slot, tile_live, qg_sibling, pair0, pair1)
    kv_sibling = send(kv_sibling, "core", cores, 1)
    bits_pair = send(bits_own, "row", row_count, 1)
    bits = [bits_own, send(bits_own, "core", cores, 1), bits_pair, send(bits_pair, "core", cores, 1)]
    kv_same, kv_pair = pl.pallas_call(
        functools.partial(key_join_kernel, krows),
        out_shape=(kv_shape, kv_shape),
        in_specs=[VMEM] * 2,
        out_specs=(VMEM,) * 2,
        compiler_params=SMALL,
        name="key_join",
    )(kv_own, kv_sibling)
    kv_out = (kv_same, kv_pair)
    kv_far = pl.pallas_call(
        far_join_kernel,
        out_shape=shape(row_count - 2, 2, 2 * krows, LANES),
        in_specs=[VMEM] * (row_count - 2),
        out_specs=VMEM,
        compiler_params=SMALL,
        name="far_join",
    )(*[send(kv_out[step % 2], "row", row_count, step) for step in range(2, row_count)])
    kv_pair = send(kv_pair, "row", row_count, 1)
    qg = pl.pallas_call(
        query_join_kernel,
        out_shape=shape(QUARTERS, 2 * rows + PAD, LANES),
        in_specs=[VMEM] * QUARTERS,
        out_specs=VMEM,
        compiler_params=SMALL,
        cost_estimate=early(60),
        name="query_join",
    )(qg_own, qg_sibling, pair0, pair1)
    qg = [qg] + [send(qg, "chip", chips, step) for step in range(1, chips)]

    parts = pl.pallas_call(
        functools.partial(pair_kernel, (head_dim, tile, capacity, chips, row_count)),
        out_shape=(shape(2, query_tiles, LANES, tile),) + (kv_shape,) * row_count,
        in_specs=[VMEM] * (chips + 4 + QUARTERS),
        out_specs=(VMEM,) * (1 + row_count),
        scratch_shapes=[
            pltpu.VMEM((2, query_tiles, 2, tile, LANES), BF16),
            pltpu.VMEM((2, query_tiles, 2, tile, LANES), BF16),
            pltpu.VMEM((2, key_tiles, tile, LANES), BF16),
            pltpu.VMEM((2, key_tiles, tile, LANES), BF16),
            pltpu.VMEM((2, key_tiles, LANES, 2 * tile), BF16),
            pltpu.VMEM((2, query_tiles, 2, tile), F32),
            pltpu.VMEM((2, query_tiles, PAD, tile), F32),
            pltpu.VMEM((2, query_tiles, LANES, tile), F32),
            pltpu.VMEM((2, key_tiles, tile, LANES), F32),
            pltpu.VMEM((2, key_tiles, tile, LANES), F32),
            pltpu.SMEM((QUARTERS, 8, LANES), I32),
            pltpu.SemaphoreType.DMA((QUARTERS,)),
        ],
        compiler_params=MEDIUM,
        name="pair",
    )(*qg, kv_same, kv_pair, kv_far, *bits, lse_own)

    dkv = parts[1:]
    dq = pl.pallas_call(
        functools.partial(turn_kernel, rows),
        out_shape=(shape(QUARTERS, rows, LANES),) * chips,
        in_specs=[VMEM],
        out_specs=(VMEM,) * chips,
        scratch_shapes=[pltpu.VMEM((2, query_tiles * tile, LANES), BF16)],
        compiler_params=SMALL,
        name="turn",
    )(parts[0])
    dq = [dq[0]] + [send(dq[step], "chip", chips, step) for step in range(1, chips)]
    dkv = [dkv[0]] + [send(dkv[step], "row", row_count, step) for step in range(1, row_count)]
    dq_same, dq_pair = pl.pallas_call(
        functools.partial(query_sum_kernel, chips),
        out_shape=(shape(2, rows, LANES),) * 2,
        in_specs=[VMEM] * chips,
        out_specs=(VMEM,) * 2,
        compiler_params=SMALL,
        name="query_sum",
    )(*dq)
    dq_pair = send(dq_pair, "row", row_count, 1)
    dkv_own, dkv_sibling = pl.pallas_call(
        functools.partial(key_sum_kernel, row_count),
        out_shape=(kv_shape,) * 2,
        in_specs=[VMEM] * row_count,
        out_specs=(VMEM,) * 2,
        compiler_params=SMALL,
        cost_estimate=early(20),
        name="key_sum",
    )(*dkv)
    to_sibling = pl.pallas_call(
        bundle_kernel,
        out_shape=shape(2, 2 * krows + rows, LANES),
        in_specs=[VMEM] * 3,
        out_specs=VMEM,
        compiler_params=SMALL,
        name="bundle",
    )(dkv_sibling, dq_same, dq_pair)
    from_sibling = send(to_sibling, "core", cores, 1)
    return pl.pallas_call(
        functools.partial(finish_kernel, krows),
        out_shape=(shape(1, rows, width), shape(1, krows, width), shape(1, krows, width)),
        in_specs=[VMEM] * 4,
        out_specs=(VMEM,) * 3,
        compiler_params=SMALL,
        name="finish",
    )(dkv_own, dq_same, dq_pair, from_sibling)


def solution(mesh):
    row_count, columns = mesh.devices.shape
    cores = 2
    chips = columns // cores
    fine = Mesh(mesh.devices.reshape(row_count, chips, cores), ("row", "chip", "core"))
    col = ("chip", "core")
    in_specs = (
        P("row", col, None),
        P(col, "row", None),
        P(col, "row", None),
        P("row", col, None),
        P("row", col, None),
        P("row", None, None),
        P("row", col, None),
        P("row", col),
        P("row", col, None, None, None),
    )
    out_specs = (P("row", col, None), P(col, "row", None), P(col, "row", None))
    return jax.shard_map(
        functools.partial(body, (row_count, chips, cores)),
        mesh=fine, in_specs=in_specs, out_specs=out_specs, check_vma=False,
    )
```

```python
import functools

import jax
import jax.numpy as jnp
from jax import lax
from jax.experimental import pallas as pl
from jax.experimental.pallas import tpu as pltpu
from jax.sharding import Mesh
from jax.sharding import PartitionSpec as P


F32 = jnp.float32
BF16 = jnp.bfloat16
I32 = jnp.int32
LANES = 128
PAD = 16
QUARTERS = 4
TOGETHER = 4
NT = (((1,), (1,)), ((), ()))
NN = (((1,), (0,)), ((), ()))
MEDIUM = pltpu.CompilerParams(vmem_limit_bytes=28 * 1024 * 1024)
PACK = pltpu.CompilerParams(vmem_limit_bytes=int(53.4 * 1024 * 1024))
SMALL = pltpu.CompilerParams(vmem_limit_bytes=12 * 1024 * 1024)
def early(gigaflops):
    return pl.CostEstimate(flops=gigaflops * 10**9, bytes_accessed=0, transcendentals=0)


VMEM = pl.BlockSpec(memory_space=pltpu.VMEM)
HBM = pl.BlockSpec(memory_space=pltpu.HBM)


def lanes_of(quarter):
    return pl.ds(pl.multiple_of(quarter * LANES, LANES), LANES)


def my_place():
    row, chip, core = (lax.axis_index(name) for name in ("row", "chip", "core"))
    return row, chip, core, row % 2 * 2 + core


def pack_kernel(
    heads, q_hbm, g_hbm, o_hbm, k_hbm, v_hbm, bits_hbm, slot_ref, live_ref,
    qg_own, qg_pair0, qg_pair1, kv_own, sib_ref, packed_ref,
    q_ref, g_ref, o_ref, k_ref, v_ref, bits_ref, delta_ref, sems,
):
    arrays = (
        (q_hbm, q_ref), (g_hbm, g_ref), (o_hbm, o_ref),
        (k_hbm, k_ref), (v_hbm, v_ref), (bits_hbm, bits_ref),
    )
    copies = [pltpu.make_async_copy(a, b, sems.at[i]) for i, (a, b) in enumerate(arrays)]
    for copy in copies:
        copy.start()
    rows, width = q_ref.shape[1:]
    krows = k_ref.shape[1]
    head_dim = width // heads
    local = heads // QUARTERS
    capacity = bits_ref.shape[2]
    quarter = my_place()[3]
    feature = lax.broadcasted_iota(I32, (QUARTERS * PAD, width), 1)
    line = lax.broadcasted_iota(I32, (QUARTERS * PAD, width), 0)
    wanted = jnp.where(line % PAD < local, line // PAD * local + line % PAD, -1)
    pick = (feature // head_dim == wanted).astype(F32)
    packed_ref[capacity // 2] = jnp.zeros((8, LANES), I32)
    packed_ref[capacity // 2, 0:1, 0:capacity] = slot_ref[0]
    packed_ref[capacity // 2, 1:2, 0:1] = live_ref[...]
    for copy in copies:
        copy.wait()
    product = g_ref[0].astype(F32) * o_ref[0].astype(F32)
    delta = lax.dot_general(
        pick, product, NT, precision=lax.Precision.HIGHEST, preferred_element_type=F32
    ).astype(BF16)
    for index in range(QUARTERS):
        delta_ref[index] = delta[index * PAD : (index + 1) * PAD]
    base = 4 * krows
    for step, (ref, start) in enumerate(
        ((qg_own, 0), (sib_ref, base), (qg_pair0, 0), (qg_pair1, 0))
    ):
        lanes = lanes_of(quarter ^ step)
        ref[start : start + rows] = q_ref[0, :, lanes]
        ref[start + rows : start + 2 * rows] = g_ref[0, :, lanes]
        if rows < LANES:
            ref[start + 2 * rows : start + 2 * rows + PAD] = jnp.zeros((PAD, LANES), BF16)
        ref[start + 2 * rows : start + 2 * rows + PAD, :rows] = delta_ref[quarter ^ step]
    for side in range(2):
        for ref, step in ((kv_own, 2 * side), (sib_ref, 2 * side + 1)):
            lanes = lanes_of(quarter ^ step)
            start = side * 2 * krows
            ref[start : start + krows] = k_ref[0, :, lanes]
            ref[start + krows : start + 2 * krows] = v_ref[0, :, lanes]
    for entry in range(capacity):
        words = bits_ref[0, 0, entry]
        span = slice(entry % 2 * 4, entry % 2 * 4 + 4)
        packed_ref[entry // 2, span] = words[:4] | lax.shift_left(words[4:], I32(16))


def key_join_kernel(krows, kv_own, sib_ref, kv_same, kv_pair):
    core = my_place()[2]
    for side, ref in enumerate((kv_same, kv_pair)):
        span = slice(side * 2 * krows, (side + 1) * 2 * krows)
        ref[core] = kv_own[span]
        ref[1 - core] = sib_ref[span]


def query_join_kernel(
    krows, tile, qg_own, sib_ref, qg_pair0, qg_pair1, bits_own, bits_pair, lse_own, lse_pair,
    qg_out, bits_out, lse_out,
):
    row, chip, core, quarter = my_place()
    side = row % 2
    qg_out[quarter] = qg_own[...]
    qg_out[quarter ^ 1] = sib_ref[4 * krows :]
    qg_out[quarter ^ 2] = qg_pair0[...]
    qg_out[quarter ^ 3] = qg_pair1[...]
    bits_out[side] = bits_own[...]
    bits_out[1 - side] = bits_pair[...]
    for step, ref in enumerate((lse_own, lse_pair)):
        every = ref[0]
        own = every[:2]
        for index in range(1, QUARTERS):
            own = jnp.where(quarter == index, every[2 * index : 2 * index + 2], own)
        for u in range(lse_out.shape[1]):
            lse_out[side ^ step, u] = own[:, u * tile : (u + 1) * tile]


def key_place_kernel(head_dim, tile, *refs):
    kv_refs, (k_out, v_out, k2t_out) = refs[:-3], refs[-3:]
    krows = kv_refs[0].shape[1] // 2
    row = my_place()[0]
    for step, ref in enumerate(kv_refs):
        start = (row ^ step) * krows
        inner = pl.multiple_of(start % tile, krows)
        for block in range(2):
            k_out[block, start // tile, pl.ds(inner, krows)] = ref[block, :krows]
            v_out[block, start // tile, pl.ds(inner, krows)] = ref[block, krows:]
    low_row = lax.broadcasted_iota(I32, (LANES, tile), 0) < head_dim
    none_t = jnp.zeros((LANES, tile), BF16)
    for block in range(2):
        for w in range(k_out.shape[1]):
            flipped = k_out[block, w].T
            k2t_out[block, w] = jnp.concatenate(
                [jnp.where(low_row, flipped, none_t), jnp.where(low_row, none_t, flipped)], axis=1
            )


def pair_kernel(sizes, *refs):
    head_dim, tile, capacity, chips, row_count = sizes
    qg_refs, refs = refs[:chips], refs[chips:]
    (k_scr, v_scr, k2t_scr), refs = refs[:3], refs[3:]
    bits_refs, lse_ref, refs = refs[:2], refs[2], refs[3:]
    dqt_ref, dkv_refs, refs = refs[0], refs[1 : 1 + row_count], refs[1 + row_count :]
    q2_scr, g2_scr, delta_scr, dqt_scr, dk_scr, dv_scr, bits_scr, info, todo, sems = refs
    rows = (qg_refs[0].shape[1] - PAD) // 2
    krows = dkv_refs[0].shape[1] // 2
    query_tiles = q2_scr.shape[1]
    key_tiles = k_scr.shape[1]
    scaling = float(head_dim) ** -0.5
    row, chip, core, quarter = my_place()
    side = row % 2

    copies = [
        pltpu.make_async_copy(
            bits_refs[i % 2].at[i // 2, capacity // 2], info.at[i], sems.at[i]
        )
        for i in range(QUARTERS)
    ]
    for copy in copies:
        copy.start()

    low = lax.broadcasted_iota(I32, (rows, LANES), 1) < head_dim
    none = jnp.zeros((rows, LANES), BF16)
    for step in range(chips):
        for index in range(QUARTERS):
            source = (chip ^ step) * 2 + index % 2
            start = source * rows
            u = start // tile
            inner = pl.multiple_of(start % tile, rows)
            block = index // 2
            for scr, part in ((q2_scr, 0), (g2_scr, 1)):
                piece = qg_refs[step][index, part * rows : (part + 1) * rows]
                if part == 0:
                    piece = (piece.astype(F32) * scaling).astype(BF16)
                scr[block, u, 0, pl.ds(inner, rows)] = jnp.where(low, piece, none)
                scr[block, u, 1, pl.ds(inner, rows)] = jnp.where(low, none, piece)
            delta = qg_refs[step][index, 2 * rows :, :rows].astype(F32)
            if rows == tile:
                delta_scr[block, u] = delta
            else:
                for part in range(tile // rows):
                    @pl.when(source % (tile // rows) == part)
                    def _(part=part, delta=delta, u=u, block=block):
                        delta_scr[block, u, :, part * rows : (part + 1) * rows] = delta
    dqt_scr[...] = jnp.zeros_like(dqt_scr)
    dk_scr[...] = jnp.zeros_like(dk_scr)
    dv_scr[...] = jnp.zeros_like(dv_scr)
    place_in = lax.broadcasted_iota(I32, (2, 4, 16, tile), 2)
    upper = lax.broadcasted_iota(I32, (2, 4, 16, tile), 0)
    bit = lax.shift_left(I32(1), place_in + 16 * upper).reshape(tile, tile)
    for step in range(QUARTERS):
        for entry in range(capacity):
            span = slice(entry % 2 * 4, entry % 2 * 4 + 4)
            bits_scr[step, entry] = bits_refs[step % 2][side ^ (step // 2), entry // 2, span]
    for i, copy in enumerate(copies):
        copy.wait()
    count = I32(0)
    for i in range(QUARTERS):
        step = (side ^ (i // 2)) * 2 + i % 2

        def listed(entry, count, i=i, step=step):
            todo[count] = info[i, 0, entry] + 32 * entry + 1024 * step
            return count + 1

        count = lax.fori_loop(0, info[i, 1, 0], listed, count)

    def some_tiles(index, _):
        work = []
        for part in range(TOGETHER):
            position = index * TOGETHER + part
            item = todo[jnp.minimum(position, count - 1)]
            slot = item % 32
            step = item // 1024
            qb = side ^ (step // 2)
            kb = core ^ (step % 2)
            u = slot // key_tiles
            w = slot % key_tiles
            words = bits_scr[step, item // 32 % 32]
            if part:
                words = words & jnp.where(position < count, I32(-1), I32(0))
            words = jnp.broadcast_to(words[:, None, :], (4, 16, tile)).reshape(64, tile)
            edge = (jnp.concatenate([words, words], axis=0) & bit) != 0
            q2 = q2_scr[qb, u].reshape(2 * tile, LANES)
            g2 = g2_scr[qb, u].reshape(2 * tile, LANES)
            scores = lax.dot_general(k_scr[kb, w], q2, NT, preferred_element_type=F32)
            grad_prob = lax.dot_general(v_scr[kb, w], g2, NT, preferred_element_type=F32)
            work.append((qb, kb, u, w, edge, q2, g2, scores, grad_prob))
        done = []
        for qb, kb, u, w, edge, q2, g2, scores, grad_prob in work:
            lse_tile = lse_ref[qb, u]
            delta_tile = delta_scr[qb, u]
            probs, grads = [], []
            for h in range(2):
                s = scores[:, h * tile : (h + 1) * tile]
                gp = grad_prob[:, h * tile : (h + 1) * tile]
                p = jnp.where(edge, jnp.exp(s - lse_tile[h : h + 1]), 0.0)
                ds = p * (gp - delta_tile[h : h + 1])
                probs.append(p.astype(BF16))
                grads.append(ds.astype(BF16))
            done.append((
                lax.dot_general(
                    jnp.concatenate(probs, axis=1), g2, NN, preferred_element_type=F32
                ),
                lax.dot_general(
                    jnp.concatenate(grads, axis=1), q2, NN, preferred_element_type=F32
                ),
                lax.dot_general(
                    k2t_scr[kb, w], jnp.concatenate(grads, axis=0), NN,
                    preferred_element_type=F32,
                ),
            ))
        for (qb, kb, u, w, *_), (dv, dk, dqt) in zip(work, done):
            dv_scr[kb, w] += dv
            dk_scr[kb, w] += dk
            dqt_scr[qb, u] += dqt
        return 0

    lax.fori_loop(0, (count + TOGETHER - 1) // TOGETHER, some_tiles, 0)

    for step in range(row_count):
        start = (row ^ step) * krows
        inner = pl.multiple_of(start % tile, krows)
        for block in range(2):
            dk = dk_scr[block, start // tile, pl.ds(inner, krows)]
            dv = dv_scr[block, start // tile, pl.ds(inner, krows)]
            dkv_refs[step][block, :krows] = dk.astype(BF16)
            dkv_refs[step][block, krows:] = dv.astype(BF16)
    dqt_ref[...] = (dqt_scr[...] * scaling).astype(BF16)


def turn_kernel(rows, dqt_ref, *refs):
    dq_refs, dq_scr = refs[:-1], refs[-1]
    tile = dqt_ref.shape[3]
    chip = my_place()[1]
    for block in range(2):
        for u in range(dqt_ref.shape[1]):
            dq_scr[block, u * tile : (u + 1) * tile] = dqt_ref[block, u].T
    for step, ref in enumerate(dq_refs):
        for index in range(QUARTERS):
            start = pl.multiple_of(((chip ^ step) * 2 + index % 2) * rows, rows)
            ref[index] = dq_scr[index // 2, pl.ds(start, rows)]


def query_sum_kernel(chips, *refs):
    parts, (same_ref, pair_ref) = refs[:chips], refs[chips:]
    side = my_place()[0] % 2
    for step, ref in enumerate((same_ref, pair_ref)):
        for core in range(2):
            index = (side ^ step) * 2 + core
            total = parts[0][index].astype(F32)
            for part in parts[1:]:
                total += part[index].astype(F32)
            ref[core] = total.astype(BF16)


def key_sum_kernel(row_count, *refs):
    dkv_refs, (own_ref, sib_ref) = refs[:-2], refs[-2:]
    core = my_place()[2]
    for ref, block in ((own_ref, core), (sib_ref, 1 - core)):
        for side in range(2):
            total = dkv_refs[side][block].astype(F32)
            for other in range(side + 2, row_count, 2):
                total += dkv_refs[other][block].astype(F32)
            ref[side] = total.astype(BF16)


def bundle_kernel(dkv_ref, dq_same, dq_pair, out):
    krows2 = dkv_ref.shape[1]
    sibling = 1 - my_place()[2]
    out[:, :krows2] = dkv_ref[...]
    for side, dq in enumerate((dq_same, dq_pair)):
        out[side, krows2:] = dq[sibling]


def finish_kernel(krows, dkv_own, dq_same, dq_pair, sib_ref, dq_out, dk_out, dv_out):
    row, chip, core, quarter = my_place()
    for side, dq in enumerate((dq_same, dq_pair)):
        for step, ref in enumerate((dkv_own, sib_ref)):
            lanes = lanes_of(quarter ^ (2 * side + step))
            dk_out[0, :, lanes] = ref[side, :krows]
            dv_out[0, :, lanes] = ref[side, krows : 2 * krows]
            dq_out[0, :, lanes] = ref[side, 2 * krows :] if step else dq[core]


def send(block, axes, count, step):
    return lax.ppermute(block, axes, [(place, place ^ step) for place in range(count)])


def body(sizes, queries, keys, values, outputs, grad_out, lse, tile_slot, tile_live, tile_bits):
    row_count, chips, cores = sizes
    heads = lse.shape[1]
    width = queries.shape[2]
    head_dim = width // heads
    tile = tile_bits.shape[4]
    capacity = tile_slot.shape[2]
    rows = queries.shape[1]
    krows = keys.shape[1]
    query_tiles = lse.shape[2] // tile
    key_tiles = row_count * krows // tile
    line = ("row", "core")
    places = row_count * cores

    def shape(*dims, dtype=BF16):
        return jax.ShapeDtypeStruct(dims, dtype)

    qg_shape = shape(2 * rows + PAD, LANES)
    kv_shape = shape(2, 2 * krows, LANES)
    qg_own, qg_pair0, qg_pair1, kv_own, to_sibling, bits_own = pl.pallas_call(
        functools.partial(pack_kernel, heads),
        out_shape=(
            qg_shape, qg_shape, qg_shape, shape(4 * krows, LANES),
            shape(4 * krows + 2 * rows + PAD, LANES),
            shape(capacity // 2 + 1, 8, LANES, dtype=I32),
        ),
        in_specs=[HBM] * 6 + [VMEM] * 2,
        out_specs=(VMEM,) * 6,
        scratch_shapes=[
            pltpu.VMEM(queries.shape, BF16),
            pltpu.VMEM(queries.shape, BF16),
            pltpu.VMEM(queries.shape, BF16),
            pltpu.VMEM(keys.shape, BF16),
            pltpu.VMEM(keys.shape, BF16),
            pltpu.VMEM(tile_bits.shape, I32),
            pltpu.VMEM((QUARTERS, PAD, rows), BF16),
            pltpu.SemaphoreType.DMA((6,)),
        ],
        compiler_params=PACK,
        name="pack",
    )(queries, grad_out, outputs, keys, values, tile_bits, tile_slot, tile_live)

    qg_pair0 = send(qg_pair0, line, places, 2)
    qg_pair1 = send(qg_pair1, line, places, 3)
    from_sibling = send(to_sibling, "core", cores, 1)
    bits_pair = send(bits_own, "row", row_count, 1)
    lse_pair = send(lse, "row", row_count, 1)
    kv_same, kv_pair = pl.pallas_call(
        functools.partial(key_join_kernel, krows),
        out_shape=(kv_shape, kv_shape),
        in_specs=[VMEM] * 2,
        out_specs=(VMEM,) * 2,
        compiler_params=SMALL,
        name="key_join",
    )(kv_own, from_sibling)
    kv_out = (kv_same, kv_pair)
    kv = [kv_same] + [
        send(kv_out[step % 2], "row", row_count, step) for step in range(1, row_count)
    ]
    qg, bits, lse2 = pl.pallas_call(
        functools.partial(query_join_kernel, krows, tile),
        out_shape=(
            shape(QUARTERS, 2 * rows + PAD, LANES),
            shape(2, capacity // 2 + 1, 8, LANES, dtype=I32),
            shape(2, query_tiles, 2, tile, dtype=F32),
        ),
        in_specs=[VMEM] * 8,
        out_specs=(VMEM,) * 3,
        compiler_params=SMALL,
        cost_estimate=early(20),
        name="query_join",
    )(qg_own, from_sibling, qg_pair0, qg_pair1, bits_own, bits_pair, lse, lse_pair)
    qg = [qg] + [send(qg, "chip", chips, step) for step in range(1, chips)]
    bits_sibling = send(bits, "core", cores, 1)

    placed = pl.pallas_call(
        functools.partial(key_place_kernel, head_dim, tile),
        out_shape=(
            shape(2, key_tiles, tile, LANES), shape(2, key_tiles, tile, LANES),
            shape(2, key_tiles, LANES, 2 * tile),
        ),
        in_specs=[VMEM] * row_count,
        out_specs=(VMEM,) * 3,
        compiler_params=SMALL,
        cost_estimate=early(20),
        name="key_place",
    )(*kv)
    parts = pl.pallas_call(
        functools.partial(pair_kernel, (head_dim, tile, capacity, chips, row_count)),
        out_shape=(shape(2, query_tiles, LANES, tile),) + (kv_shape,) * row_count,
        in_specs=[VMEM] * (chips + 6),
        out_specs=(VMEM,) * (1 + row_count),
        scratch_shapes=[
            pltpu.VMEM((2, query_tiles, 2, tile, LANES), BF16),
            pltpu.VMEM((2, query_tiles, 2, tile, LANES), BF16),
            pltpu.VMEM((2, query_tiles, PAD, tile), F32),
            pltpu.VMEM((2, query_tiles, LANES, tile), F32),
            pltpu.VMEM((2, key_tiles, tile, LANES), F32),
            pltpu.VMEM((2, key_tiles, tile, LANES), F32),
            pltpu.VMEM((QUARTERS, capacity, 4, LANES), I32),
            pltpu.SMEM((QUARTERS, 8, LANES), I32),
            pltpu.SMEM((QUARTERS * capacity,), I32),
            pltpu.SemaphoreType.DMA((QUARTERS,)),
        ],
        compiler_params=MEDIUM,
        name="pair",
    )(*qg, *placed, bits, bits_sibling, lse2)

    dkv = parts[1:]
    dq = pl.pallas_call(
        functools.partial(turn_kernel, rows),
        out_shape=(shape(QUARTERS, rows, LANES),) * chips,
        in_specs=[VMEM],
        out_specs=(VMEM,) * chips,
        scratch_shapes=[pltpu.VMEM((2, query_tiles * tile, LANES), BF16)],
        compiler_params=SMALL,
        name="turn",
    )(parts[0])
    dq = [dq[0]] + [send(dq[step], "chip", chips, step) for step in range(1, chips)]
    dkv = [dkv[0]] + [send(dkv[step], "row", row_count, step) for step in range(1, row_count)]
    dq_same, dq_pair = pl.pallas_call(
        functools.partial(query_sum_kernel, chips),
        out_shape=(shape(2, rows, LANES),) * 2,
        in_specs=[VMEM] * chips,
        out_specs=(VMEM,) * 2,
        compiler_params=SMALL,
        name="query_sum",
    )(*dq)
    dq_pair = send(dq_pair, "row", row_count, 1)
    dkv_own, dkv_sibling = pl.pallas_call(
        functools.partial(key_sum_kernel, row_count),
        out_shape=(kv_shape,) * 2,
        in_specs=[VMEM] * row_count,
        out_specs=(VMEM,) * 2,
        compiler_params=SMALL,
        cost_estimate=early(20),
        name="key_sum",
    )(*dkv)
    to_sibling = pl.pallas_call(
        bundle_kernel,
        out_shape=shape(2, 2 * krows + rows, LANES),
        in_specs=[VMEM] * 3,
        out_specs=VMEM,
        compiler_params=SMALL,
        name="bundle",
    )(dkv_sibling, dq_same, dq_pair)
    from_sibling = send(to_sibling, "core", cores, 1)
    return pl.pallas_call(
        functools.partial(finish_kernel, krows),
        out_shape=(shape(1, rows, width), shape(1, krows, width), shape(1, krows, width)),
        in_specs=[VMEM] * 4,
        out_specs=(VMEM,) * 3,
        compiler_params=SMALL,
        name="finish",
    )(dkv_own, dq_same, dq_pair, from_sibling)


def solution(mesh):
    row_count, columns = mesh.devices.shape
    cores = 2
    chips = columns // cores
    fine = Mesh(mesh.devices.reshape(row_count, chips, cores), ("row", "chip", "core"))
    col = ("chip", "core")
    in_specs = (
        P("row", col, None),
        P(col, "row", None),
        P(col, "row", None),
        P("row", col, None),
        P("row", col, None),
        P("row", None, None),
        P("row", col, None),
        P("row", col),
        P("row", col, None, None, None),
    )
    out_specs = (P("row", col, None), P(col, "row", None), P(col, "row", None))
    return jax.shard_map(
        functools.partial(body, (row_count, chips, cores)),
        mesh=fine, in_specs=in_specs, out_specs=out_specs, check_vma=False,
    )
```

```python
import functools

import jax
import jax.numpy as jnp
from jax import lax
from jax.experimental import pallas as pl
from jax.experimental.pallas import tpu as pltpu
from jax.sharding import Mesh
from jax.sharding import PartitionSpec as P


F32 = jnp.float32
BF16 = jnp.bfloat16
I32 = jnp.int32
LANES = 128
PAD = 16
QUARTERS = 4
TOGETHER = 8
LSE_UNIT = 2.0**21
NT = (((1,), (1,)), ((), ()))
NN = (((1,), (0,)), ((), ()))
MEDIUM = pltpu.CompilerParams(vmem_limit_bytes=28 * 1024 * 1024)
PACK = pltpu.CompilerParams(vmem_limit_bytes=int(53.6 * 1024 * 1024))
SMALL = pltpu.CompilerParams(vmem_limit_bytes=12 * 1024 * 1024)
def early(gigaflops):
    return pl.CostEstimate(flops=gigaflops * 10**9, bytes_accessed=0, transcendentals=0)


VMEM = pl.BlockSpec(memory_space=pltpu.VMEM)
HBM = pl.BlockSpec(memory_space=pltpu.HBM)


def lanes_of(quarter):
    return pl.ds(pl.multiple_of(quarter * LANES, LANES), LANES)


def my_place():
    row, chip, core = (lax.axis_index(name) for name in ("row", "chip", "core"))
    return row, chip, core, row % 2 * 2 + core


def pack_kernel(
    heads, q_hbm, g_hbm, o_hbm, k_hbm, v_hbm, bits_hbm, lse_hbm, slot_ref, live_ref,
    qg_own, pair0_ref, pair1_ref, kv_own, sib_ref, packed_ref, lse_own,
    q_ref, g_ref, o_ref, k_ref, v_ref, bits_ref, lse_ref, delta_ref, sems,
):
    arrays = (
        (q_hbm, q_ref), (g_hbm, g_ref), (o_hbm, o_ref), (k_hbm, k_ref),
        (v_hbm, v_ref), (bits_hbm, bits_ref), (lse_hbm, lse_ref),
    )
    copies = [pltpu.make_async_copy(a, b, sems.at[i]) for i, (a, b) in enumerate(arrays)]
    for copy in copies:
        copy.start()
    rows, width = q_ref.shape[1:]
    krows = k_ref.shape[1]
    head_dim = width // heads
    local = heads // QUARTERS
    capacity = bits_ref.shape[2]
    quarter = my_place()[3]
    feature = lax.broadcasted_iota(I32, (QUARTERS * PAD, width), 1)
    line = lax.broadcasted_iota(I32, (QUARTERS * PAD, width), 0)
    wanted = jnp.where(line % PAD < local, line // PAD * local + line % PAD, -1)
    pick = (feature // head_dim == wanted).astype(F32)
    packed_ref[capacity // 2] = jnp.zeros((8, LANES), I32)
    packed_ref[capacity // 2, 0:1, 0:capacity] = slot_ref[0]
    packed_ref[capacity // 2, 1:2, 0:1] = live_ref[...]
    for copy in copies:
        copy.wait()
    product = g_ref[0].astype(F32) * o_ref[0].astype(F32)
    delta = lax.dot_general(
        pick, product, NT, precision=lax.Precision.HIGHEST, preferred_element_type=F32
    ).astype(BF16)
    for index in range(QUARTERS):
        delta_ref[index] = delta[index * PAD : (index + 1) * PAD]
    for step, (ref, start) in enumerate(
        ((qg_own, 0), (sib_ref, 4 * krows), (pair0_ref, 0), (pair1_ref, 0))
    ):
        lanes = lanes_of(quarter ^ step)
        ref[start : start + rows] = q_ref[0, :, lanes]
        ref[start + rows : start + 2 * rows] = g_ref[0, :, lanes]
        if rows < LANES:
            ref[start + 2 * rows : start + 2 * rows + PAD] = jnp.zeros((PAD, LANES), BF16)
        ref[start + 2 * rows : start + 2 * rows + PAD, :rows] = delta_ref[quarter ^ step]
    for step in range(QUARTERS):
        ref = (kv_own, sib_ref)[step % 2]
        lanes = lanes_of(quarter ^ step)
        start = step // 2 * 2 * krows
        ref[start : start + krows] = k_ref[0, :, lanes]
        ref[start + krows : start + 2 * krows] = v_ref[0, :, lanes]
    every = lse_ref[0]

    def lse_of(wanted_quarter):
        own = every[:local]
        for index in range(1, QUARTERS):
            own = jnp.where(
                wanted_quarter == index, every[local * index : local * (index + 1)], own
            )
        return own

    mine = lse_of(quarter)
    other = (lse_of(quarter ^ 2) * LSE_UNIT).astype(I32)
    for u in range(lse_own.shape[0]):
        lanes = slice(u * LANES, (u + 1) * LANES)
        lse_own[u] = mine[:, lanes]
        packed_ref[capacity // 2 + 1 + u // 4, u % 4 * 2 : u % 4 * 2 + 2] = other[:, lanes]
    for entry in range(capacity):
        words = bits_ref[0, 0, entry]
        span = slice(entry % 2 * 4, entry % 2 * 4 + 4)
        packed_ref[entry // 2, span] = words[:4] | lax.shift_left(words[4:], I32(16))


def key_join_kernel(krows, kv_own, sib_ref, kv_same, kv_pair):
    core = my_place()[2]
    for side, ref in enumerate((kv_same, kv_pair)):
        span = slice(side * 2 * krows, (side + 1) * 2 * krows)
        ref[core] = kv_own[span]
        ref[1 - core] = sib_ref[span]


def query_join_kernel(
    krows, slabs, qg_own, sib_ref, pair0_ref, pair1_ref, bits_own, bits_pair, lse_own,
    qg_out, bits_out, lse_out,
):
    row, chip, core, quarter = my_place()
    side = row % 2
    qg_out[quarter] = qg_own[...]
    qg_out[quarter ^ 1] = sib_ref[4 * krows :]
    qg_out[quarter ^ 2] = pair0_ref[...]
    qg_out[quarter ^ 3] = pair1_ref[...]
    bits_out[side] = bits_own[:slabs]
    bits_out[1 - side] = bits_pair[:slabs]
    lse_out[side] = lse_own[...]
    for u in range(lse_out.shape[1]):
        fixed = bits_pair[slabs + u // 4, u % 4 * 2 : u % 4 * 2 + 2]
        lse_out[1 - side, u] = fixed.astype(F32) * (1.0 / LSE_UNIT)


def key_place_kernel(head_dim, tile, *refs):
    kv_refs, (k_out, v_out, k2t_out) = refs[:-3], refs[-3:]
    krows = kv_refs[0].shape[1] // 2
    row = my_place()[0]
    for step, ref in enumerate(kv_refs):
        start = (row ^ step) * krows
        inner = pl.multiple_of(start % tile, krows)
        for block in range(2):
            k_out[block, start // tile, pl.ds(inner, krows)] = ref[block, :krows]
            v_out[block, start // tile, pl.ds(inner, krows)] = ref[block, krows:]
    low_row = lax.broadcasted_iota(I32, (LANES, tile), 0) < head_dim
    none_t = jnp.zeros((LANES, tile), BF16)
    for block in range(2):
        for w in range(k_out.shape[1]):
            flipped = k_out[block, w].T
            k2t_out[block, w] = jnp.concatenate(
                [jnp.where(low_row, flipped, none_t), jnp.where(low_row, none_t, flipped)], axis=1
            )


def pair_kernel(sizes, *refs):
    head_dim, tile, capacity, chips, row_count = sizes
    qg_refs, refs = refs[:chips], refs[chips:]
    (k_scr, v_scr, k2t_scr), refs = refs[:3], refs[3:]
    bits_refs, lse_ref, refs = refs[:2], refs[2], refs[3:]
    dqt_ref, dkv_refs, refs = refs[0], refs[1 : 1 + row_count], refs[1 + row_count :]
    q2_scr, g2_scr, delta_scr, dqt_scr, dk_scr, dv_scr, bits_scr, info, todo, sems = refs
    rows = (qg_refs[0].shape[1] - PAD) // 2
    krows = dkv_refs[0].shape[1] // 2
    query_tiles = q2_scr.shape[1]
    key_tiles = k_scr.shape[1]
    scaling = float(head_dim) ** -0.5
    row, chip, core, quarter = my_place()
    side = row % 2

    copies = [
        pltpu.make_async_copy(
            bits_refs[i % 2].at[i // 2, capacity // 2], info.at[i], sems.at[i]
        )
        for i in range(QUARTERS)
    ]
    for copy in copies:
        copy.start()

    low = lax.broadcasted_iota(I32, (rows, LANES), 1) < head_dim
    none = jnp.zeros((rows, LANES), BF16)
    for step in range(chips):
        for index in range(QUARTERS):
            source = (chip ^ step) * 2 + index % 2
            start = source * rows
            u = start // tile
            inner = pl.multiple_of(start % tile, rows)
            block = index // 2
            for scr, part in ((q2_scr, 0), (g2_scr, 1)):
                piece = qg_refs[step][index, part * rows : (part + 1) * rows]
                if part == 0:
                    piece = (piece.astype(F32) * scaling).astype(BF16)
                scr[block, u, 0, pl.ds(inner, rows)] = jnp.where(low, piece, none)
                scr[block, u, 1, pl.ds(inner, rows)] = jnp.where(low, none, piece)
            delta = qg_refs[step][index, 2 * rows :, :rows].astype(F32)
            if rows == tile:
                delta_scr[block, u] = delta
            else:
                for part in range(tile // rows):
                    @pl.when(source % (tile // rows) == part)
                    def _(part=part, delta=delta, u=u, block=block):
                        delta_scr[block, u, :, part * rows : (part + 1) * rows] = delta
    dqt_scr[...] = jnp.zeros_like(dqt_scr)
    dk_scr[...] = jnp.zeros_like(dk_scr)
    dv_scr[...] = jnp.zeros_like(dv_scr)
    place_in = lax.broadcasted_iota(I32, (2, 4, 16, tile), 2)
    upper = lax.broadcasted_iota(I32, (2, 4, 16, tile), 0)
    bit = lax.shift_left(I32(1), place_in + 16 * upper).reshape(tile, tile)
    for step in range(QUARTERS):
        for entry in range(capacity):
            span = slice(entry % 2 * 4, entry % 2 * 4 + 4)
            bits_scr[step, entry] = bits_refs[step % 2][side ^ (step // 2), entry // 2, span]
    for i, copy in enumerate(copies):
        copy.wait()
    count = I32(0)
    for i in range(QUARTERS):
        step = (side ^ (i // 2)) * 2 + i % 2

        def listed(entry, count, i=i, step=step):
            todo[count] = info[i, 0, entry] + 32 * entry + 1024 * step
            return count + 1

        count = lax.fori_loop(0, info[i, 1, 0], listed, count)

    def some_tiles(index, _):
        work = []
        for part in range(TOGETHER):
            position = index * TOGETHER + part
            item = todo[jnp.minimum(position, count - 1)]
            slot = item % 32
            step = item // 1024
            qb = side ^ (step // 2)
            kb = core ^ (step % 2)
            u = slot // key_tiles
            w = slot % key_tiles
            words = bits_scr[step, item // 32 % 32]
            if part:
                words = words & jnp.where(position < count, I32(-1), I32(0))
            words = jnp.broadcast_to(words[:, None, :], (4, 16, tile)).reshape(64, tile)
            edge = (jnp.concatenate([words, words], axis=0) & bit) != 0
            q2 = q2_scr[qb, u].reshape(2 * tile, LANES)
            g2 = g2_scr[qb, u].reshape(2 * tile, LANES)
            scores = lax.dot_general(k_scr[kb, w], q2, NT, preferred_element_type=F32)
            grad_prob = lax.dot_general(v_scr[kb, w], g2, NT, preferred_element_type=F32)
            work.append((qb, kb, u, w, edge, q2, g2, scores, grad_prob))
        done = []
        for qb, kb, u, w, edge, q2, g2, scores, grad_prob in work:
            lse_tile = lse_ref[qb, u]
            delta_tile = delta_scr[qb, u]
            probs, grads = [], []
            for h in range(2):
                s = scores[:, h * tile : (h + 1) * tile]
                gp = grad_prob[:, h * tile : (h + 1) * tile]
                p = jnp.where(edge, jnp.exp(s - lse_tile[h : h + 1]), 0.0)
                ds = p * (gp - delta_tile[h : h + 1])
                probs.append(p.astype(BF16))
                grads.append(ds.astype(BF16))
            done.append((
                lax.dot_general(
                    jnp.concatenate(probs, axis=1), g2, NN, preferred_element_type=F32
                ),
                lax.dot_general(
                    jnp.concatenate(grads, axis=1), q2, NN, preferred_element_type=F32
                ),
                lax.dot_general(
                    k2t_scr[kb, w], jnp.concatenate(grads, axis=0), NN,
                    preferred_element_type=F32,
                ),
            ))
        for (qb, kb, u, w, *_), (dv, dk, dqt) in zip(work, done):
            dv_scr[kb, w] += dv
            dk_scr[kb, w] += dk
            dqt_scr[qb, u] += dqt
        return 0

    lax.fori_loop(0, (count + TOGETHER - 1) // TOGETHER, some_tiles, 0)

    for step in range(row_count):
        start = (row ^ step) * krows
        inner = pl.multiple_of(start % tile, krows)
        for block in range(2):
            dk = dk_scr[block, start // tile, pl.ds(inner, krows)]
            dv = dv_scr[block, start // tile, pl.ds(inner, krows)]
            dkv_refs[step][block, :krows] = dk.astype(BF16)
            dkv_refs[step][block, krows:] = dv.astype(BF16)
    dqt_ref[...] = (dqt_scr[...] * scaling).astype(BF16)


def turn_kernel(rows, dqt_ref, *refs):
    dq_refs, dq_scr = refs[:-1], refs[-1]
    tile = dqt_ref.shape[3]
    chip = my_place()[1]
    for block in range(2):
        for u in range(dqt_ref.shape[1]):
            dq_scr[block, u * tile : (u + 1) * tile] = dqt_ref[block, u].T
    for step, ref in enumerate(dq_refs):
        for index in range(QUARTERS):
            start = pl.multiple_of(((chip ^ step) * 2 + index % 2) * rows, rows)
            ref[index] = dq_scr[index // 2, pl.ds(start, rows)]


def query_sum_kernel(chips, *refs):
    parts, (same_ref, pair_ref) = refs[:chips], refs[chips:]
    side = my_place()[0] % 2
    for step, ref in enumerate((same_ref, pair_ref)):
        for core in range(2):
            index = (side ^ step) * 2 + core
            total = parts[0][index].astype(F32)
            for part in parts[1:]:
                total += part[index].astype(F32)
            ref[core] = total.astype(BF16)


def key_sum_kernel(row_count, *refs):
    dkv_refs, (own_ref, sib_ref) = refs[:-2], refs[-2:]
    core = my_place()[2]
    for ref, block in ((own_ref, core), (sib_ref, 1 - core)):
        for side in range(2):
            total = dkv_refs[side][block].astype(F32)
            for other in range(side + 2, row_count, 2):
                total += dkv_refs[other][block].astype(F32)
            ref[side] = total.astype(BF16)


def bundle_kernel(dkv_ref, dq_same, dq_pair, out):
    krows2 = dkv_ref.shape[1]
    sibling = 1 - my_place()[2]
    out[:, :krows2] = dkv_ref[...]
    for side, dq in enumerate((dq_same, dq_pair)):
        out[side, krows2:] = dq[sibling]


def finish_kernel(krows, dkv_own, dq_same, dq_pair, sib_ref, dq_out, dk_out, dv_out):
    row, chip, core, quarter = my_place()
    for side, dq in enumerate((dq_same, dq_pair)):
        for step, ref in enumerate((dkv_own, sib_ref)):
            lanes = lanes_of(quarter ^ (2 * side + step))
            dk_out[0, :, lanes] = ref[side, :krows]
            dv_out[0, :, lanes] = ref[side, krows : 2 * krows]
            dq_out[0, :, lanes] = ref[side, 2 * krows :] if step else dq[core]


def send(block, axes, count, step):
    return lax.ppermute(block, axes, [(place, place ^ step) for place in range(count)])


def body(sizes, queries, keys, values, outputs, grad_out, lse, tile_slot, tile_live, tile_bits):
    row_count, chips, cores = sizes
    heads = lse.shape[1]
    width = queries.shape[2]
    head_dim = width // heads
    tile = tile_bits.shape[4]
    capacity = tile_slot.shape[2]
    rows = queries.shape[1]
    krows = keys.shape[1]
    query_tiles = lse.shape[2] // tile
    key_tiles = row_count * krows // tile
    line = ("row", "core")
    places = row_count * cores

    def shape(*dims, dtype=BF16):
        return jax.ShapeDtypeStruct(dims, dtype)

    qg_shape = shape(2 * rows + PAD, LANES)
    kv_shape = shape(2, 2 * krows, LANES)
    slabs = capacity // 2 + 1
    qg_own, pair0, pair1, kv_own, to_sibling, bits_own, lse_own = pl.pallas_call(
        functools.partial(pack_kernel, heads),
        out_shape=(
            qg_shape, qg_shape, qg_shape, shape(4 * krows, LANES),
            shape(4 * krows + 2 * rows + PAD, LANES),
            shape(slabs + query_tiles // 4, 8, LANES, dtype=I32),
            shape(query_tiles, 2, tile, dtype=F32),
        ),
        in_specs=[HBM] * 7 + [VMEM] * 2,
        out_specs=(VMEM,) * 7,
        scratch_shapes=[
            pltpu.VMEM(queries.shape, BF16),
            pltpu.VMEM(queries.shape, BF16),
            pltpu.VMEM(queries.shape, BF16),
            pltpu.VMEM(keys.shape, BF16),
            pltpu.VMEM(keys.shape, BF16),
            pltpu.VMEM(tile_bits.shape, I32),
            pltpu.VMEM(lse.shape, F32),
            pltpu.VMEM((QUARTERS, PAD, rows), BF16),
            pltpu.SemaphoreType.DMA((7,)),
        ],
        compiler_params=PACK,
        name="pack",
    )(queries, grad_out, outputs, keys, values, tile_bits, lse, tile_slot, tile_live)

    pair0 = send(pair0, line, places, 2)
    pair1 = send(pair1, line, places, 3)
    from_sibling = send(to_sibling, "core", cores, 1)
    bits_pair = send(bits_own, "row", row_count, 1)
    kv_same, kv_pair = pl.pallas_call(
        functools.partial(key_join_kernel, krows),
        out_shape=(kv_shape, kv_shape),
        in_specs=[VMEM] * 2,
        out_specs=(VMEM,) * 2,
        compiler_params=SMALL,
        name="key_join",
    )(kv_own, from_sibling)
    kv_out = (kv_same, kv_pair)
    kv = [kv_same] + [
        send(kv_out[step % 2], "row", row_count, step) for step in range(1, row_count)
    ]
    qg, bits, lse2 = pl.pallas_call(
        functools.partial(query_join_kernel, krows, slabs),
        out_shape=(
            shape(QUARTERS, 2 * rows + PAD, LANES),
            shape(2, capacity // 2 + 1, 8, LANES, dtype=I32),
            shape(2, query_tiles, 2, tile, dtype=F32),
        ),
        in_specs=[VMEM] * 7,
        out_specs=(VMEM,) * 3,
        compiler_params=SMALL,
        cost_estimate=early(20),
        name="query_join",
    )(qg_own, from_sibling, pair0, pair1, bits_own, bits_pair, lse_own)
    qg = [qg] + [send(qg, "chip", chips, step) for step in range(1, chips)]
    bits_sibling = send(bits, "core", cores, 1)

    placed = pl.pallas_call(
        functools.partial(key_place_kernel, head_dim, tile),
        out_shape=(
            shape(2, key_tiles, tile, LANES), shape(2, key_tiles, tile, LANES),
            shape(2, key_tiles, LANES, 2 * tile),
        ),
        in_specs=[VMEM] * row_count,
        out_specs=(VMEM,) * 3,
        compiler_params=SMALL,
        cost_estimate=early(20),
        name="key_place",
    )(*kv)
    parts = pl.pallas_call(
        functools.partial(pair_kernel, (head_dim, tile, capacity, chips, row_count)),
        out_shape=(shape(2, query_tiles, LANES, tile),) + (kv_shape,) * row_count,
        in_specs=[VMEM] * (chips + 6),
        out_specs=(VMEM,) * (1 + row_count),
        scratch_shapes=[
            pltpu.VMEM((2, query_tiles, 2, tile, LANES), BF16),
            pltpu.VMEM((2, query_tiles, 2, tile, LANES), BF16),
            pltpu.VMEM((2, query_tiles, PAD, tile), F32),
            pltpu.VMEM((2, query_tiles, LANES, tile), F32),
            pltpu.VMEM((2, key_tiles, tile, LANES), F32),
            pltpu.VMEM((2, key_tiles, tile, LANES), F32),
            pltpu.VMEM((QUARTERS, capacity, 4, LANES), I32),
            pltpu.SMEM((QUARTERS, 8, LANES), I32),
            pltpu.SMEM((QUARTERS * capacity,), I32),
            pltpu.SemaphoreType.DMA((QUARTERS,)),
        ],
        compiler_params=MEDIUM,
        name="pair",
    )(*qg, *placed, bits, bits_sibling, lse2)

    dkv = parts[1:]
    dq = pl.pallas_call(
        functools.partial(turn_kernel, rows),
        out_shape=(shape(QUARTERS, rows, LANES),) * chips,
        in_specs=[VMEM],
        out_specs=(VMEM,) * chips,
        scratch_shapes=[pltpu.VMEM((2, query_tiles * tile, LANES), BF16)],
        compiler_params=SMALL,
        name="turn",
    )(parts[0])
    dq = [dq[0]] + [send(dq[step], "chip", chips, step) for step in range(1, chips)]
    dkv = [dkv[0]] + [send(dkv[step], "row", row_count, step) for step in range(1, row_count)]
    dq_same, dq_pair = pl.pallas_call(
        functools.partial(query_sum_kernel, chips),
        out_shape=(shape(2, rows, LANES),) * 2,
        in_specs=[VMEM] * chips,
        out_specs=(VMEM,) * 2,
        compiler_params=SMALL,
        name="query_sum",
    )(*dq)
    dq_pair = send(dq_pair, "row", row_count, 1)
    dkv_own, dkv_sibling = pl.pallas_call(
        functools.partial(key_sum_kernel, row_count),
        out_shape=(kv_shape,) * 2,
        in_specs=[VMEM] * row_count,
        out_specs=(VMEM,) * 2,
        compiler_params=SMALL,
        cost_estimate=early(20),
        name="key_sum",
    )(*dkv)
    to_sibling = pl.pallas_call(
        bundle_kernel,
        out_shape=shape(2, 2 * krows + rows, LANES),
        in_specs=[VMEM] * 3,
        out_specs=VMEM,
        compiler_params=SMALL,
        name="bundle",
    )(dkv_sibling, dq_same, dq_pair)
    from_sibling = send(to_sibling, "core", cores, 1)
    return pl.pallas_call(
        functools.partial(finish_kernel, krows),
        out_shape=(shape(1, rows, width), shape(1, krows, width), shape(1, krows, width)),
        in_specs=[VMEM] * 4,
        out_specs=(VMEM,) * 3,
        compiler_params=SMALL,
        name="finish",
    )(dkv_own, dq_same, dq_pair, from_sibling)


def solution(mesh):
    row_count, columns = mesh.devices.shape
    cores = 2
    chips = columns // cores
    fine = Mesh(mesh.devices.reshape(row_count, chips, cores), ("row", "chip", "core"))
    col = ("chip", "core")
    in_specs = (
        P("row", col, None),
        P(col, "row", None),
        P(col, "row", None),
        P("row", col, None),
        P("row", col, None),
        P("row", None, None),
        P("row", col, None),
        P("row", col),
        P("row", col, None, None, None),
    )
    out_specs = (P("row", col, None), P(col, "row", None), P(col, "row", None))
    return jax.shard_map(
        functools.partial(body, (row_count, chips, cores)),
        mesh=fine, in_specs=in_specs, out_specs=out_specs, check_vma=False,
    )
```

```python
import functools

import jax
import jax.numpy as jnp
from jax import lax
from jax.experimental import pallas as pl
from jax.experimental.pallas import tpu as pltpu
from jax.sharding import Mesh
from jax.sharding import PartitionSpec as P


F32 = jnp.float32
BF16 = jnp.bfloat16
I32 = jnp.int32
LANES = 128
PAD = 16
QUARTERS = 4
TOGETHER = 8
LSE_UNIT = 2.0**21
NT = (((1,), (1,)), ((), ()))
NN = (((1,), (0,)), ((), ()))
MEDIUM = pltpu.CompilerParams(vmem_limit_bytes=28 * 1024 * 1024)
PACK = pltpu.CompilerParams(vmem_limit_bytes=int(53.6 * 1024 * 1024))
SMALL = pltpu.CompilerParams(vmem_limit_bytes=12 * 1024 * 1024)
def early(gigaflops):
    return pl.CostEstimate(flops=gigaflops * 10**9, bytes_accessed=0, transcendentals=0)


VMEM = pl.BlockSpec(memory_space=pltpu.VMEM)
HBM = pl.BlockSpec(memory_space=pltpu.HBM)


def lanes_of(quarter):
    return pl.ds(pl.multiple_of(quarter * LANES, LANES), LANES)


def my_place():
    row, chip, core = (lax.axis_index(name) for name in ("row", "chip", "core"))
    return row, chip, core, row % 2 * 2 + core


def pack_kernel(
    heads, q_hbm, g_hbm, o_hbm, k_hbm, v_hbm, bits_hbm, lse_hbm, slot_ref, live_ref,
    qg_own, pair0_ref, pair1_ref, kv_own, sib_ref, packed_ref, lse_own,
    q_ref, g_ref, o_ref, k_ref, v_ref, bits_ref, lse_ref, delta_ref, sems,
):
    arrays = (
        (q_hbm, q_ref), (g_hbm, g_ref), (o_hbm, o_ref), (k_hbm, k_ref),
        (v_hbm, v_ref), (bits_hbm, bits_ref), (lse_hbm, lse_ref),
    )
    copies = [pltpu.make_async_copy(a, b, sems.at[i]) for i, (a, b) in enumerate(arrays)]
    for copy in copies:
        copy.start()
    rows, width = q_ref.shape[1:]
    krows = k_ref.shape[1]
    head_dim = width // heads
    local = heads // QUARTERS
    capacity = bits_ref.shape[2]
    quarter = my_place()[3]
    feature = lax.broadcasted_iota(I32, (QUARTERS * PAD, width), 1)
    line = lax.broadcasted_iota(I32, (QUARTERS * PAD, width), 0)
    wanted = jnp.where(line % PAD < local, line // PAD * local + line % PAD, -1)
    pick = (feature // head_dim == wanted).astype(F32)
    packed_ref[capacity // 2] = jnp.zeros((8, LANES), I32)
    packed_ref[capacity // 2, 0:1, 0:capacity] = slot_ref[0]
    packed_ref[capacity // 2, 1:2, 0:1] = live_ref[...]
    for copy in copies:
        copy.wait()
    product = g_ref[0].astype(F32) * o_ref[0].astype(F32)
    delta = lax.dot_general(
        pick, product, NT, precision=lax.Precision.HIGHEST, preferred_element_type=F32
    ).astype(BF16)
    for index in range(QUARTERS):
        delta_ref[index] = delta[index * PAD : (index + 1) * PAD]
    for step, (ref, start) in enumerate(
        ((qg_own, 0), (sib_ref, 4 * krows), (pair0_ref, 0), (pair1_ref, 0))
    ):
        lanes = lanes_of(quarter ^ step)
        ref[start : start + rows] = q_ref[0, :, lanes]
        ref[start + rows : start + 2 * rows] = g_ref[0, :, lanes]
        if rows < LANES:
            ref[start + 2 * rows : start + 2 * rows + PAD] = jnp.zeros((PAD, LANES), BF16)
        ref[start + 2 * rows : start + 2 * rows + PAD, :rows] = delta_ref[quarter ^ step]
    for step in range(QUARTERS):
        ref = (kv_own, sib_ref)[step % 2]
        lanes = lanes_of(quarter ^ step)
        start = step // 2 * 2 * krows
        ref[start : start + krows] = k_ref[0, :, lanes]
        ref[start + krows : start + 2 * krows] = v_ref[0, :, lanes]
    every = lse_ref[0]

    def lse_of(wanted_quarter):
        own = every[:local]
        for index in range(1, QUARTERS):
            own = jnp.where(
                wanted_quarter == index, every[local * index : local * (index + 1)], own
            )
        return own

    mine = lse_of(quarter)
    other = (lse_of(quarter ^ 2) * LSE_UNIT).astype(I32)
    for u in range(lse_own.shape[0]):
        lanes = slice(u * LANES, (u + 1) * LANES)
        lse_own[u] = mine[:, lanes]
        packed_ref[capacity // 2 + 1 + u // 4, u % 4 * 2 : u % 4 * 2 + 2] = other[:, lanes]
    for entry in range(capacity):
        words = bits_ref[0, 0, entry]
        span = slice(entry % 2 * 4, entry % 2 * 4 + 4)
        packed_ref[entry // 2, span] = words[:4] | lax.shift_left(words[4:], I32(16))


def key_join_kernel(krows, kv_own, sib_ref, kv_same, kv_pair):
    core = my_place()[2]
    for side, ref in enumerate((kv_same, kv_pair)):
        span = slice(side * 2 * krows, (side + 1) * 2 * krows)
        ref[core] = kv_own[span]
        ref[1 - core] = sib_ref[span]


def query_join_kernel(
    krows, slabs, qg_own, sib_ref, pair0_ref, pair1_ref, bits_own, bits_pair, lse_own,
    qg_out, bits_out, lse_out,
):
    row, chip, core, quarter = my_place()
    side = row % 2
    qg_out[quarter] = qg_own[...]
    qg_out[quarter ^ 1] = sib_ref[4 * krows :]
    qg_out[quarter ^ 2] = pair0_ref[...]
    qg_out[quarter ^ 3] = pair1_ref[...]
    bits_out[side] = bits_own[:slabs]
    bits_out[1 - side] = bits_pair[:slabs]
    lse_out[side] = lse_own[...]
    for u in range(lse_out.shape[1]):
        fixed = bits_pair[slabs + u // 4, u % 4 * 2 : u % 4 * 2 + 2]
        lse_out[1 - side, u] = fixed.astype(F32) * (1.0 / LSE_UNIT)


def far_join_kernel(pair_ref, *refs):
    parts, (far_out, pair_out) = refs[:-2], refs[-2:]
    for index, ref in enumerate(parts):
        far_out[index] = ref[...]
    pair_out[...] = pair_ref[...]


def key_place_kernel(head_dim, tile, same_ref, pair_ref, far_ref, k_out, v_out, k2t_out):
    kv_refs = [same_ref, pair_ref] + [far_ref.at[index] for index in range(far_ref.shape[0])]
    krows = kv_refs[0].shape[1] // 2
    row = my_place()[0]
    for step, ref in enumerate(kv_refs):
        start = (row ^ step) * krows
        inner = pl.multiple_of(start % tile, krows)
        for block in range(2):
            k_out[block, start // tile, pl.ds(inner, krows)] = ref[block, :krows]
            v_out[block, start // tile, pl.ds(inner, krows)] = ref[block, krows:]
    low_row = lax.broadcasted_iota(I32, (LANES, tile), 0) < head_dim
    none_t = jnp.zeros((LANES, tile), BF16)
    for block in range(2):
        for w in range(k_out.shape[1]):
            flipped = k_out[block, w].T
            k2t_out[block, w] = jnp.concatenate(
                [jnp.where(low_row, flipped, none_t), jnp.where(low_row, none_t, flipped)], axis=1
            )


def pair_kernel(sizes, *refs):
    head_dim, tile, capacity, chips, row_count = sizes
    qg_refs, refs = refs[:chips], refs[chips:]
    (k_scr, v_scr, k2t_scr), refs = refs[:3], refs[3:]
    bits_refs, lse_ref, refs = refs[:2], refs[2], refs[3:]
    dqt_ref, dkv_refs, refs = refs[0], refs[1 : 1 + row_count], refs[1 + row_count :]
    q2_scr, g2_scr, delta_scr, dqt_scr, dk_scr, dv_scr, bits_scr, info, todo, sems = refs
    rows = (qg_refs[0].shape[1] - PAD) // 2
    krows = dkv_refs[0].shape[1] // 2
    query_tiles = q2_scr.shape[1]
    key_tiles = k_scr.shape[1]
    scaling = float(head_dim) ** -0.5
    row, chip, core, quarter = my_place()
    side = row % 2

    copies = [
        pltpu.make_async_copy(
            bits_refs[i % 2].at[i // 2, capacity // 2], info.at[i], sems.at[i]
        )
        for i in range(QUARTERS)
    ]
    for copy in copies:
        copy.start()

    low = lax.broadcasted_iota(I32, (rows, LANES), 1) < head_dim
    none = jnp.zeros((rows, LANES), BF16)
    for step in range(chips):
        for index in range(QUARTERS):
            source = (chip ^ step) * 2 + index % 2
            start = source * rows
            u = start // tile
            inner = pl.multiple_of(start % tile, rows)
            block = index // 2
            for scr, part in ((q2_scr, 0), (g2_scr, 1)):
                piece = qg_refs[step][index, part * rows : (part + 1) * rows]
                if part == 0:
                    piece = (piece.astype(F32) * scaling).astype(BF16)
                scr[block, u, 0, pl.ds(inner, rows)] = jnp.where(low, piece, none)
                scr[block, u, 1, pl.ds(inner, rows)] = jnp.where(low, none, piece)
            delta = qg_refs[step][index, 2 * rows :, :rows].astype(F32)
            if rows == tile:
                delta_scr[block, u] = delta
            else:
                for part in range(tile // rows):
                    @pl.when(source % (tile // rows) == part)
                    def _(part=part, delta=delta, u=u, block=block):
                        delta_scr[block, u, :, part * rows : (part + 1) * rows] = delta
    dqt_scr[...] = jnp.zeros_like(dqt_scr)
    dk_scr[...] = jnp.zeros_like(dk_scr)
    dv_scr[...] = jnp.zeros_like(dv_scr)
    place_in = lax.broadcasted_iota(I32, (2, 4, 16, tile), 2)
    upper = lax.broadcasted_iota(I32, (2, 4, 16, tile), 0)
    bit = lax.shift_left(I32(1), place_in + 16 * upper).reshape(tile, tile)
    for step in range(QUARTERS):
        for entry in range(capacity):
            span = slice(entry % 2 * 4, entry % 2 * 4 + 4)
            bits_scr[step, entry] = bits_refs[step % 2][side ^ (step // 2), entry // 2, span]
    for i, copy in enumerate(copies):
        copy.wait()
    count = I32(0)
    for i in range(QUARTERS):
        step = (side ^ (i // 2)) * 2 + i % 2

        def listed(entry, count, i=i, step=step):
            todo[count] = info[i, 0, entry] + 32 * entry + 1024 * step
            return count + 1

        count = lax.fori_loop(0, info[i, 1, 0], listed, count)

    def some_tiles(index, _):
        work = []
        for part in range(TOGETHER):
            position = index * TOGETHER + part
            item = todo[jnp.minimum(position, count - 1)]
            slot = item % 32
            step = item // 1024
            qb = side ^ (step // 2)
            kb = core ^ (step % 2)
            u = slot // key_tiles
            w = slot % key_tiles
            words = bits_scr[step, item // 32 % 32]
            if part:
                words = words & jnp.where(position < count, I32(-1), I32(0))
            words = jnp.broadcast_to(words[:, None, :], (4, 16, tile)).reshape(64, tile)
            edge = (jnp.concatenate([words, words], axis=0) & bit) != 0
            q2 = q2_scr[qb, u].reshape(2 * tile, LANES)
            g2 = g2_scr[qb, u].reshape(2 * tile, LANES)
            scores = lax.dot_general(k_scr[kb, w], q2, NT, preferred_element_type=F32)
            grad_prob = lax.dot_general(v_scr[kb, w], g2, NT, preferred_element_type=F32)
            work.append((qb, kb, u, w, edge, q2, g2, scores, grad_prob))
        done = []
        for qb, kb, u, w, edge, q2, g2, scores, grad_prob in work:
            lse_tile = lse_ref[qb, u]
            delta_tile = delta_scr[qb, u]
            probs, grads = [], []
            for h in range(2):
                s = scores[:, h * tile : (h + 1) * tile]
                gp = grad_prob[:, h * tile : (h + 1) * tile]
                p = jnp.where(edge, jnp.exp(s - lse_tile[h : h + 1]), 0.0)
                ds = p * (gp - delta_tile[h : h + 1])
                probs.append(p.astype(BF16))
                grads.append(ds.astype(BF16))
            done.append((
                lax.dot_general(
                    jnp.concatenate(probs, axis=1), g2, NN, preferred_element_type=F32
                ),
                lax.dot_general(
                    jnp.concatenate(grads, axis=1), q2, NN, preferred_element_type=F32
                ),
                lax.dot_general(
                    k2t_scr[kb, w], jnp.concatenate(grads, axis=0), NN,
                    preferred_element_type=F32,
                ),
            ))
        for (qb, kb, u, w, *_), (dv, dk, dqt) in zip(work, done):
            dv_scr[kb, w] += dv
            dk_scr[kb, w] += dk
            dqt_scr[qb, u] += dqt
        return 0

    lax.fori_loop(0, (count + TOGETHER - 1) // TOGETHER, some_tiles, 0)

    for step in range(row_count):
        start = (row ^ step) * krows
        inner = pl.multiple_of(start % tile, krows)
        for block in range(2):
            dk = dk_scr[block, start // tile, pl.ds(inner, krows)]
            dv = dv_scr[block, start // tile, pl.ds(inner, krows)]
            dkv_refs[step][block, :krows] = dk.astype(BF16)
            dkv_refs[step][block, krows:] = dv.astype(BF16)
    dqt_ref[...] = (dqt_scr[...] * scaling).astype(BF16)


def turn_kernel(rows, dqt_ref, *refs):
    dq_refs, dq_scr = refs[:-1], refs[-1]
    tile = dqt_ref.shape[3]
    chip = my_place()[1]
    for block in range(2):
        for u in range(dqt_ref.shape[1]):
            dq_scr[block, u * tile : (u + 1) * tile] = dqt_ref[block, u].T
    for step, ref in enumerate(dq_refs):
        for index in range(QUARTERS):
            start = pl.multiple_of(((chip ^ step) * 2 + index % 2) * rows, rows)
            ref[index] = dq_scr[index // 2, pl.ds(start, rows)]


def query_sum_kernel(chips, *refs):
    parts, (same_ref, pair_ref) = refs[:chips], refs[chips:]
    side = my_place()[0] % 2
    for step, ref in enumerate((same_ref, pair_ref)):
        for core in range(2):
            index = (side ^ step) * 2 + core
            total = parts[0][index].astype(F32)
            for part in parts[1:]:
                total += part[index].astype(F32)
            ref[core] = total.astype(BF16)


def key_sum_kernel(row_count, *refs):
    dkv_refs, (own_ref, sib_ref) = refs[:-2], refs[-2:]
    core = my_place()[2]
    for ref, block in ((own_ref, core), (sib_ref, 1 - core)):
        for side in range(2):
            total = dkv_refs[side][block].astype(F32)
            for other in range(side + 2, row_count, 2):
                total += dkv_refs[other][block].astype(F32)
            ref[side] = total.astype(BF16)


def bundle_kernel(dkv_ref, dq_same, dq_pair, out):
    krows2 = dkv_ref.shape[1]
    sibling = 1 - my_place()[2]
    out[:, :krows2] = dkv_ref[...]
    for side, dq in enumerate((dq_same, dq_pair)):
        out[side, krows2:] = dq[sibling]


def finish_kernel(krows, dkv_own, dq_same, dq_pair, sib_ref, dq_out, dk_out, dv_out):
    row, chip, core, quarter = my_place()
    for side, dq in enumerate((dq_same, dq_pair)):
        for step, ref in enumerate((dkv_own, sib_ref)):
            lanes = lanes_of(quarter ^ (2 * side + step))
            dk_out[0, :, lanes] = ref[side, :krows]
            dv_out[0, :, lanes] = ref[side, krows : 2 * krows]
            dq_out[0, :, lanes] = ref[side, 2 * krows :] if step else dq[core]


def send(block, axes, count, step):
    return lax.ppermute(block, axes, [(place, place ^ step) for place in range(count)])


def body(sizes, queries, keys, values, outputs, grad_out, lse, tile_slot, tile_live, tile_bits):
    row_count, chips, cores = sizes
    heads = lse.shape[1]
    width = queries.shape[2]
    head_dim = width // heads
    tile = tile_bits.shape[4]
    capacity = tile_slot.shape[2]
    rows = queries.shape[1]
    krows = keys.shape[1]
    query_tiles = lse.shape[2] // tile
    key_tiles = row_count * krows // tile
    line = ("row", "core")
    places = row_count * cores

    def shape(*dims, dtype=BF16):
        return jax.ShapeDtypeStruct(dims, dtype)

    qg_shape = shape(2 * rows + PAD, LANES)
    kv_shape = shape(2, 2 * krows, LANES)
    slabs = capacity // 2 + 1
    qg_own, pair0, pair1, kv_own, to_sibling, bits_own, lse_own = pl.pallas_call(
        functools.partial(pack_kernel, heads),
        out_shape=(
            qg_shape, qg_shape, qg_shape, shape(4 * krows, LANES),
            shape(4 * krows + 2 * rows + PAD, LANES),
            shape(slabs + query_tiles // 4, 8, LANES, dtype=I32),
            shape(query_tiles, 2, tile, dtype=F32),
        ),
        in_specs=[HBM] * 7 + [VMEM] * 2,
        out_specs=(VMEM,) * 7,
        scratch_shapes=[
            pltpu.VMEM(queries.shape, BF16),
            pltpu.VMEM(queries.shape, BF16),
            pltpu.VMEM(queries.shape, BF16),
            pltpu.VMEM(keys.shape, BF16),
            pltpu.VMEM(keys.shape, BF16),
            pltpu.VMEM(tile_bits.shape, I32),
            pltpu.VMEM(lse.shape, F32),
            pltpu.VMEM((QUARTERS, PAD, rows), BF16),
            pltpu.SemaphoreType.DMA((7,)),
        ],
        compiler_params=PACK,
        name="pack",
    )(queries, grad_out, outputs, keys, values, tile_bits, lse, tile_slot, tile_live)

    pair0 = send(pair0, line, places, 2)
    pair1 = send(pair1, line, places, 3)
    from_sibling = send(to_sibling, "core", cores, 1)
    bits_pair = send(bits_own, "row", row_count, 1)
    kv_same, kv_pair = pl.pallas_call(
        functools.partial(key_join_kernel, krows),
        out_shape=(kv_shape, kv_shape),
        in_specs=[VMEM] * 2,
        out_specs=(VMEM,) * 2,
        compiler_params=SMALL,
        name="key_join",
    )(kv_own, from_sibling)
    kv_out = (kv_same, kv_pair)
    kv_far, kv_pair = pl.pallas_call(
        far_join_kernel,
        out_shape=(shape(row_count - 2, *kv_shape.shape), kv_shape),
        in_specs=[VMEM] * (row_count - 1),
        out_specs=(VMEM, VMEM),
        compiler_params=SMALL,
        cost_estimate=early(20),
        name="far_join",
    )(kv_pair, *[send(kv_out[step % 2], "row", row_count, step) for step in range(2, row_count)])
    kv = (kv_same, send(kv_pair, "row", row_count, 1), kv_far)
    qg, bits, lse2 = pl.pallas_call(
        functools.partial(query_join_kernel, krows, slabs),
        out_shape=(
            shape(QUARTERS, 2 * rows + PAD, LANES),
            shape(2, capacity // 2 + 1, 8, LANES, dtype=I32),
            shape(2, query_tiles, 2, tile, dtype=F32),
        ),
        in_specs=[VMEM] * 7,
        out_specs=(VMEM,) * 3,
        compiler_params=SMALL,
        cost_estimate=early(20),
        name="query_join",
    )(qg_own, from_sibling, pair0, pair1, bits_own, bits_pair, lse_own)
    qg = [qg] + [send(qg, "chip", chips, step) for step in range(1, chips)]
    bits_sibling = send(bits, "core", cores, 1)

    placed = pl.pallas_call(
        functools.partial(key_place_kernel, head_dim, tile),
        out_shape=(
            shape(2, key_tiles, tile, LANES), shape(2, key_tiles, tile, LANES),
            shape(2, key_tiles, LANES, 2 * tile),
        ),
        in_specs=[VMEM] * 3,
        out_specs=(VMEM,) * 3,
        compiler_params=SMALL,
        name="key_place",
    )(*kv)
    parts = pl.pallas_call(
        functools.partial(pair_kernel, (head_dim, tile, capacity, chips, row_count)),
        out_shape=(shape(2, query_tiles, LANES, tile),) + (kv_shape,) * row_count,
        in_specs=[VMEM] * (chips + 6),
        out_specs=(VMEM,) * (1 + row_count),
        scratch_shapes=[
            pltpu.VMEM((2, query_tiles, 2, tile, LANES), BF16),
            pltpu.VMEM((2, query_tiles, 2, tile, LANES), BF16),
            pltpu.VMEM((2, query_tiles, PAD, tile), F32),
            pltpu.VMEM((2, query_tiles, LANES, tile), F32),
            pltpu.VMEM((2, key_tiles, tile, LANES), F32),
            pltpu.VMEM((2, key_tiles, tile, LANES), F32),
            pltpu.VMEM((QUARTERS, capacity, 4, LANES), I32),
            pltpu.SMEM((QUARTERS, 8, LANES), I32),
            pltpu.SMEM((QUARTERS * capacity,), I32),
            pltpu.SemaphoreType.DMA((QUARTERS,)),
        ],
        compiler_params=MEDIUM,
        name="pair",
    )(*qg, *placed, bits, bits_sibling, lse2)

    dkv = parts[1:]
    dq = pl.pallas_call(
        functools.partial(turn_kernel, rows),
        out_shape=(shape(QUARTERS, rows, LANES),) * chips,
        in_specs=[VMEM],
        out_specs=(VMEM,) * chips,
        scratch_shapes=[pltpu.VMEM((2, query_tiles * tile, LANES), BF16)],
        compiler_params=SMALL,
        name="turn",
    )(parts[0])
    dq = [dq[0]] + [send(dq[step], "chip", chips, step) for step in range(1, chips)]
    dkv = [dkv[0]] + [send(dkv[step], "row", row_count, step) for step in range(1, row_count)]
    dq_same, dq_pair = pl.pallas_call(
        functools.partial(query_sum_kernel, chips),
        out_shape=(shape(2, rows, LANES),) * 2,
        in_specs=[VMEM] * chips,
        out_specs=(VMEM,) * 2,
        compiler_params=SMALL,
        name="query_sum",
    )(*dq)
    dq_pair = send(dq_pair, "row", row_count, 1)
    dkv_own, dkv_sibling = pl.pallas_call(
        functools.partial(key_sum_kernel, row_count),
        out_shape=(kv_shape,) * 2,
        in_specs=[VMEM] * row_count,
        out_specs=(VMEM,) * 2,
        compiler_params=SMALL,
        cost_estimate=early(20),
        name="key_sum",
    )(*dkv)
    to_sibling = pl.pallas_call(
        bundle_kernel,
        out_shape=shape(2, 2 * krows + rows, LANES),
        in_specs=[VMEM] * 3,
        out_specs=VMEM,
        compiler_params=SMALL,
        name="bundle",
    )(dkv_sibling, dq_same, dq_pair)
    from_sibling = send(to_sibling, "core", cores, 1)
    return pl.pallas_call(
        functools.partial(finish_kernel, krows),
        out_shape=(shape(1, rows, width), shape(1, krows, width), shape(1, krows, width)),
        in_specs=[VMEM] * 4,
        out_specs=(VMEM,) * 3,
        compiler_params=SMALL,
        name="finish",
    )(dkv_own, dq_same, dq_pair, from_sibling)


def solution(mesh):
    row_count, columns = mesh.devices.shape
    cores = 2
    chips = columns // cores
    fine = Mesh(mesh.devices.reshape(row_count, chips, cores), ("row", "chip", "core"))
    col = ("chip", "core")
    in_specs = (
        P("row", col, None),
        P(col, "row", None),
        P(col, "row", None),
        P("row", col, None),
        P("row", col, None),
        P("row", None, None),
        P("row", col, None),
        P("row", col),
        P("row", col, None, None, None),
    )
    out_specs = (P("row", col, None), P(col, "row", None), P(col, "row", None))
    return jax.shard_map(
        functools.partial(body, (row_count, chips, cores)),
        mesh=fine, in_specs=in_specs, out_specs=out_specs, check_vma=False,
    )
```

```python
import functools

import jax
import jax.numpy as jnp
from jax import lax
from jax.experimental import pallas as pl
from jax.experimental.pallas import tpu as pltpu
from jax.sharding import Mesh
from jax.sharding import PartitionSpec as P


F32 = jnp.float32
BF16 = jnp.bfloat16
I32 = jnp.int32
LANES = 128
PAD = 16
QUARTERS = 4
TOGETHER = 8
LSE_UNIT = 2.0**21
NT = (((1,), (1,)), ((), ()))
NN = (((1,), (0,)), ((), ()))
MEDIUM = pltpu.CompilerParams(vmem_limit_bytes=28 * 1024 * 1024)
PACK = pltpu.CompilerParams(vmem_limit_bytes=int(53.6 * 1024 * 1024))
SMALL = pltpu.CompilerParams(vmem_limit_bytes=12 * 1024 * 1024)
def early(gigaflops):
    return pl.CostEstimate(flops=gigaflops * 10**9, bytes_accessed=0, transcendentals=0)


VMEM = pl.BlockSpec(memory_space=pltpu.VMEM)
HBM = pl.BlockSpec(memory_space=pltpu.HBM)


def lanes_of(quarter):
    return pl.ds(pl.multiple_of(quarter * LANES, LANES), LANES)


def my_place():
    row, chip, core = (lax.axis_index(name) for name in ("row", "chip", "core"))
    return row, chip, core, row % 2 * 2 + core


def pack_kernel(
    heads, q_hbm, g_hbm, o_hbm, k_hbm, v_hbm, bits_hbm, lse_hbm, slot_ref, live_ref,
    qg_own, pair0_ref, pair1_ref, kv_own, sib_ref, packed_ref, lse_own,
    q_ref, g_ref, o_ref, k_ref, v_ref, bits_ref, lse_ref, delta_ref, sems,
):
    arrays = (
        (q_hbm, q_ref), (g_hbm, g_ref), (o_hbm, o_ref), (k_hbm, k_ref),
        (v_hbm, v_ref), (bits_hbm, bits_ref), (lse_hbm, lse_ref),
    )
    copies = [pltpu.make_async_copy(a, b, sems.at[i]) for i, (a, b) in enumerate(arrays)]
    for copy in copies:
        copy.start()
    rows, width = q_ref.shape[1:]
    krows = k_ref.shape[1]
    head_dim = width // heads
    local = heads // QUARTERS
    capacity = bits_ref.shape[2]
    quarter = my_place()[3]
    feature = lax.broadcasted_iota(I32, (QUARTERS * PAD, width), 1)
    line = lax.broadcasted_iota(I32, (QUARTERS * PAD, width), 0)
    wanted = jnp.where(line % PAD < local, line // PAD * local + line % PAD, -1)
    pick = (feature // head_dim == wanted).astype(F32)
    packed_ref[capacity // 2] = jnp.zeros((8, LANES), I32)
    packed_ref[capacity // 2, 0:1, 0:capacity] = slot_ref[0]
    packed_ref[capacity // 2, 1:2, 0:1] = live_ref[...]
    for copy in copies:
        copy.wait()
    product = g_ref[0].astype(F32) * o_ref[0].astype(F32)
    delta = lax.dot_general(
        pick, product, NT, precision=lax.Precision.HIGHEST, preferred_element_type=F32
    ).astype(BF16)
    for index in range(QUARTERS):
        delta_ref[index] = delta[index * PAD : (index + 1) * PAD]
    for step, (ref, start) in enumerate(
        ((qg_own, 0), (sib_ref, 4 * krows), (pair0_ref, 0), (pair1_ref, 0))
    ):
        lanes = lanes_of(quarter ^ step)
        ref[start : start + rows] = q_ref[0, :, lanes]
        ref[start + rows : start + 2 * rows] = g_ref[0, :, lanes]
        if rows < LANES:
            ref[start + 2 * rows : start + 2 * rows + PAD] = jnp.zeros((PAD, LANES), BF16)
        ref[start + 2 * rows : start + 2 * rows + PAD, :rows] = delta_ref[quarter ^ step]
    for step in range(QUARTERS):
        ref = (kv_own, sib_ref)[step % 2]
        lanes = lanes_of(quarter ^ step)
        start = step // 2 * 2 * krows
        ref[start : start + krows] = k_ref[0, :, lanes]
        ref[start + krows : start + 2 * krows] = v_ref[0, :, lanes]
    every = lse_ref[0]

    def lse_of(wanted_quarter):
        own = every[:local]
        for index in range(1, QUARTERS):
            own = jnp.where(
                wanted_quarter == index, every[local * index : local * (index + 1)], own
            )
        return own

    mine = lse_of(quarter)
    other = (lse_of(quarter ^ 2) * LSE_UNIT).astype(I32)
    for u in range(lse_own.shape[0]):
        lanes = slice(u * LANES, (u + 1) * LANES)
        lse_own[u] = mine[:, lanes]
        packed_ref[capacity // 2 + 1 + u // 4, u % 4 * 2 : u % 4 * 2 + 2] = other[:, lanes]
    for entry in range(capacity):
        words = bits_ref[0, 0, entry]
        span = slice(entry % 2 * 4, entry % 2 * 4 + 4)
        packed_ref[entry // 2, span] = words[:4] | lax.shift_left(words[4:], I32(16))


def key_join_kernel(krows, kv_own, sib_ref, kv_same, kv_pair):
    core = my_place()[2]
    for side, ref in enumerate((kv_same, kv_pair)):
        span = slice(side * 2 * krows, (side + 1) * 2 * krows)
        ref[core] = kv_own[span]
        ref[1 - core] = sib_ref[span]


def query_join_kernel(
    krows, slabs, qg_own, sib_ref, pair0_ref, pair1_ref, bits_own, bits_pair, lse_own,
    qg_out, bits_out, lse_out,
):
    row, chip, core, quarter = my_place()
    side = row % 2
    qg_out[quarter] = qg_own[...]
    qg_out[quarter ^ 1] = sib_ref[4 * krows :]
    qg_out[quarter ^ 2] = pair0_ref[...]
    qg_out[quarter ^ 3] = pair1_ref[...]
    bits_out[side] = bits_own[:slabs]
    bits_out[1 - side] = bits_pair[:slabs]
    lse_out[side] = lse_own[...]
    for u in range(lse_out.shape[1]):
        fixed = bits_pair[slabs + u // 4, u % 4 * 2 : u % 4 * 2 + 2]
        lse_out[1 - side, u] = fixed.astype(F32) * (1.0 / LSE_UNIT)


def far_join_kernel(pair_ref, *refs):
    parts, (far_out, pair_out) = refs[:-2], refs[-2:]
    for index, ref in enumerate(parts):
        far_out[index] = ref[...]
    pair_out[...] = pair_ref[...]


def key_place_kernel(head_dim, tile, same_ref, pair_ref, far_ref, k_out, v_out, k2t_out):
    kv_refs = [same_ref, pair_ref] + [far_ref.at[index] for index in range(far_ref.shape[0])]
    krows = kv_refs[0].shape[1] // 2
    row = my_place()[0]
    for step, ref in enumerate(kv_refs):
        start = (row ^ step) * krows
        inner = pl.multiple_of(start % tile, krows)
        for block in range(2):
            k_out[block, start // tile, pl.ds(inner, krows)] = ref[block, :krows]
            v_out[block, start // tile, pl.ds(inner, krows)] = ref[block, krows:]
    low_row = lax.broadcasted_iota(I32, (LANES, tile), 0) < head_dim
    none_t = jnp.zeros((LANES, tile), BF16)
    for block in range(2):
        for w in range(k_out.shape[1]):
            flipped = k_out[block, w].T
            k2t_out[block, w] = jnp.concatenate(
                [jnp.where(low_row, flipped, none_t), jnp.where(low_row, none_t, flipped)], axis=1
            )


def pair_kernel(sizes, *refs):
    head_dim, tile, capacity, chips, row_count = sizes
    qg_refs, refs = refs[:chips], refs[chips:]
    (k_scr, v_scr, k2t_scr), refs = refs[:3], refs[3:]
    bits_refs, lse_ref, refs = refs[:2], refs[2], refs[3:]
    dqt_ref, dkv_refs, refs = refs[0], refs[1 : 1 + row_count], refs[1 + row_count :]
    q2_scr, g2_scr, delta_scr, dqt_scr, dk_scr, dv_scr, bits_scr, info, todo, sems = refs
    rows = (qg_refs[0].shape[1] - PAD) // 2
    krows = dkv_refs[0].shape[1] // 2
    query_tiles = q2_scr.shape[1]
    key_tiles = k_scr.shape[1]
    scaling = float(head_dim) ** -0.5
    row, chip, core, quarter = my_place()
    side = row % 2

    copies = [
        pltpu.make_async_copy(
            bits_refs[i % 2].at[i // 2, capacity // 2], info.at[i], sems.at[i]
        )
        for i in range(QUARTERS)
    ]
    for copy in copies:
        copy.start()

    low = lax.broadcasted_iota(I32, (rows, LANES), 1) < head_dim
    none = jnp.zeros((rows, LANES), BF16)
    for step in range(chips):
        for index in range(QUARTERS):
            source = (chip ^ step) * 2 + index % 2
            start = source * rows
            u = start // tile
            inner = pl.multiple_of(start % tile, rows)
            block = index // 2
            for scr, part in ((q2_scr, 0), (g2_scr, 1)):
                piece = qg_refs[step][index, part * rows : (part + 1) * rows]
                if part == 0:
                    piece = (piece.astype(F32) * scaling).astype(BF16)
                scr[block, u, 0, pl.ds(inner, rows)] = jnp.where(low, piece, none)
                scr[block, u, 1, pl.ds(inner, rows)] = jnp.where(low, none, piece)
            delta = qg_refs[step][index, 2 * rows :, :rows].astype(F32)
            if rows == tile:
                delta_scr[block, u] = delta
            else:
                for part in range(tile // rows):
                    @pl.when(source % (tile // rows) == part)
                    def _(part=part, delta=delta, u=u, block=block):
                        delta_scr[block, u, :, part * rows : (part + 1) * rows] = delta
    dqt_scr[...] = jnp.zeros_like(dqt_scr)
    dk_scr[...] = jnp.zeros_like(dk_scr)
    dv_scr[...] = jnp.zeros_like(dv_scr)
    place_in = lax.broadcasted_iota(I32, (2, 4, 16, tile), 2)
    upper = lax.broadcasted_iota(I32, (2, 4, 16, tile), 0)
    bit = lax.shift_left(I32(1), place_in + 16 * upper).reshape(tile, tile)
    for step in range(QUARTERS):
        for entry in range(capacity):
            span = slice(entry % 2 * 4, entry % 2 * 4 + 4)
            bits_scr[step, entry] = bits_refs[step % 2][side ^ (step // 2), entry // 2, span]
    for i, copy in enumerate(copies):
        copy.wait()
    count = I32(0)
    for i in range(QUARTERS):
        step = (side ^ (i // 2)) * 2 + i % 2

        def listed(entry, count, i=i, step=step):
            todo[count] = info[i, 0, entry] + 32 * entry + 1024 * step
            return count + 1

        count = lax.fori_loop(0, info[i, 1, 0], listed, count)

    def some_tiles(index, _):
        work = []
        for part in range(TOGETHER):
            position = index * TOGETHER + part
            item = todo[jnp.minimum(position, count - 1)]
            slot = item % 32
            step = item // 1024
            qb = side ^ (step // 2)
            kb = core ^ (step % 2)
            u = slot // key_tiles
            w = slot % key_tiles
            words = bits_scr[step, item // 32 % 32]
            if part:
                words = words & jnp.where(position < count, I32(-1), I32(0))
            words = jnp.broadcast_to(words[:, None, :], (4, 16, tile)).reshape(64, tile)
            edge = (jnp.concatenate([words, words], axis=0) & bit) != 0
            q2 = q2_scr[qb, u].reshape(2 * tile, LANES)
            g2 = g2_scr[qb, u].reshape(2 * tile, LANES)
            scores = lax.dot_general(k_scr[kb, w], q2, NT, preferred_element_type=F32)
            grad_prob = lax.dot_general(v_scr[kb, w], g2, NT, preferred_element_type=F32)
            work.append((qb, kb, u, w, edge, q2, g2, scores, grad_prob))
        done = []
        for qb, kb, u, w, edge, q2, g2, scores, grad_prob in work:
            lse_tile = lse_ref[qb, u]
            delta_tile = delta_scr[qb, u]
            probs, grads = [], []
            for h in range(2):
                s = scores[:, h * tile : (h + 1) * tile]
                gp = grad_prob[:, h * tile : (h + 1) * tile]
                p = jnp.where(edge, jnp.exp(s - lse_tile[h : h + 1]), 0.0)
                ds = p * (gp - delta_tile[h : h + 1])
                probs.append(p.astype(BF16))
                grads.append(ds.astype(BF16))
            done.append((
                lax.dot_general(
                    jnp.concatenate(probs, axis=1), g2, NN, preferred_element_type=F32
                ),
                lax.dot_general(
                    jnp.concatenate(grads, axis=1), q2, NN, preferred_element_type=F32
                ),
                lax.dot_general(
                    k2t_scr[kb, w], jnp.concatenate(grads, axis=0), NN,
                    preferred_element_type=F32,
                ),
            ))
        for (qb, kb, u, w, *_), (dv, dk, dqt) in zip(work, done):
            dv_scr[kb, w] += dv
            dk_scr[kb, w] += dk
            dqt_scr[qb, u] += dqt
        return 0

    lax.fori_loop(0, (count + TOGETHER - 1) // TOGETHER, some_tiles, 0)

    for step in range(row_count):
        start = (row ^ step) * krows
        inner = pl.multiple_of(start % tile, krows)
        for block in range(2):
            dk = dk_scr[block, start // tile, pl.ds(inner, krows)]
            dv = dv_scr[block, start // tile, pl.ds(inner, krows)]
            dkv_refs[step][block, :krows] = dk.astype(BF16)
            dkv_refs[step][block, krows:] = dv.astype(BF16)
    dqt_ref[...] = (dqt_scr[...] * scaling).astype(BF16)


def turn_kernel(rows, dqt_ref, *refs):
    dq_refs, dq_scr = refs[:-1], refs[-1]
    tile = dqt_ref.shape[3]
    chip = my_place()[1]
    for block in range(2):
        for u in range(dqt_ref.shape[1]):
            dq_scr[block, u * tile : (u + 1) * tile] = dqt_ref[block, u].T
    for step, ref in enumerate(dq_refs):
        for index in range(QUARTERS):
            start = pl.multiple_of(((chip ^ step) * 2 + index % 2) * rows, rows)
            ref[index] = dq_scr[index // 2, pl.ds(start, rows)]


def query_sum_kernel(chips, *refs):
    parts, (same_ref, pair_ref) = refs[:chips], refs[chips:]
    side = my_place()[0] % 2
    for step, ref in enumerate((same_ref, pair_ref)):
        for core in range(2):
            index = (side ^ step) * 2 + core
            total = parts[0][index].astype(F32)
            for part in parts[1:]:
                total += part[index].astype(F32)
            ref[core] = total.astype(BF16)


def key_sum_kernel(row_count, *refs):
    dkv_refs, (own_ref, sib_ref) = refs[:1] + refs[row_count - 1 : 0 : -1], refs[-2:]
    core = my_place()[2]
    for ref, block in ((own_ref, core), (sib_ref, 1 - core)):
        for side in range(2):
            total = dkv_refs[side][block].astype(F32)
            for other in range(side + 2, row_count, 2):
                total += dkv_refs[other][block].astype(F32)
            ref[side] = total.astype(BF16)


def bundle_kernel(dkv_ref, dq_same, dq_pair, out):
    krows2 = dkv_ref.shape[1]
    sibling = 1 - my_place()[2]
    out[:, :krows2] = dkv_ref[...]
    for side, dq in enumerate((dq_same, dq_pair)):
        out[side, krows2:] = dq[sibling]


def finish_kernel(krows, dkv_own, dq_same, dq_pair, sib_ref, dq_out, dk_out, dv_out):
    row, chip, core, quarter = my_place()
    for side, dq in enumerate((dq_same, dq_pair)):
        for step, ref in enumerate((dkv_own, sib_ref)):
            lanes = lanes_of(quarter ^ (2 * side + step))
            dk_out[0, :, lanes] = ref[side, :krows]
            dv_out[0, :, lanes] = ref[side, krows : 2 * krows]
            dq_out[0, :, lanes] = ref[side, 2 * krows :] if step else dq[core]


def send(block, axes, count, step):
    return lax.ppermute(block, axes, [(place, place ^ step) for place in range(count)])


def body(sizes, queries, keys, values, outputs, grad_out, lse, tile_slot, tile_live, tile_bits):
    row_count, chips, cores = sizes
    heads = lse.shape[1]
    width = queries.shape[2]
    head_dim = width // heads
    tile = tile_bits.shape[4]
    capacity = tile_slot.shape[2]
    rows = queries.shape[1]
    krows = keys.shape[1]
    query_tiles = lse.shape[2] // tile
    key_tiles = row_count * krows // tile
    line = ("row", "core")
    places = row_count * cores

    def shape(*dims, dtype=BF16):
        return jax.ShapeDtypeStruct(dims, dtype)

    qg_shape = shape(2 * rows + PAD, LANES)
    kv_shape = shape(2, 2 * krows, LANES)
    slabs = capacity // 2 + 1
    qg_own, pair0, pair1, kv_own, to_sibling, bits_own, lse_own = pl.pallas_call(
        functools.partial(pack_kernel, heads),
        out_shape=(
            qg_shape, qg_shape, qg_shape, shape(4 * krows, LANES),
            shape(4 * krows + 2 * rows + PAD, LANES),
            shape(slabs + query_tiles // 4, 8, LANES, dtype=I32),
            shape(query_tiles, 2, tile, dtype=F32),
        ),
        in_specs=[HBM] * 7 + [VMEM] * 2,
        out_specs=(VMEM,) * 7,
        scratch_shapes=[
            pltpu.VMEM(queries.shape, BF16),
            pltpu.VMEM(queries.shape, BF16),
            pltpu.VMEM(queries.shape, BF16),
            pltpu.VMEM(keys.shape, BF16),
            pltpu.VMEM(keys.shape, BF16),
            pltpu.VMEM(tile_bits.shape, I32),
            pltpu.VMEM(lse.shape, F32),
            pltpu.VMEM((QUARTERS, PAD, rows), BF16),
            pltpu.SemaphoreType.DMA((7,)),
        ],
        compiler_params=PACK,
        name="pack",
    )(queries, grad_out, outputs, keys, values, tile_bits, lse, tile_slot, tile_live)

    pair0 = send(pair0, line, places, 2)
    pair1 = send(pair1, line, places, 3)
    from_sibling = send(to_sibling, "core", cores, 1)
    bits_pair = send(bits_own, "row", row_count, 1)
    kv_same, kv_pair = pl.pallas_call(
        functools.partial(key_join_kernel, krows),
        out_shape=(kv_shape, kv_shape),
        in_specs=[VMEM] * 2,
        out_specs=(VMEM,) * 2,
        compiler_params=SMALL,
        name="key_join",
    )(kv_own, from_sibling)
    kv_out = (kv_same, kv_pair)
    kv_far, kv_pair = pl.pallas_call(
        far_join_kernel,
        out_shape=(shape(row_count - 2, *kv_shape.shape), kv_shape),
        in_specs=[VMEM] * (row_count - 1),
        out_specs=(VMEM, VMEM),
        compiler_params=SMALL,
        cost_estimate=early(20),
        name="far_join",
    )(kv_pair, *[send(kv_out[step % 2], "row", row_count, step) for step in range(2, row_count)])
    kv = (kv_same, send(kv_pair, "row", row_count, 1), kv_far)
    qg, bits, lse2 = pl.pallas_call(
        functools.partial(query_join_kernel, krows, slabs),
        out_shape=(
            shape(QUARTERS, 2 * rows + PAD, LANES),
            shape(2, capacity // 2 + 1, 8, LANES, dtype=I32),
            shape(2, query_tiles, 2, tile, dtype=F32),
        ),
        in_specs=[VMEM] * 7,
        out_specs=(VMEM,) * 3,
        compiler_params=SMALL,
        cost_estimate=early(20),
        name="query_join",
    )(qg_own, from_sibling, pair0, pair1, bits_own, bits_pair, lse_own)
    qg = [qg] + [send(qg, "chip", chips, step) for step in range(1, chips)]
    bits_sibling = send(bits, "core", cores, 1)

    placed = pl.pallas_call(
        functools.partial(key_place_kernel, head_dim, tile),
        out_shape=(
            shape(2, key_tiles, tile, LANES), shape(2, key_tiles, tile, LANES),
            shape(2, key_tiles, LANES, 2 * tile),
        ),
        in_specs=[VMEM] * 3,
        out_specs=(VMEM,) * 3,
        compiler_params=SMALL,
        name="key_place",
    )(*kv)
    parts = pl.pallas_call(
        functools.partial(pair_kernel, (head_dim, tile, capacity, chips, row_count)),
        out_shape=(shape(2, query_tiles, LANES, tile),) + (kv_shape,) * row_count,
        in_specs=[VMEM] * (chips + 6),
        out_specs=(VMEM,) * (1 + row_count),
        scratch_shapes=[
            pltpu.VMEM((2, query_tiles, 2, tile, LANES), BF16),
            pltpu.VMEM((2, query_tiles, 2, tile, LANES), BF16),
            pltpu.VMEM((2, query_tiles, PAD, tile), F32),
            pltpu.VMEM((2, query_tiles, LANES, tile), F32),
            pltpu.VMEM((2, key_tiles, tile, LANES), F32),
            pltpu.VMEM((2, key_tiles, tile, LANES), F32),
            pltpu.VMEM((QUARTERS, capacity, 4, LANES), I32),
            pltpu.SMEM((QUARTERS, 8, LANES), I32),
            pltpu.SMEM((QUARTERS * capacity,), I32),
            pltpu.SemaphoreType.DMA((QUARTERS,)),
        ],
        compiler_params=MEDIUM,
        name="pair",
    )(*qg, *placed, bits, bits_sibling, lse2)

    dkv = parts[1:]
    dq = pl.pallas_call(
        functools.partial(turn_kernel, rows),
        out_shape=(shape(QUARTERS, rows, LANES),) * chips,
        in_specs=[VMEM],
        out_specs=(VMEM,) * chips,
        scratch_shapes=[pltpu.VMEM((2, query_tiles * tile, LANES), BF16)],
        compiler_params=SMALL,
        name="turn",
    )(parts[0])
    dq = [dq[0]] + [send(dq[step], "chip", chips, step) for step in range(1, chips)]
    dkv = [dkv[0]] + [
        send(dkv[step], "row", row_count, step) for step in range(row_count - 1, 0, -1)
    ]
    dq_same, dq_pair = pl.pallas_call(
        functools.partial(query_sum_kernel, chips),
        out_shape=(shape(2, rows, LANES),) * 2,
        in_specs=[VMEM] * chips,
        out_specs=(VMEM,) * 2,
        compiler_params=SMALL,
        name="query_sum",
    )(*dq)
    dq_pair = send(dq_pair, "row", row_count, 1)
    dkv_own, dkv_sibling = pl.pallas_call(
        functools.partial(key_sum_kernel, row_count),
        out_shape=(kv_shape,) * 2,
        in_specs=[VMEM] * row_count,
        out_specs=(VMEM,) * 2,
        compiler_params=SMALL,
        cost_estimate=early(20),
        name="key_sum",
    )(*dkv)
    to_sibling = pl.pallas_call(
        bundle_kernel,
        out_shape=shape(2, 2 * krows + rows, LANES),
        in_specs=[VMEM] * 3,
        out_specs=VMEM,
        compiler_params=SMALL,
        name="bundle",
    )(dkv_sibling, dq_same, dq_pair)
    from_sibling = send(to_sibling, "core", cores, 1)
    return pl.pallas_call(
        functools.partial(finish_kernel, krows),
        out_shape=(shape(1, rows, width), shape(1, krows, width), shape(1, krows, width)),
        in_specs=[VMEM] * 4,
        out_specs=(VMEM,) * 3,
        compiler_params=SMALL,
        name="finish",
    )(dkv_own, dq_same, dq_pair, from_sibling)


def solution(mesh):
    row_count, columns = mesh.devices.shape
    cores = 2
    chips = columns // cores
    fine = Mesh(mesh.devices.reshape(row_count, chips, cores), ("row", "chip", "core"))
    col = ("chip", "core")
    in_specs = (
        P("row", col, None),
        P(col, "row", None),
        P(col, "row", None),
        P("row", col, None),
        P("row", col, None),
        P("row", None, None),
        P("row", col, None),
        P("row", col),
        P("row", col, None, None, None),
    )
    out_specs = (P("row", col, None), P(col, "row", None), P(col, "row", None))
    return jax.shard_map(
        functools.partial(body, (row_count, chips, cores)),
        mesh=fine, in_specs=in_specs, out_specs=out_specs, check_vma=False,
    )
```

```python
import functools

import jax
import jax.numpy as jnp
from jax import lax
from jax.experimental import pallas as pl
from jax.experimental.pallas import tpu as pltpu
from jax.sharding import Mesh
from jax.sharding import PartitionSpec as P


F32 = jnp.float32
BF16 = jnp.bfloat16
I32 = jnp.int32
LANES = 128
PAD = 16
QUARTERS = 4
TOGETHER = 8
LSE_UNIT = 2.0**21
NT = (((1,), (1,)), ((), ()))
NN = (((1,), (0,)), ((), ()))
MEDIUM = pltpu.CompilerParams(vmem_limit_bytes=28 * 1024 * 1024)
PACK = pltpu.CompilerParams(vmem_limit_bytes=int(53.6 * 1024 * 1024))
SMALL = pltpu.CompilerParams(vmem_limit_bytes=12 * 1024 * 1024)
def early(gigaflops):
    return pl.CostEstimate(flops=gigaflops * 10**9, bytes_accessed=0, transcendentals=0)


VMEM = pl.BlockSpec(memory_space=pltpu.VMEM)
HBM = pl.BlockSpec(memory_space=pltpu.HBM)


def lanes_of(quarter):
    return pl.ds(pl.multiple_of(quarter * LANES, LANES), LANES)


def my_place():
    row, chip, core = (lax.axis_index(name) for name in ("row", "chip", "core"))
    return row, chip, core, row % 2 * 2 + core


def pack_kernel(
    heads, q_hbm, g_hbm, o_hbm, k_hbm, v_hbm, bits_hbm, lse_hbm, slot_ref, live_ref,
    qg_own, pair0_ref, pair1_ref, kv_own, sib_ref, packed_ref, lse_own,
    q_ref, g_ref, o_ref, k_ref, v_ref, bits_ref, lse_ref, delta_ref, sems,
):
    arrays = (
        (q_hbm, q_ref), (g_hbm, g_ref), (o_hbm, o_ref), (k_hbm, k_ref),
        (v_hbm, v_ref), (bits_hbm, bits_ref), (lse_hbm, lse_ref),
    )
    copies = [pltpu.make_async_copy(a, b, sems.at[i]) for i, (a, b) in enumerate(arrays)]
    for copy in copies:
        copy.start()
    rows, width = q_ref.shape[1:]
    krows = k_ref.shape[1]
    head_dim = width // heads
    local = heads // QUARTERS
    capacity = bits_ref.shape[2]
    quarter = my_place()[3]
    feature = lax.broadcasted_iota(I32, (QUARTERS * PAD, width), 1)
    line = lax.broadcasted_iota(I32, (QUARTERS * PAD, width), 0)
    wanted = jnp.where(line % PAD < local, line // PAD * local + line % PAD, -1)
    pick = (feature // head_dim == wanted).astype(F32)
    packed_ref[capacity // 2] = jnp.zeros((8, LANES), I32)
    packed_ref[capacity // 2, 0:1, 0:capacity] = slot_ref[0]
    packed_ref[capacity // 2, 1:2, 0:1] = live_ref[...]
    for copy in copies:
        copy.wait()
    product = g_ref[0].astype(F32) * o_ref[0].astype(F32)
    delta = lax.dot_general(
        pick, product, NT, precision=lax.Precision.HIGHEST, preferred_element_type=F32
    ).astype(BF16)
    for index in range(QUARTERS):
        delta_ref[index] = delta[index * PAD : (index + 1) * PAD]
    for step, (ref, start) in enumerate(
        ((qg_own, 0), (sib_ref, 4 * krows), (pair0_ref, 0), (pair1_ref, 0))
    ):
        lanes = lanes_of(quarter ^ step)
        ref[start : start + rows] = q_ref[0, :, lanes]
        ref[start + rows : start + 2 * rows] = g_ref[0, :, lanes]
        if rows < LANES:
            ref[start + 2 * rows : start + 2 * rows + PAD] = jnp.zeros((PAD, LANES), BF16)
        ref[start + 2 * rows : start + 2 * rows + PAD, :rows] = delta_ref[quarter ^ step]
    for step in range(QUARTERS):
        ref = (kv_own, sib_ref)[step % 2]
        lanes = lanes_of(quarter ^ step)
        start = step // 2 * 2 * krows
        ref[start : start + krows] = k_ref[0, :, lanes]
        ref[start + krows : start + 2 * krows] = v_ref[0, :, lanes]
    every = lse_ref[0]

    def lse_of(wanted_quarter):
        own = every[:local]
        for index in range(1, QUARTERS):
            own = jnp.where(
                wanted_quarter == index, every[local * index : local * (index + 1)], own
            )
        return own

    mine = lse_of(quarter)
    other = (lse_of(quarter ^ 2) * LSE_UNIT).astype(I32)
    for u in range(lse_own.shape[0]):
        lanes = slice(u * LANES, (u + 1) * LANES)
        lse_own[u] = mine[:, lanes]
        packed_ref[capacity // 2 + 1 + u // 4, u % 4 * 2 : u % 4 * 2 + 2] = other[:, lanes]
    for entry in range(capacity):
        words = bits_ref[0, 0, entry]
        span = slice(entry % 2 * 4, entry % 2 * 4 + 4)
        packed_ref[entry // 2, span] = words[:4] | lax.shift_left(words[4:], I32(16))


def key_join_kernel(krows, kv_own, sib_ref, kv_same, kv_pair):
    core = my_place()[2]
    for side, ref in enumerate((kv_same, kv_pair)):
        span = slice(side * 2 * krows, (side + 1) * 2 * krows)
        ref[core] = kv_own[span]
        ref[1 - core] = sib_ref[span]


def query_join_kernel(
    krows, slabs, qg_own, sib_ref, pair0_ref, pair1_ref, bits_own, bits_pair, lse_own,
    qg_out, bits_out, lse_out,
):
    row, chip, core, quarter = my_place()
    side = row % 2
    qg_out[quarter] = qg_own[...]
    qg_out[quarter ^ 1] = sib_ref[4 * krows :]
    qg_out[quarter ^ 2] = pair0_ref[...]
    qg_out[quarter ^ 3] = pair1_ref[...]
    bits_out[side] = bits_own[:slabs]
    bits_out[1 - side] = bits_pair[:slabs]
    lse_out[side] = lse_own[...]
    for u in range(lse_out.shape[1]):
        fixed = bits_pair[slabs + u // 4, u % 4 * 2 : u % 4 * 2 + 2]
        lse_out[1 - side, u] = fixed.astype(F32) * (1.0 / LSE_UNIT)


def far_join_kernel(pair_ref, *refs):
    parts, (far_out, pair_out) = refs[:-2], refs[-2:]
    for index, ref in enumerate(parts):
        far_out[index] = ref[...]
    pair_out[...] = pair_ref[...]


def key_place_kernel(head_dim, tile, same_ref, pair_ref, far_ref, k_out, v_out, k2t_out):
    kv_refs = [same_ref, pair_ref] + [far_ref.at[index] for index in range(far_ref.shape[0])]
    krows = kv_refs[0].shape[1] // 2
    row = my_place()[0]
    for step, ref in enumerate(kv_refs):
        start = (row ^ step) * krows
        inner = pl.multiple_of(start % tile, krows)
        for block in range(2):
            k_out[block, start // tile, pl.ds(inner, krows)] = ref[block, :krows]
            v_out[block, start // tile, pl.ds(inner, krows)] = ref[block, krows:]
    low_row = lax.broadcasted_iota(I32, (LANES, tile), 0) < head_dim
    none_t = jnp.zeros((LANES, tile), BF16)
    for block in range(2):
        for w in range(k_out.shape[1]):
            flipped = k_out[block, w].T
            k2t_out[block, w] = jnp.concatenate(
                [jnp.where(low_row, flipped, none_t), jnp.where(low_row, none_t, flipped)], axis=1
            )


def pair_kernel(sizes, *refs):
    head_dim, tile, capacity, chips, row_count = sizes
    qg_refs, refs = refs[:chips], refs[chips:]
    (k_scr, v_scr, k2t_scr), refs = refs[:3], refs[3:]
    bits_refs, lse_ref, refs = refs[:2], refs[2], refs[3:]
    dqt_ref, dkv_refs, refs = refs[0], refs[1 : 1 + row_count], refs[1 + row_count :]
    q2_scr, g2_scr, delta_scr, dqt_scr, dk_scr, dv_scr, bits_scr, info, todo, sems = refs
    rows = (qg_refs[0].shape[1] - PAD) // 2
    krows = dkv_refs[0].shape[1] // 2
    query_tiles = q2_scr.shape[1]
    key_tiles = k_scr.shape[1]
    scaling = float(head_dim) ** -0.5
    row, chip, core, quarter = my_place()
    side = row % 2

    copies = [
        pltpu.make_async_copy(
            bits_refs[i % 2].at[i // 2, capacity // 2], info.at[i], sems.at[i]
        )
        for i in range(QUARTERS)
    ]
    for copy in copies:
        copy.start()

    low = lax.broadcasted_iota(I32, (rows, LANES), 1) < head_dim
    none = jnp.zeros((rows, LANES), BF16)
    for step in range(chips):
        for index in range(QUARTERS):
            source = (chip ^ step) * 2 + index % 2
            start = source * rows
            u = start // tile
            inner = pl.multiple_of(start % tile, rows)
            block = index // 2
            for scr, part in ((q2_scr, 0), (g2_scr, 1)):
                piece = qg_refs[step][index, part * rows : (part + 1) * rows]
                if part == 0:
                    piece = (piece.astype(F32) * scaling).astype(BF16)
                scr[block, u, 0, pl.ds(inner, rows)] = jnp.where(low, piece, none)
                scr[block, u, 1, pl.ds(inner, rows)] = jnp.where(low, none, piece)
            delta = qg_refs[step][index, 2 * rows :, :rows].astype(F32)
            if rows == tile:
                delta_scr[block, u] = delta
            else:
                for part in range(tile // rows):
                    @pl.when(source % (tile // rows) == part)
                    def _(part=part, delta=delta, u=u, block=block):
                        delta_scr[block, u, :, part * rows : (part + 1) * rows] = delta
    dqt_scr[...] = jnp.zeros_like(dqt_scr)
    dk_scr[...] = jnp.zeros_like(dk_scr)
    dv_scr[...] = jnp.zeros_like(dv_scr)
    place_in = lax.broadcasted_iota(I32, (2, 4, 16, tile), 2)
    upper = lax.broadcasted_iota(I32, (2, 4, 16, tile), 0)
    bit = lax.shift_left(I32(1), place_in + 16 * upper).reshape(tile, tile)
    for step in range(QUARTERS):
        for entry in range(capacity):
            span = slice(entry % 2 * 4, entry % 2 * 4 + 4)
            bits_scr[step, entry] = bits_refs[step % 2][side ^ (step // 2), entry // 2, span]
    for i, copy in enumerate(copies):
        copy.wait()
    count = I32(0)
    for i in range(QUARTERS):
        step = (side ^ (i // 2)) * 2 + i % 2

        def listed(entry, count, i=i, step=step):
            todo[count] = info[i, 0, entry] + 32 * entry + 1024 * step
            return count + 1

        count = lax.fori_loop(0, info[i, 1, 0], listed, count)

    def some_tiles(index, _):
        work = []
        for part in range(TOGETHER):
            position = index * TOGETHER + part
            item = todo[jnp.minimum(position, count - 1)]
            slot = item % 32
            step = item // 1024
            qb = side ^ (step // 2)
            kb = core ^ (step % 2)
            u = slot // key_tiles
            w = slot % key_tiles
            words = bits_scr[step, item // 32 % 32]
            if part:
                words = words & jnp.where(position < count, I32(-1), I32(0))
            words = jnp.broadcast_to(words[:, None, :], (4, 16, tile)).reshape(64, tile)
            edge = (jnp.concatenate([words, words], axis=0) & bit) != 0
            q2 = q2_scr[qb, u].reshape(2 * tile, LANES)
            g2 = g2_scr[qb, u].reshape(2 * tile, LANES)
            scores = lax.dot_general(k_scr[kb, w], q2, NT, preferred_element_type=F32)
            grad_prob = lax.dot_general(v_scr[kb, w], g2, NT, preferred_element_type=F32)
            work.append((qb, kb, u, w, edge, q2, g2, scores, grad_prob))
        done = []
        for qb, kb, u, w, edge, q2, g2, scores, grad_prob in work:
            lse_tile = lse_ref[qb, u]
            delta_tile = delta_scr[qb, u]
            probs, grads = [], []
            for h in range(2):
                s = scores[:, h * tile : (h + 1) * tile]
                gp = grad_prob[:, h * tile : (h + 1) * tile]
                p = jnp.where(edge, jnp.exp(s - lse_tile[h : h + 1]), 0.0)
                ds = p * (gp - delta_tile[h : h + 1])
                probs.append(p.astype(BF16))
                grads.append(ds.astype(BF16))
            done.append((
                lax.dot_general(
                    jnp.concatenate(probs, axis=1), g2, NN, preferred_element_type=F32
                ),
                lax.dot_general(
                    jnp.concatenate(grads, axis=1), q2, NN, preferred_element_type=F32
                ),
                lax.dot_general(
                    k2t_scr[kb, w], jnp.concatenate(grads, axis=0), NN,
                    preferred_element_type=F32,
                ),
            ))
        for (qb, kb, u, w, *_), (dv, dk, dqt) in zip(work, done):
            dv_scr[kb, w] += dv
            dk_scr[kb, w] += dk
            dqt_scr[qb, u] += dqt
        return 0

    lax.fori_loop(0, (count + TOGETHER - 1) // TOGETHER, some_tiles, 0)

    for step in range(row_count):
        start = (row ^ step) * krows
        inner = pl.multiple_of(start % tile, krows)
        for block in range(2):
            dk = dk_scr[block, start // tile, pl.ds(inner, krows)]
            dv = dv_scr[block, start // tile, pl.ds(inner, krows)]
            dkv_refs[step][block, :krows] = dk.astype(BF16)
            dkv_refs[step][block, krows:] = dv.astype(BF16)
    dqt_ref[...] = (dqt_scr[...] * scaling).astype(BF16)


def turn_kernel(rows, dqt_ref, *refs):
    dq_refs, dq_scr = refs[:-1], refs[-1]
    tile = dqt_ref.shape[3]
    chip = my_place()[1]
    for block in range(2):
        for u in range(dqt_ref.shape[1]):
            dq_scr[block, u * tile : (u + 1) * tile] = dqt_ref[block, u].T
    for step, ref in enumerate(dq_refs):
        for index in range(QUARTERS):
            start = pl.multiple_of(((chip ^ step) * 2 + index % 2) * rows, rows)
            ref[index] = dq_scr[index // 2, pl.ds(start, rows)]


def query_sum_kernel(chips, *refs):
    parts, (same_ref, pair_ref) = refs[:chips], refs[chips:]
    side = my_place()[0] % 2
    for step, ref in enumerate((same_ref, pair_ref)):
        for core in range(2):
            index = (side ^ step) * 2 + core
            total = parts[0][index].astype(F32)
            for part in parts[1:]:
                total += part[index].astype(F32)
            ref[core] = total.astype(BF16)


def key_sum_kernel(row_count, *refs):
    dkv_refs, (own_ref, sib_ref) = refs[:1] + refs[row_count - 1 : 0 : -1], refs[-2:]
    core = my_place()[2]
    for ref, block in ((own_ref, core), (sib_ref, 1 - core)):
        for side in range(2):
            total = dkv_refs[side][block].astype(F32)
            for other in range(side + 2, row_count, 2):
                total += dkv_refs[other][block].astype(F32)
            ref[side] = total.astype(BF16)


def bundle_kernel(dkv_ref, dq_same, dq_pair, out):
    krows2 = dkv_ref.shape[1]
    sibling = 1 - my_place()[2]
    out[:, :krows2] = dkv_ref[...]
    for side, dq in enumerate((dq_same, dq_pair)):
        out[side, krows2:] = dq[sibling]


def finish_kernel(krows, dkv_own, dq_same, dq_pair, sib_ref, dq_out, dk_out, dv_out):
    row, chip, core, quarter = my_place()
    for side, dq in enumerate((dq_same, dq_pair)):
        for step, ref in enumerate((dkv_own, sib_ref)):
            lanes = lanes_of(quarter ^ (2 * side + step))
            dk_out[0, :, lanes] = ref[side, :krows]
            dv_out[0, :, lanes] = ref[side, krows : 2 * krows]
            dq_out[0, :, lanes] = ref[side, 2 * krows :] if step else dq[core]


def send(block, axes, count, step):
    return lax.ppermute(block, axes, [(place, place ^ step) for place in range(count)])


def body(sizes, queries, keys, values, outputs, grad_out, lse, tile_slot, tile_live, tile_bits):
    row_count, chips, cores = sizes
    heads = lse.shape[1]
    width = queries.shape[2]
    head_dim = width // heads
    tile = tile_bits.shape[4]
    capacity = tile_slot.shape[2]
    rows = queries.shape[1]
    krows = keys.shape[1]
    query_tiles = lse.shape[2] // tile
    key_tiles = row_count * krows // tile
    line = ("row", "core")
    places = row_count * cores

    def shape(*dims, dtype=BF16):
        return jax.ShapeDtypeStruct(dims, dtype)

    qg_shape = shape(2 * rows + PAD, LANES)
    kv_shape = shape(2, 2 * krows, LANES)
    slabs = capacity // 2 + 1
    qg_own, pair0, pair1, kv_own, to_sibling, bits_own, lse_own = pl.pallas_call(
        functools.partial(pack_kernel, heads),
        out_shape=(
            qg_shape, qg_shape, qg_shape, shape(4 * krows, LANES),
            shape(4 * krows + 2 * rows + PAD, LANES),
            shape(slabs + query_tiles // 4, 8, LANES, dtype=I32),
            shape(query_tiles, 2, tile, dtype=F32),
        ),
        in_specs=[HBM] * 7 + [VMEM] * 2,
        out_specs=(VMEM,) * 7,
        scratch_shapes=[
            pltpu.VMEM(queries.shape, BF16),
            pltpu.VMEM(queries.shape, BF16),
            pltpu.VMEM(queries.shape, BF16),
            pltpu.VMEM(keys.shape, BF16),
            pltpu.VMEM(keys.shape, BF16),
            pltpu.VMEM(tile_bits.shape, I32),
            pltpu.VMEM(lse.shape, F32),
            pltpu.VMEM((QUARTERS, PAD, rows), BF16),
            pltpu.SemaphoreType.DMA((7,)),
        ],
        compiler_params=PACK,
        name="pack",
    )(queries, grad_out, outputs, keys, values, tile_bits, lse, tile_slot, tile_live)

    pair0 = send(pair0, line, places, 2)
    pair1 = send(pair1, line, places, 3)
    from_sibling = send(to_sibling, "core", cores, 1)
    bits_pair = send(bits_own, "row", row_count, 1)
    kv_same, kv_pair = pl.pallas_call(
        functools.partial(key_join_kernel, krows),
        out_shape=(kv_shape, kv_shape),
        in_specs=[VMEM] * 2,
        out_specs=(VMEM,) * 2,
        compiler_params=SMALL,
        name="key_join",
    )(kv_own, from_sibling)
    kv_out = (kv_same, kv_pair)
    kv_far, kv_pair = pl.pallas_call(
        far_join_kernel,
        out_shape=(shape(row_count - 2, *kv_shape.shape), kv_shape),
        in_specs=[VMEM] * (row_count - 1),
        out_specs=(VMEM, VMEM),
        compiler_params=SMALL,
        cost_estimate=early(20),
        name="far_join",
    )(kv_pair, *[send(kv_out[step % 2], "row", row_count, step) for step in range(2, row_count)])
    kv = (kv_same, send(kv_pair, "row", row_count, 1), kv_far)
    qg, bits, lse2 = pl.pallas_call(
        functools.partial(query_join_kernel, krows, slabs),
        out_shape=(
            shape(QUARTERS, 2 * rows + PAD, LANES),
            shape(2, capacity // 2 + 1, 8, LANES, dtype=I32),
            shape(2, query_tiles, 2, tile, dtype=F32),
        ),
        in_specs=[VMEM] * 7,
        out_specs=(VMEM,) * 3,
        compiler_params=SMALL,
        cost_estimate=early(20),
        name="query_join",
    )(qg_own, from_sibling, pair0, pair1, bits_own, bits_pair, lse_own)
    qg = [qg] + [send(qg, "chip", chips, step) for step in range(1, chips)]
    bits_sibling = send(bits, "core", cores, 1)

    placed = pl.pallas_call(
        functools.partial(key_place_kernel, head_dim, tile),
        out_shape=(
            shape(2, key_tiles, tile, LANES), shape(2, key_tiles, tile, LANES),
            shape(2, key_tiles, LANES, 2 * tile),
        ),
        in_specs=[VMEM] * 3,
        out_specs=(VMEM,) * 3,
        compiler_params=SMALL,
        name="key_place",
    )(*kv)
    parts = pl.pallas_call(
        functools.partial(pair_kernel, (head_dim, tile, capacity, chips, row_count)),
        out_shape=(shape(2, query_tiles, LANES, tile),) + (kv_shape,) * row_count,
        in_specs=[VMEM] * (chips + 6),
        out_specs=(VMEM,) * (1 + row_count),
        scratch_shapes=[
            pltpu.VMEM((2, query_tiles, 2, tile, LANES), BF16),
            pltpu.VMEM((2, query_tiles, 2, tile, LANES), BF16),
            pltpu.VMEM((2, query_tiles, PAD, tile), F32),
            pltpu.VMEM((2, query_tiles, LANES, tile), F32),
            pltpu.VMEM((2, key_tiles, tile, LANES), F32),
            pltpu.VMEM((2, key_tiles, tile, LANES), F32),
            pltpu.VMEM((QUARTERS, capacity, 4, LANES), I32),
            pltpu.SMEM((QUARTERS, 8, LANES), I32),
            pltpu.SMEM((QUARTERS * capacity,), I32),
            pltpu.SemaphoreType.DMA((QUARTERS,)),
        ],
        compiler_params=MEDIUM,
        name="pair",
    )(*qg, *placed, bits, bits_sibling, lse2)

    dkv = parts[1:]
    dq = pl.pallas_call(
        functools.partial(turn_kernel, rows),
        out_shape=(shape(QUARTERS, rows, LANES),) * chips,
        in_specs=[VMEM],
        out_specs=(VMEM,) * chips,
        scratch_shapes=[pltpu.VMEM((2, query_tiles * tile, LANES), BF16)],
        compiler_params=SMALL,
        name="turn",
    )(parts[0])
    dq = [dq[0]] + [send(dq[step], "chip", chips, step) for step in range(chips - 1, 0, -1)]
    dkv = [dkv[0]] + [
        send(dkv[step], "row", row_count, step) for step in range(row_count - 1, 0, -1)
    ]
    dq_same, dq_pair = pl.pallas_call(
        functools.partial(query_sum_kernel, chips),
        out_shape=(shape(2, rows, LANES),) * 2,
        in_specs=[VMEM] * chips,
        out_specs=(VMEM,) * 2,
        compiler_params=SMALL,
        name="query_sum",
    )(*dq)
    dq_pair = send(dq_pair, "row", row_count, 1)
    dkv_own, dkv_sibling = pl.pallas_call(
        functools.partial(key_sum_kernel, row_count),
        out_shape=(kv_shape,) * 2,
        in_specs=[VMEM] * row_count,
        out_specs=(VMEM,) * 2,
        compiler_params=SMALL,
        cost_estimate=early(20),
        name="key_sum",
    )(*dkv)
    to_sibling = pl.pallas_call(
        bundle_kernel,
        out_shape=shape(2, 2 * krows + rows, LANES),
        in_specs=[VMEM] * 3,
        out_specs=VMEM,
        compiler_params=SMALL,
        name="bundle",
    )(dkv_sibling, dq_same, dq_pair)
    from_sibling = send(to_sibling, "core", cores, 1)
    return pl.pallas_call(
        functools.partial(finish_kernel, krows),
        out_shape=(shape(1, rows, width), shape(1, krows, width), shape(1, krows, width)),
        in_specs=[VMEM] * 4,
        out_specs=(VMEM,) * 3,
        compiler_params=SMALL,
        name="finish",
    )(dkv_own, dq_same, dq_pair, from_sibling)


def solution(mesh):
    row_count, columns = mesh.devices.shape
    cores = 2
    chips = columns // cores
    fine = Mesh(mesh.devices.reshape(row_count, chips, cores), ("row", "chip", "core"))
    col = ("chip", "core")
    in_specs = (
        P("row", col, None),
        P(col, "row", None),
        P(col, "row", None),
        P("row", col, None),
        P("row", col, None),
        P("row", None, None),
        P("row", col, None),
        P("row", col),
        P("row", col, None, None, None),
    )
    out_specs = (P("row", col, None), P(col, "row", None), P(col, "row", None))
    return jax.shard_map(
        functools.partial(body, (row_count, chips, cores)),
        mesh=fine, in_specs=in_specs, out_specs=out_specs, check_vma=False,
    )
```
